32 devices in a mesh: dp: 8 (over y, x, core), fsdp: 4 (over z).
Axes of the slice: x: 2, y: 2, z: 4, core: 2. Of those that a mesh axis runs over, the one named last changes fastest.
Arguments:
- source: bfloat16 [96, 256, 512], P(('dp', 'fsdp')), may hold values from -6 to 6
- target: bfloat16 [96, 256, 512], P(('dp', 'fsdp')), may hold values from -6 to 6
- cotangent: bfloat16 [96, 256, 512], P(('dp', 'fsdp')), may hold values from -6 to 6
- pair_order: int32 [96], P(('dp', 'fsdp')), may hold values from 0 to 95, each once
- source_lengths: int32 [96], replicated, may hold values from 1 to 256, 10752 in all
- target_lengths: int32 [96], replicated, may hold values from 1 to 256, 12288 in all
- enc_qkv: bfloat16 [512, 1536], P(('dp', 'fsdp')), may hold values from -0.25 to 0.25
- enc_out: bfloat16 [512, 512], P(('dp', 'fsdp')), may hold values from -1 to 1
- enc_ffn_in: bfloat16 [512, 2048], P(('dp', 'fsdp')), may hold values from -0.25 to 0.25
- enc_ffn_out: bfloat16 [2048, 512], P(('dp', 'fsdp')), may hold values from -0.125 to 0.125
- enc_bias: bfloat16 [4, 512], P(None, ('dp', 'fsdp')), may hold values from -1.75 to 1.75
- enc_ffn_bias: bfloat16 [2048], P(('dp', 'fsdp')), may hold values from -1.75 to 1.75
- enc_gain: bfloat16 [2, 512], P(None, ('dp', 'fsdp')), may hold values from 0.5 to 1.5
- enc_shift: bfloat16 [2, 512], P(None, ('dp', 'fsdp')), may hold values from -1.75 to 1.75
- dec_qkv: bfloat16 [512, 1536], P(('dp', 'fsdp')), may hold values from -0.25 to 0.25
- dec_out: bfloat16 [512, 512], P(('dp', 'fsdp')), may hold values from -1 to 1
- cross_q: bfloat16 [512, 512], P(('dp', 'fsdp')), may hold values from -0.25 to 0.25
- cross_kv: bfloat16 [512, 1024], P(('dp', 'fsdp')), may hold values from -0.25 to 0.25
- cross_out: bfloat16 [512, 512], P(('dp', 'fsdp')), may hold values from -1 to 1
- dec_ffn_in: bfloat16 [512, 2048], P(('dp', 'fsdp')), may hold values from -0.25 to 0.25
- dec_ffn_out: bfloat16 [2048, 512], P(('dp', 'fsdp')), may hold values from -0.125 to 0.125
- dec_bias: bfloat16 [7, 512], P(None, ('dp', 'fsdp')), may hold values from -1.75 to 1.75
- dec_ffn_bias: bfloat16 [2048], P(('dp', 'fsdp')), may hold values from -1.75 to 1.75
- dec_gain: bfloat16 [3, 512], P(None, ('dp', 'fsdp')), may hold values from 0.5 to 1.5
- dec_shift: bfloat16 [3, 512], P(None, ('dp', 'fsdp')), may hold values from -1.75 to 1.75
Outputs:
- decoded: bfloat16 [96, 256, 512], P(('dp', 'fsdp'))
- source_grad: bfloat16 [96, 256, 512], P(('dp', 'fsdp'))
- target_grad: bfloat16 [96, 256, 512], P(('dp', 'fsdp'))
- enc_qkv_grad: float32 [512, 1536], P(('dp', 'fsdp'))
- enc_out_grad: float32 [512, 512], P(('dp', 'fsdp'))
- enc_ffn_in_grad: float32 [512, 2048], P(('dp', 'fsdp'))
- enc_ffn_out_grad: float32 [2048, 512], P(('dp', 'fsdp'))
- enc_bias_grad: float32 [4, 512], P(None, ('dp', 'fsdp'))
- enc_ffn_bias_grad: float32 [2048], P(('dp', 'fsdp'))
- enc_gain_grad: float32 [2, 512], P(None, ('dp', 'fsdp'))
- enc_shift_grad: float32 [2, 512], P(None, ('dp', 'fsdp'))
- dec_qkv_grad: float32 [512, 1536], P(('dp', 'fsdp'))
- dec_out_grad: float32 [512, 512], P(('dp', 'fsdp'))
- cross_q_grad: float32 [512, 512], P(('dp', 'fsdp'))
- cross_kv_grad: float32 [512, 1024], P(('dp', 'fsdp'))
- cross_out_grad: float32 [512, 512], P(('dp', 'fsdp'))
- dec_ffn_in_grad: float32 [512, 2048], P(('dp', 'fsdp'))
- dec_ffn_out_grad: float32 [2048, 512], P(('dp', 'fsdp'))
- dec_bias_grad: float32 [7, 512], P(None, ('dp', 'fsdp'))
- dec_ffn_bias_grad: float32 [2048], P(('dp', 'fsdp'))
- dec_gain_grad: float32 [3, 512], P(None, ('dp', 'fsdp'))
- dec_shift_grad: float32 [3, 512], P(None, ('dp', 'fsdp'))
The draws below stay inside these ranges and needn't reach their ends.
Inputs may be any that keep to these rules, and one draw needn't show every extreme that they name: Row r of source, target and cotangent holds sentence pair pair_order[r]; every pair stands in exactly one row. The source sentence of pair p fills the positions below source_lengths[p] of its row; the rest is padding. The target sentence of pair p fills the positions below target_lengths[p] of its row; the rest is padding.
All inputs are finite; a program needn't handle non-finite values.
Results may differ from the reference program's by a relative error of at most 0.02.
Values may be sent and summed in bfloat16 or wider, within the bound.
No kernel may reach another device: no remote copies, remote signals or barrier semaphores. Data moves between devices by JAX's collectives and lax.ppermute only.
A program may use at most 192 MiB of HBM per device.

```python
import math
import jax
import jax.numpy as jnp
import numpy as np
from jax import lax

D = 512
HEAD_DIM = 64
FF = 2048
MAXLEN = 256
BATCH = 96


def shard_levels(own_key, dims, cuts, smallest, top_value):
    loudness = 1.0
    for dim, blocks in cuts:
        heights = jax.random.uniform(jax.random.fold_in(jax.random.fold_in(own_key, 6), dim), (blocks,), jnp.float32, smallest / len(cuts), top_value / len(cuts))
        loudness = loudness * jnp.repeat(jnp.exp(heights), dims[dim] // blocks).reshape((-1,) + (1,) * (len(dims) - 1 - dim))
    return loudness


def length_profile(number_of, total, limit, slope):
    loads = [(1 << 20) // math.isqrt(standing ** slope) + 1 for standing in range(2, number_of + 1)]
    surplus, counts = total - limit - (number_of - 1), [1] * (number_of - 1)
    while surplus > 0:
        candidates = [i for i in range(number_of - 1) if counts[i] < limit]
        whole, budget = sum([loads[i] for i in candidates]), surplus
        for i in candidates:
            more = min(limit - counts[i], max(1, budget * loads[i] // whole), surplus)
            counts[i] = counts[i] + more
            surplus = surplus - more
    return np.array([limit] + counts)


def ragged(key, count, total, most, lean):
    if count == 2:
        one = jax.random.randint(key, (), max(1, total - most), min(most, total - 1) + 1)
        return jnp.stack([one, total - one])
    sizes = jnp.asarray(length_profile(count, total, most, lean), jnp.int32)
    couples = (count - 1) // 2
    donor, taker = sizes[1:1 + 2 * couples:2], sizes[2:2 + 2 * couples:2]
    room = jnp.minimum(donor - 1, most - taker)
    moved = jax.random.randint(jax.random.fold_in(key, 1), (couples,), 0, 1 << 20) % (room + 1)
    sizes = sizes.at[1:1 + 2 * couples:2].set(donor - moved).at[2:2 + 2 * couples:2].set(taker + moved)
    return sizes[jax.random.permutation(jax.random.fold_in(key, 2), count)]


def normal_values(own_key, dims, scale, reach, pieces=(), kind=jnp.bfloat16):
    drawn = jax.random.normal(own_key, dims, jnp.float32) * scale
    if len(pieces) > 0:
        drawn = shard_levels(own_key, dims, pieces, -0.22, 0.18) * drawn
    return jnp.clip(drawn, min=-reach, max=reach).astype(kind)


def setup_inputs(seed: int = 0) -> dict:
    key_list = jax.random.split(jax.random.key(seed), 26)
    return {
        "source": normal_values(key_list[0], (BATCH, MAXLEN, D), 1.0, 6.0, ((0, 32),)),
        "target": normal_values(key_list[1], (BATCH, MAXLEN, D), 1.0, 6.0, ((0, 32),)),
        "cotangent": normal_values(key_list[2], (BATCH, MAXLEN, D), 1.0, 6.0, ((0, 32),)),
        "pair_order": jax.random.permutation(key_list[3], BATCH).astype(jnp.int32),
        "source_lengths": ragged(key_list[4], BATCH, BATCH * MAXLEN * 7 // 16, MAXLEN, 2).astype(jnp.int32),
        "target_lengths": ragged(key_list[5], BATCH, BATCH * MAXLEN // 2, MAXLEN, 2).astype(jnp.int32),
        "enc_qkv": normal_values(key_list[6], (D, 3 * D), D ** -0.5, 0.25, ((0, 32),)),
        "enc_out": normal_values(key_list[7], (D, D), (D // 16) ** -0.5, 1.0, ((0, 32),)),
        "enc_ffn_in": normal_values(key_list[8], (D, FF), D ** -0.5, 0.25, ((0, 32),)),
        "enc_ffn_out": normal_values(key_list[9], (FF, D), FF ** -0.5, 0.125, ((0, 32),)),
        "enc_bias": normal_values(key_list[10], (4, D), 0.3, 1.75, ((1, 32),)),
        "enc_ffn_bias": normal_values(key_list[11], (FF,), 0.3, 1.75, ((0, 32),)),
        "enc_gain": jnp.clip(1.0 + 0.1 * jax.random.normal(key_list[12], (2, D), jnp.float32), 0.5, 1.5).astype(jnp.bfloat16),
        "enc_shift": normal_values(key_list[13], (2, D), 0.3, 1.75, ((1, 32),)),
        "dec_qkv": normal_values(key_list[14], (D, 3 * D), D ** -0.5, 0.25, ((0, 32),)),
        "dec_out": normal_values(key_list[15], (D, D), (D // 16) ** -0.5, 1.0, ((0, 32),)),
        "cross_q": normal_values(key_list[16], (D, D), D ** -0.5, 0.25, ((0, 32),)),
        "cross_kv": normal_values(key_list[17], (D, 2 * D), D ** -0.5, 0.25, ((0, 32),)),
        "cross_out": normal_values(key_list[18], (D, D), (D // 16) ** -0.5, 1.0, ((0, 32),)),
        "dec_ffn_in": normal_values(key_list[19], (D, FF), D ** -0.5, 0.25, ((0, 32),)),
        "dec_ffn_out": normal_values(key_list[20], (FF, D), FF ** -0.5, 0.125, ((0, 32),)),
        "dec_bias": normal_values(key_list[21], (7, D), 0.3, 1.75, ((1, 32),)),
        "dec_ffn_bias": normal_values(key_list[22], (FF,), 0.3, 1.75, ((0, 32),)),
        "dec_gain": jnp.clip(1.0 + 0.1 * jax.random.normal(key_list[23], (3, D), jnp.float32), 0.5, 1.5).astype(jnp.bfloat16),
        "dec_shift": normal_values(key_list[24], (3, D), 0.3, 1.75, ((1, 32),)),
    }


epsilon = 1e-05

@jax.custom_vjp
def low(v):
    return lax.optimization_barrier(v.astype(jnp.bfloat16)).astype(jnp.float32)

@jax.custom_vjp
def low_back(v):
    return v

def low_keep(v):
    return (low(v), None)

def low_pass(kept, grad):
    return (grad,)

def back_keep(v):
    return (v, None)

def back_low(kept, grad):
    return (low(grad),)
low.defvjp(low_keep, low_pass)
low_back.defvjp(back_keep, back_low)

def product(operand, weight):
    return low_back(jnp.dot(low(operand), weight, precision=lax.Precision.HIGHEST))

def score_product(scaled, keys_split):
    return low_back(jnp.einsum('gqhe,gkhe->ghqk', low(scaled), low(keys_split), precision=lax.Precision.HIGHEST))

def mix_product(shares, values_split):
    return low_back(jnp.einsum('ghqk,gkhe->gqhe', low(shares), low(values_split), precision=lax.Precision.HIGHEST))

def layer_norm(inputs, norm_gain, norm_shift):
    centered = inputs - lax.optimization_barrier(jnp.mean(inputs, axis=-1, keepdims=True))
    spread = lax.optimization_barrier(jnp.mean(centered * centered, axis=-1, keepdims=True))
    return centered * lax.rsqrt(spread + epsilon) * norm_gain + norm_shift

@jax.checkpoint
def attend(queries, key_rows, value_rows, allowed):
    groups, query_len, features = queries.shape
    key_len = key_rows.shape[1]
    head_count = features // HEAD_DIM
    scaled = (queries * HEAD_DIM ** (-0.5)).reshape(groups, query_len, head_count, HEAD_DIM)
    keys_split = key_rows.reshape(groups, key_len, head_count, HEAD_DIM)
    values_split = value_rows.reshape(groups, key_len, head_count, HEAD_DIM)
    scores = score_product(scaled, keys_split)
    scores = jnp.where(allowed[:, None], scores, -1e+30)
    largest = lax.optimization_barrier(jnp.max(scores, axis=-1, keepdims=True))
    exponent = jnp.exp(scores - largest)
    shares = exponent / lax.optimization_barrier(jnp.sum(exponent, axis=-1, keepdims=True))
    mixture = mix_product(shares, values_split)
    return mixture.reshape(groups, query_len, features)

def encoder(source_rows, source_len, params):
    qkv_weight, out_weight, ffn_in, ffn_out, biases, ffn_bias, norm_gain, norm_shift = params
    groups, source_size, features = source_rows.shape
    position = jnp.arange(source_size)
    allowed = jnp.broadcast_to(position[None, None, :] < source_len[:, None, None], (groups, source_size, source_size))
    projected = product(source_rows, qkv_weight)
    queries = projected[..., :features] + biases[0]
    key_rows = projected[..., features:2 * features]
    value_rows = projected[..., 2 * features:] + biases[1]
    attended = attend(queries, key_rows, value_rows, allowed)
    after_self = layer_norm(source_rows + product(attended, out_weight) + biases[2], norm_gain[0], norm_shift[0])
    hidden = jax.nn.gelu(product(after_self, ffn_in) + ffn_bias)
    return layer_norm(after_self + product(hidden, ffn_out) + biases[3] + source_rows, norm_gain[1], norm_shift[1])

def decoder(target_rows, memory, source_len, target_len, params):
    qkv_weight, out_weight, cross_query, cross_pair, cross_output, ffn_in, ffn_out, biases, ffn_bias, norm_gain, norm_shift = params
    groups, target_size, features = target_rows.shape
    source_size = memory.shape[1]
    position = jnp.arange(target_size)
    source_position = jnp.arange(source_size)
    causal = (position[None, None, :] <= position[None, :, None]) & (position[None, None, :] < target_len[:, None, None])
    cross_mask = jnp.broadcast_to(source_position[None, None, :] < source_len[:, None, None], (groups, target_size, source_size))
    projected = product(target_rows, qkv_weight)
    queries = projected[..., :features] + biases[0]
    key_rows = projected[..., features:2 * features]
    value_rows = projected[..., 2 * features:] + biases[1]
    attended = attend(queries, key_rows, value_rows, causal)
    after_self = layer_norm(target_rows + product(attended, out_weight) + biases[2], norm_gain[0], norm_shift[0])
    cross_queries = product(after_self, cross_query) + biases[3]
    cross_values = product(memory, cross_pair)
    crossed = attend(cross_queries, cross_values[..., :features], cross_values[..., features:] + biases[4], cross_mask)
    after_cross = layer_norm(after_self + product(crossed, cross_output) + biases[5], norm_gain[1], norm_shift[1])
    hidden = jax.nn.gelu(product(after_cross, ffn_in) + ffn_bias)
    result = layer_norm(after_cross + product(hidden, ffn_out) + biases[6] + target_rows, norm_gain[2], norm_shift[2])
    valid_rows = position[None, :, None] < target_len[:, None, None]
    return jnp.where(valid_rows, result, 0.0)

def forward(source_rows, target_rows, source_len, target_len, encoder_in, decoder_in):
    memory = encoder(source_rows, source_len, encoder_in)
    return decoder(target_rows, memory, source_len, target_len, decoder_in)

def reference(source, target, cotangent, pair_order, source_lengths, target_lengths, enc_qkv, enc_out, enc_ffn_in, enc_ffn_out, enc_bias, enc_ffn_bias, enc_gain, enc_shift, dec_qkv, dec_out, cross_q, cross_kv, cross_out, dec_ffn_in, dec_ffn_out, dec_bias, dec_ffn_bias, dec_gain, dec_shift):
    enc_weights = tuple((tensor.astype(jnp.float32) for tensor in (enc_qkv, enc_out, enc_ffn_in, enc_ffn_out, enc_bias, enc_ffn_bias, enc_gain, enc_shift)))
    dec_weights = tuple((tensor.astype(jnp.float32) for tensor in (dec_qkv, dec_out, cross_q, cross_kv, cross_out, dec_ffn_in, dec_ffn_out, dec_bias, dec_ffn_bias, dec_gain, dec_shift)))
    source_len = jnp.take(source_lengths, pair_order).astype(jnp.int32)
    target_len = jnp.take(target_lengths, pair_order).astype(jnp.int32)
    group_size = 8
    group_count = source.shape[0] // group_size

    def by_group(tensor):
        return tensor.reshape((group_count, group_size) + tensor.shape[1:])

    def group_step(totals, inputs):
        source_rows, target_rows, cotangent_rows, source_part, target_part = inputs

        def local_pass(source_in, target_in, encoder_in, decoder_in):
            return forward(source_in, target_in, source_part, target_part, encoder_in, decoder_in)
        outputs, pullback = jax.vjp(local_pass, source_rows.astype(jnp.float32), target_rows.astype(jnp.float32), enc_weights, dec_weights)
        source_part_grad, target_part_grad, enc_grads, dec_grads = pullback(cotangent_rows.astype(jnp.float32))
        totals = jax.tree.map(jnp.add, totals, (enc_grads, dec_grads))
        return (totals, (outputs.astype(jnp.bfloat16), source_part_grad.astype(jnp.bfloat16), target_part_grad.astype(jnp.bfloat16)))
    zero_sums = jax.tree.map(jnp.zeros_like, (enc_weights, dec_weights))
    sums, stacked = lax.scan(group_step, zero_sums, (by_group(source), by_group(target), by_group(cotangent), by_group(source_len), by_group(target_len)))
    enc_sums, dec_sums = sums
    decoded = stacked[0].reshape(source.shape)
    source_grad = stacked[1].reshape(source.shape)
    target_grad = stacked[2].reshape(target.shape)
    return (decoded, source_grad, target_grad, enc_sums[0], enc_sums[1], enc_sums[2], enc_sums[3], enc_sums[4], enc_sums[5], enc_sums[6], enc_sums[7], dec_sums[0], dec_sums[1], dec_sums[2], dec_sums[3], dec_sums[4], dec_sums[5], dec_sums[6], dec_sums[7], dec_sums[8], dec_sums[9], dec_sums[10])
```

```python
import functools

import jax
import jax.numpy as jnp
from jax import lax
from jax.experimental import pallas as pl
from jax.experimental.pallas import tpu as pltpu
from jax.sharding import PartitionSpec as P

F32 = jnp.float32
BF16 = jnp.bfloat16
AXES = ("dp", "fsdp")
HEAD_DIM = 64
PAIR = 2 * HEAD_DIM
TILE = 512
epsilon = 1e-05
VMEM_LIMIT = 56 * 1024 * 1024

ENC_BIAS, ENC_GAIN, ENC_SHIFT = 0, 4, 6
DEC_BIAS, DEC_GAIN, DEC_SHIFT = 8, 15, 18
ENC_FFN_BIAS, DEC_FFN_BIAS = 24, 28
SMALL_ROWS = 32

GROUPS = {
    "enc_self": ("enc_qkv", "enc_out"),
    "enc_ffn": ("enc_ffn_in", "enc_ffn_out"),
    "dec_self": ("dec_qkv", "dec_out"),
    "cross": ("cross_q", "cross_kv", "cross_out"),
    "dec_ffn": ("dec_ffn_in", "dec_ffn_out"),
}


def nn(a, b):
    return lax.dot_general(a, b, (((1,), (0,)), ((), ())), preferred_element_type=F32)


def nt(a, b):
    return lax.dot_general(a, b, (((1,), (1,)), ((), ())), preferred_element_type=F32)


def tn(a, b):
    return lax.dot_general(a, b, (((0,), (0,)), ((), ())), preferred_element_type=F32)


def tokens_sum(v):
    return jnp.sum(v, axis=0, keepdims=True)


def normalize(h):
    c = h - jnp.mean(h, axis=-1, keepdims=True)
    r = lax.rsqrt(jnp.mean(c * c, axis=-1, keepdims=True) + epsilon)
    return c * r, r


def norm_back(dv, xh, r, g):
    hh = dv * g
    return r * (
        hh - jnp.mean(hh, axis=-1, keepdims=True) - xh * jnp.mean(hh * xh, axis=-1, keepdims=True)
    )


def gelu_parts(u):
    c = 0.7978845608028654
    sq = u * u
    t = jnp.tanh(u * (c + (c * 0.044715) * sq))
    half = 0.5 * (1.0 + t)
    slope = half + (0.5 * u) * (1.0 - t * t) * (c + (3.0 * c * 0.044715) * sq)
    return u * half, slope


class Layout:
    def __init__(self, group, shapes, pieces, nd, nz):
        self.names = GROUPS[group]
        self.shapes = [shapes[n] for n in self.names]
        self.pieces = pieces
        self.nd, self.nz = nd, nz
        self.offsets, row = [], 0
        for rows, cols in self.shapes:
            self.offsets.append(row)
            row += (rows // (nd * nz)) * (cols // TILE)
        self.rows = row
        self.first = 0

    def n_sources(self):
        return self.nd if self.pieces else len(self.names)

    def w_scratch(self):
        return [pltpu.VMEM(s, BF16) for s in self.shapes] + [
            pltpu.SemaphoreType.DMA((len(self.shapes),))
        ]

    def acc_scratch(self):
        return (
            [pltpu.VMEM(s, F32) for s in self.shapes]
            + [pltpu.VMEM(s, BF16) for s in self.shapes]
            + [pltpu.SemaphoreType.DMA((len(self.shapes),))]
        )

    def start_loads(self, sources, weights, sems, dp):
        for j, (rows, cols) in enumerate(self.shapes):
            if not self.pieces:
                pltpu.make_async_copy(sources[j], weights[j], sems.at[j]).start()
                continue
            rd = rows // (self.nd * self.nz)
            view = weights[j].reshape(self.nd, self.nz, rd, cols)
            for m in range(self.nd):
                for cb in range(cols // TILE):
                    pltpu.make_async_copy(
                        sources[m].at[:, pl.ds(self.first + self.offsets[j] + cb * rd, rd), :],
                        view.at[dp ^ m, :, :, pl.ds(cb * TILE, TILE)],
                        sems.at[j],
                    ).start()

    def wait_load(self, weights, sems, j):
        pltpu.make_async_copy(weights[j], weights[j], sems.at[j]).wait()

    def grad_shapes(self):
        if not self.pieces:
            return [jax.ShapeDtypeStruct(s, BF16) for s in self.shapes]
        return [jax.ShapeDtypeStruct((self.nd // 2, self.nz, self.rows, TILE), BF16)] * 2

    def start_store(self, acc, stage, outs, sems, dp, j):
        rows, cols = self.shapes[j]
        stage[j][...] = acc[j][...].astype(BF16)
        if not self.pieces:
            pltpu.make_async_copy(stage[j], outs[j], sems.at[j]).start()
            return
        rd = rows // (self.nd * self.nz)
        view = stage[j].reshape(self.nd, self.nz, rd, cols)
        for m in range(self.nd):
            for cb in range(cols // TILE):
                pltpu.make_async_copy(
                    view.at[dp ^ m, :, :, pl.ds(cb * TILE, TILE)],
                    outs[m % 2].at[m // 2, :, pl.ds(self.offsets[j] + cb * rd, rd), :],
                    sems.at[j],
                ).start()

    def wait_store(self, stage, sems, j):
        pltpu.make_async_copy(stage[j], stage[j], sems.at[j]).wait()


def take(refs, *counts):
    out, at = [], 0
    for c in counts:
        out.append(refs[at] if c is None else list(refs[at : at + c]))
        at += 1 if c is None else c
    assert at == len(refs), (at, len(refs))
    return out


def low_lanes(rows):
    return lax.broadcasted_iota(jnp.int32, (rows, PAIR), 1) < HEAD_DIM


def split_pair(v):
    low = low_lanes(v.shape[0])
    zero = jnp.zeros_like(v)
    return jnp.concatenate([jnp.where(low, v, zero), jnp.where(low, zero, v)], axis=0)


def allowed_keys(length, causal, size):
    col = lax.broadcasted_iota(jnp.int32, (size, size), 1)
    ok = col < length
    if causal:
        ok = ok & (col <= lax.broadcasted_iota(jnp.int32, (size, size), 0))
    return ok


def pair_forward(q, k, v, ok):
    size = q.shape[0]
    s = nt(split_pair(q), k)
    s = jnp.where(jnp.concatenate([ok, ok], axis=0), s, -1e30)
    e = jnp.exp(s - jnp.max(s, axis=-1, keepdims=True))
    a = (e * (1.0 / jnp.sum(e, axis=-1, keepdims=True))).astype(BF16)
    mixed = nn(jnp.concatenate([a[:size], a[size:]], axis=1), split_pair(v))
    return a, mixed


def pair_backward(q, k, v, a, g):
    size = q.shape[0]
    g2 = split_pair(g)
    af = a.astype(F32)
    da = nt(g2, v)
    ds = (af * (da - jnp.sum(af * da, axis=-1, keepdims=True))).astype(BF16)
    dv = tn(a, g2)
    dk = tn(ds, split_pair(q))
    dq = nn(jnp.concatenate([ds[:size], ds[size:]], axis=1), split_pair(k))
    return dq * (HEAD_DIM**-0.5), dk, dv


def self_fwd_kernel(layout, causal, bias, length_at, meta, *refs):
    x_ref, small, sources, h_ref, qkv_ref, a_ref, o_ref, weights, sems = take(
        refs, None, None, layout.n_sources(), None, None, None, None, len(layout.names), None
    )
    step = pl.program_id(0)
    size, width = x_ref.shape[1:]
    dp = meta[0]

    @pl.when(step == 0)
    def _():
        layout.start_loads(sources, weights, sems, dp)
        layout.wait_load(weights, sems, 0)

    x = x_ref[0]
    ok = allowed_keys(meta[length_at + step], causal, size)
    q = (nn(x, weights[0][:, :width]) + small[bias : bias + 1]) * (HEAD_DIM**-0.5)
    qkv_ref[0, :, :width] = q.astype(BF16)
    qkv_ref[0, :, width : 2 * width] = nn(x, weights[0][:, width : 2 * width]).astype(BF16)
    v = nn(x, weights[0][:, 2 * width :]) + small[bias + 1 : bias + 2]
    qkv_ref[0, :, 2 * width :] = v.astype(BF16)
    for p in range(width // PAIR):
        at = p * PAIR
        a, mixed = pair_forward(
            qkv_ref[0, :, at : at + PAIR],
            qkv_ref[0, :, width + at : width + at + PAIR],
            qkv_ref[0, :, 2 * width + at : 2 * width + at + PAIR],
            ok,
        )
        a_ref[0, p] = a
        o_ref[0, :, at : at + PAIR] = mixed.astype(BF16)

    @pl.when(step == 0)
    def _():
        layout.wait_load(weights, sems, 1)

    h_ref[0] = x.astype(F32) + nn(o_ref[0], weights[1][...]) + small[bias + 2 : bias + 3]


def cross_fwd_kernel(layout, meta, *refs):
    h3_ref, h2_ref, small, sources, h_ref, q_ref, kv_ref, a_ref, o_ref, weights, sems = take(
        refs, None, None, None, layout.n_sources(), None, None, None, None, None, len(layout.names), None
    )
    step = pl.program_id(0)
    size, width = h3_ref.shape[1:]
    dp = meta[0]

    @pl.when(step == 0)
    def _():
        layout.start_loads(sources, weights, sems, dp)
        layout.wait_load(weights, sems, 0)
        layout.wait_load(weights, sems, 1)

    ok = allowed_keys(meta[2 + step], False, size)
    first = normalize(h3_ref[0])[0] * small[DEC_GAIN : DEC_GAIN + 1] + small[DEC_SHIFT : DEC_SHIFT + 1]
    memory = (
        normalize(h2_ref[0])[0] * small[ENC_GAIN + 1 : ENC_GAIN + 2]
        + small[ENC_SHIFT + 1 : ENC_SHIFT + 2]
    ).astype(BF16)
    q = (nn(first.astype(BF16), weights[0][...]) + small[DEC_BIAS + 3 : DEC_BIAS + 4]) * (HEAD_DIM**-0.5)
    q_ref[0] = q.astype(BF16)
    kv_ref[0, :, :width] = nn(memory, weights[1][:, :width]).astype(BF16)
    kv_ref[0, :, width:] = (
        nn(memory, weights[1][:, width:]) + small[DEC_BIAS + 4 : DEC_BIAS + 5]
    ).astype(BF16)
    for p in range(width // PAIR):
        at = p * PAIR
        a, mixed = pair_forward(
            q_ref[0, :, at : at + PAIR],
            kv_ref[0, :, at : at + PAIR],
            kv_ref[0, :, width + at : width + at + PAIR],
            ok,
        )
        a_ref[0, p] = a
        o_ref[0, :, at : at + PAIR] = mixed.astype(BF16)

    @pl.when(step == 0)
    def _():
        layout.wait_load(weights, sems, 2)

    h_ref[0] = first + nn(o_ref[0], weights[2][...]) + small[DEC_BIAS + 5 : DEC_BIAS + 6]


def ffn_fwd_kernel(layout, meta, *refs):
    h1_ref, x_ref, small, sources, h_ref, hid_ref, slope_ref, weights, sems = take(
        refs, None, None, None, layout.n_sources(), None, None, None, len(layout.names), None
    )
    step = pl.program_id(0)
    hidden = hid_ref.shape[2]

    @pl.when(step == 0)
    def _():
        layout.start_loads(sources, weights, sems, meta[0])
        layout.wait_load(weights, sems, 0)
        layout.wait_load(weights, sems, 1)

    first = normalize(h1_ref[0])[0] * small[ENC_GAIN : ENC_GAIN + 1] + small[ENC_SHIFT : ENC_SHIFT + 1]
    low = first.astype(BF16)
    total = first + small[ENC_BIAS + 3 : ENC_BIAS + 4] + x_ref[0].astype(F32)
    for t in range(hidden // TILE):
        cols = slice(t * TILE, (t + 1) * TILE)
        u = nn(low, weights[0][:, cols]) + small[ENC_FFN_BIAS + t : ENC_FFN_BIAS + t + 1]
        hid, slope = gelu_parts(u)
        hid = hid.astype(BF16)
        hid_ref[0, :, cols] = hid
        slope_ref[0, :, cols] = slope.astype(BF16)
        total = total + nn(hid, weights[1][cols, :])
    h_ref[0] = total


def ffn_back_steps(layout, low, hids, slopes, g, weights, acc, sg, first):
    low_t = low.T
    total = None
    for t in range(layout.shapes[0][1] // TILE):
        cols = slice(t * TILE, (t + 1) * TILE)
        acc[1][cols, :] += nn(hids(t).T, g)
        du = nt(g, weights[1][cols, :]) * slopes(t).astype(F32)
        sg[4 + t : 5 + t, :] += tokens_sum(du)
        gu = du.astype(BF16)
        acc[0][:, cols] += nn(low_t, gu)
        part = nt(gu, weights[0][:, cols])
        total = part if total is None else total + part
    return total


def clear(acc, sg):
    for ref in acc:
        ref[...] = jnp.zeros_like(ref)
    sg[...] = jnp.zeros_like(sg)


def finish(layout, acc, stage, outs, sems, dp):
    count = len(layout.names)
    for j in range(count):
        layout.start_store(acc, stage, outs, sems, dp, j)
    for j in range(count):
        layout.wait_store(stage, sems, j)


def ffn_both_kernel(layout, meta, *refs):
    n = len(layout.names)
    (h4_ref, x_ref, cot_ref, small, sources, out_ref, dd2_ref, dh5_ref, sg, grads, weights, wsem, acc, stage,
     gsem, hid_s, slope_s) = take(
        refs, None, None, None, None, layout.n_sources(), None, None, None, None,
        len(layout.grad_shapes()), n, None, n, n, None, None, None,
    )
    step = pl.program_id(0)
    size, width = x_ref.shape[1:]
    hidden = hid_s.shape[1]

    @pl.when(step == 0)
    def _():
        layout.start_loads(sources, weights, wsem, meta[0])
        clear(acc, sg)
        layout.wait_load(weights, wsem, 0)
        layout.wait_load(weights, wsem, 1)

    xh4, _ = normalize(h4_ref[0])
    second = xh4 * small[DEC_GAIN + 1 : DEC_GAIN + 2] + small[DEC_SHIFT + 1 : DEC_SHIFT + 2]
    low = second.astype(BF16)
    total = second + small[DEC_BIAS + 6 : DEC_BIAS + 7] + x_ref[0].astype(F32)
    for t in range(hidden // TILE):
        cols = slice(t * TILE, (t + 1) * TILE)
        u = nn(low, weights[0][:, cols]) + small[DEC_FFN_BIAS + t : DEC_FFN_BIAS + t + 1]
        hid, slope = gelu_parts(u)
        hid = hid.astype(BF16)
        hid_s[:, cols] = hid
        slope_s[:, cols] = slope.astype(BF16)
        total = total + nn(hid, weights[1][cols, :])
    xh, r = normalize(total)
    gain = small[DEC_GAIN + 2 : DEC_GAIN + 3]
    valid = lax.broadcasted_iota(jnp.int32, (size, width), 0) < meta[2 + pl.num_programs(0) + step]
    out_ref[0] = jnp.where(valid, xh * gain + small[DEC_SHIFT + 2 : DEC_SHIFT + 3], 0.0).astype(BF16)

    dv = jnp.where(valid, cot_ref[0].astype(F32), 0.0)
    dh = norm_back(dv, xh, r, gain)
    sg[0:1, :] += tokens_sum(dh)
    sg[1:2, :] += tokens_sum(dv * xh)
    sg[2:3, :] += tokens_sum(dv)
    dh5_ref[0] = dh
    back = ffn_back_steps(
        layout, low,
        lambda t: hid_s[:, t * TILE : (t + 1) * TILE],
        lambda t: slope_s[:, t * TILE : (t + 1) * TILE],
        dh.astype(BF16), weights, acc, sg, None,
    )
    dd2_ref[0] = dh + back

    @pl.when(step == pl.num_programs(0) - 1)
    def _():
        finish(layout, acc, stage, grads, gsem, meta[0])


def ffn_bwd_kernel(layout, meta, *refs):
    n = len(layout.names)
    (dm_ref, h2_ref, h1_ref, hid_ref, slope_ref, small, sources, de1_ref, dh2_ref, sg, grads, weights, wsem,
     acc, stage, gsem) = take(
        refs, None, None, None, None, None, None, layout.n_sources(), None, None, None,
        len(layout.grad_shapes()), n, None, n, n, None,
    )
    step = pl.program_id(0)

    @pl.when(step == 0)
    def _():
        layout.start_loads(sources, weights, wsem, meta[0])
        clear(acc, sg)
        layout.wait_load(weights, wsem, 0)
        layout.wait_load(weights, wsem, 1)

    low = (
        normalize(h1_ref[0])[0] * small[ENC_GAIN : ENC_GAIN + 1] + small[ENC_SHIFT : ENC_SHIFT + 1]
    ).astype(BF16)
    xh, r = normalize(h2_ref[0])
    dv = dm_ref[0]
    dh = norm_back(dv, xh, r, small[ENC_GAIN + 1 : ENC_GAIN + 2])
    sg[0:1, :] += tokens_sum(dh)
    sg[1:2, :] += tokens_sum(dv * xh)
    sg[2:3, :] += tokens_sum(dv)
    dh2_ref[0] = dh
    back = ffn_back_steps(
        layout, low,
        lambda t: hid_ref[0, :, t * TILE : (t + 1) * TILE],
        lambda t: slope_ref[0, :, t * TILE : (t + 1) * TILE],
        dh.astype(BF16), weights, acc, sg, None,
    )
    de1_ref[0] = dh + back

    @pl.when(step == pl.num_programs(0) - 1)
    def _():
        finish(layout, acc, stage, grads, gsem, meta[0])


def self_bwd_kernel(layout, gain_row, meta, *refs):
    n = len(layout.names)
    (dout_ref, h_ref, x_ref, extra_ref, qkv_ref, a_ref, o_ref, small, sources, dx_ref, sg, grads, weights, wsem,
     acc, stage, gsem, go_s, g_s) = take(
        refs, None, None, None, None, None, None, None, None, layout.n_sources(), None, None,
        len(layout.grad_shapes()), n, None, n, n, None, None, None,
    )
    step = pl.program_id(0)
    size, width = x_ref.shape[1:]

    @pl.when(step == 0)
    def _():
        layout.start_loads(sources, weights, wsem, meta[0])
        clear(acc, sg)
        layout.wait_load(weights, wsem, 0)
        layout.wait_load(weights, wsem, 1)

    xh, r = normalize(h_ref[0])
    dv = dout_ref[0]
    dh = norm_back(dv, xh, r, small[gain_row : gain_row + 1])
    sg[2:3, :] += tokens_sum(dh)
    sg[3:4, :] += tokens_sum(dv * xh)
    sg[4:5, :] += tokens_sum(dv)
    g = dh.astype(BF16)
    acc[1][...] += nn(o_ref[0].T, g)
    go_s[...] = nt(g, weights[1][...]).astype(BF16)
    for p in range(width // PAIR):
        at = p * PAIR
        dq, dk, dvv = pair_backward(
            qkv_ref[0, :, at : at + PAIR],
            qkv_ref[0, :, width + at : width + at + PAIR],
            qkv_ref[0, :, 2 * width + at : 2 * width + at + PAIR],
            a_ref[0, p],
            go_s[:, at : at + PAIR],
        )
        sg[0:1, at : at + PAIR] += tokens_sum(dq)
        sg[1:2, at : at + PAIR] += tokens_sum(dvv)
        g_s[:, at : at + PAIR] = dq.astype(BF16)
        g_s[:, width + at : width + at + PAIR] = dk.astype(BF16)
        g_s[:, 2 * width + at : 2 * width + at + PAIR] = dvv.astype(BF16)
    x_t = x_ref[0].T
    for t in range(3):
        cols = slice(t * width, (t + 1) * width)
        acc[0][:, cols] += nn(x_t, g_s[:, cols])
    dx_ref[0] = (dh + extra_ref[0] + nt(g_s[...], weights[0][...])).astype(BF16)

    @pl.when(step == pl.num_programs(0) - 1)
    def _():
        finish(layout, acc, stage, grads, gsem, meta[0])


def cross_bwd_kernel(layout, meta, *refs):
    n = len(layout.names)
    (dd2_ref, h4_ref, h3_ref, h2_ref, q_ref, kv_ref, a_ref, o_ref, small, sources, dd1_ref, dm_ref, sg, grads,
     weights, wsem, acc, stage, gsem, go_s, gq_s, gkv_s) = take(
        refs, None, None, None, None, None, None, None, None, None, layout.n_sources(), None, None, None,
        len(layout.grad_shapes()), n, None, n, n, None, None, None, None,
    )
    step = pl.program_id(0)
    size, width = h4_ref.shape[1:]

    @pl.when(step == 0)
    def _():
        layout.start_loads(sources, weights, wsem, meta[0])
        clear(acc, sg)
        for j in range(n):
            layout.wait_load(weights, wsem, j)

    first = (
        normalize(h3_ref[0])[0] * small[DEC_GAIN : DEC_GAIN + 1] + small[DEC_SHIFT : DEC_SHIFT + 1]
    ).astype(BF16)
    memory = (
        normalize(h2_ref[0])[0] * small[ENC_GAIN + 1 : ENC_GAIN + 2]
        + small[ENC_SHIFT + 1 : ENC_SHIFT + 2]
    ).astype(BF16)
    xh, r = normalize(h4_ref[0])
    dv = dd2_ref[0]
    dh = norm_back(dv, xh, r, small[DEC_GAIN + 1 : DEC_GAIN + 2])
    sg[2:3, :] += tokens_sum(dh)
    sg[3:4, :] += tokens_sum(dv * xh)
    sg[4:5, :] += tokens_sum(dv)
    g = dh.astype(BF16)
    acc[2][...] += nn(o_ref[0].T, g)
    go_s[...] = nt(g, weights[2][...]).astype(BF16)
    for p in range(width // PAIR):
        at = p * PAIR
        dq, dk, dvv = pair_backward(
            q_ref[0, :, at : at + PAIR],
            kv_ref[0, :, at : at + PAIR],
            kv_ref[0, :, width + at : width + at + PAIR],
            a_ref[0, p],
            go_s[:, at : at + PAIR],
        )
        sg[0:1, at : at + PAIR] += tokens_sum(dq)
        sg[1:2, at : at + PAIR] += tokens_sum(dvv)
        gq_s[:, at : at + PAIR] = dq.astype(BF16)
        gkv_s[:, at : at + PAIR] = dk.astype(BF16)
        gkv_s[:, width + at : width + at + PAIR] = dvv.astype(BF16)
    acc[0][...] += nn(first.T, gq_s[...])
    memory_t = memory.T
    for t in range(2):
        cols = slice(t * width, (t + 1) * width)
        acc[1][:, cols] += nn(memory_t, gkv_s[:, cols])
    dd1_ref[0] = dh + nt(gq_s[...], weights[0][...])
    dm_ref[0] = nt(gkv_s[...], weights[1][...])

    @pl.when(step == pl.num_programs(0) - 1)
    def _():
        finish(layout, acc, stage, grads, gsem, meta[0])


def call(kernel, name, count, meta, rows, small, sources, out_rows, others, scratch, flops):
    def by_row(shape):
        tail = tuple(shape[1:])
        return pl.BlockSpec((1,) + tail, lambda i, m, k=len(tail): (i,) + (0,) * k)

    def whole(shape):
        return pl.BlockSpec(tuple(shape), lambda i, m, k=len(shape): (0,) * k)

    hbm = pl.BlockSpec(memory_space=pl.ANY)
    out_specs = [by_row(s.shape) for s in out_rows]
    for i, s in enumerate(others):
        out_specs.append(whole(s.shape) if i == 0 else hbm)
    moved = sum(a.size * a.dtype.itemsize for a in list(rows) + list(sources) + list(out_rows) + list(others))
    return pl.pallas_call(
        kernel,
        grid_spec=pltpu.PrefetchScalarGridSpec(
            num_scalar_prefetch=1,
            grid=(count,),
            in_specs=[by_row(a.shape) for a in rows] + [whole(small.shape)] + [hbm] * len(sources),
            out_specs=out_specs,
            scratch_shapes=scratch,
        ),
        out_shape=list(out_rows) + list(others),
        compiler_params=pltpu.CompilerParams(
            dimension_semantics=("arbitrary",), vmem_limit_bytes=VMEM_LIMIT
        ),
        cost_estimate=pl.CostEstimate(flops=int(flops), bytes_accessed=int(moved), transcendentals=0),
        name=name,
    )(meta, *rows, small, *sources)


def lookup(pair_order, lengths):
    indices = jnp.arange(lengths.shape[0], dtype=jnp.int32)
    chosen = jnp.where(pair_order[:, None] == indices[None, :], lengths[None, :], 0)
    return jnp.sum(chosen, axis=1)


ARG_NAMES = (
    "enc_qkv", "enc_out", "enc_ffn_in", "enc_ffn_out", "enc_bias", "enc_ffn_bias", "enc_gain", "enc_shift",
    "dec_qkv", "dec_out", "cross_q", "cross_kv", "cross_out", "dec_ffn_in", "dec_ffn_out", "dec_bias",
    "dec_ffn_bias", "dec_gain", "dec_shift",
)


def compute(layouts, source, target, cotangent, meta, small, w):
    count, size, width = source.shape
    hidden = layouts["enc_ffn"].shapes[0][1]
    pairs = width // PAIR
    tokens = count * size

    def f32(cols):
        return jax.ShapeDtypeStruct((count, size, cols), F32)

    def bf16(cols):
        return jax.ShapeDtypeStruct((count, size, cols), BF16)

    shares = jax.ShapeDtypeStruct((count, pairs, 2 * size, size), BF16)
    sums = jax.ShapeDtypeStruct((8, width), F32)
    attention_cost = 2 * 2 * 2 * tokens * size * width

    def cost(group, parts):
        return 2 * tokens * sum(r * c for r, c in layouts[group].shapes) * parts

    def run(kernel, name, group, rows, out_rows, others=(), scratch=(), back=False, flops=0):
        layout = layouts[group]
        return call(
            kernel, name, count, meta, rows, small, w[group], out_rows,
            ([sums] + layout.grad_shapes()) if back else [],
            layout.w_scratch() + (layout.acc_scratch() if back else []) + list(scratch),
            flops,
        )

    part = functools.partial
    lay = layouts
    h1, enc_qkv, enc_a, enc_o = run(
        part(self_fwd_kernel, lay["enc_self"], False, ENC_BIAS, 2), "enc_self_fwd", "enc_self",
        [source], [f32(width), bf16(3 * width), shares, bf16(width)],
        flops=cost("enc_self", 1) + attention_cost,
    )
    h2, hid, slope = run(
        part(ffn_fwd_kernel, lay["enc_ffn"]), "enc_ffn_fwd", "enc_ffn",
        [h1, source], [f32(width), bf16(hidden), bf16(hidden)], flops=cost("enc_ffn", 1),
    )
    h3, dec_qkv, dec_a, dec_o = run(
        part(self_fwd_kernel, lay["dec_self"], True, DEC_BIAS, 2 + count), "dec_self_fwd", "dec_self",
        [target], [f32(width), bf16(3 * width), shares, bf16(width)],
        flops=cost("dec_self", 1) + attention_cost,
    )
    h4, q, kv, cross_a, cross_o = run(
        part(cross_fwd_kernel, lay["cross"]), "cross_fwd", "cross",
        [h3, h2], [f32(width), bf16(width), bf16(2 * width), shares, bf16(width)],
        flops=cost("cross", 1) + attention_cost,
    )
    decoded, dd2, dh5, sums_df, *g_df = run(
        part(ffn_both_kernel, lay["dec_ffn"]), "dec_ffn_both", "dec_ffn",
        [h4, target, cotangent], [bf16(width), f32(width), f32(width)], back=True,
        scratch=[pltpu.VMEM((size, hidden), BF16), pltpu.VMEM((size, hidden), BF16)],
        flops=cost("dec_ffn", 3),
    )
    dd1, dm, sums_c, *g_c = run(
        part(cross_bwd_kernel, lay["cross"]), "cross_bwd", "cross",
        [dd2, h4, h3, h2, q, kv, cross_a, cross_o], [f32(width), f32(width)], back=True,
        scratch=[pltpu.VMEM((size, width), BF16), pltpu.VMEM((size, width), BF16), pltpu.VMEM((size, 2 * width), BF16)],
        flops=cost("cross", 2) + 2 * attention_cost,
    )
    self_scratch = [pltpu.VMEM((size, width), BF16), pltpu.VMEM((size, 3 * width), BF16)]
    target_grad, sums_ds, *g_ds = run(
        part(self_bwd_kernel, lay["dec_self"], DEC_GAIN), "dec_self_bwd", "dec_self",
        [dd1, h3, target, dh5, dec_qkv, dec_a, dec_o], [bf16(width)], back=True,
        scratch=self_scratch, flops=cost("dec_self", 2) + 2 * attention_cost,
    )
    de1, dh2, sums_ef, *g_ef = run(
        part(ffn_bwd_kernel, lay["enc_ffn"]), "enc_ffn_bwd", "enc_ffn",
        [dm, h2, h1, hid, slope], [f32(width), f32(width)], back=True, flops=cost("enc_ffn", 2),
    )
    source_grad, sums_es, *g_es = run(
        part(self_bwd_kernel, lay["enc_self"], ENC_GAIN), "enc_self_bwd", "enc_self",
        [de1, h1, source, dh2, enc_qkv, enc_a, enc_o], [bf16(width)], back=True,
        scratch=self_scratch, flops=cost("enc_self", 2) + 2 * attention_cost,
    )
    grads = {"enc_self": g_es, "enc_ffn": g_ef, "dec_self": g_ds, "cross": g_c, "dec_ffn": g_df}
    small_grads = {
        "enc_bias": jnp.concatenate([sums_es[0:3], sums_ef[0:1]], axis=0),
        "enc_gain": jnp.stack([sums_es[3], sums_ef[1]]),
        "enc_shift": jnp.stack([sums_es[4], sums_ef[2]]),
        "enc_ffn_bias": sums_ef[4:8].reshape(-1),
        "dec_bias": jnp.concatenate([sums_ds[0:3], sums_c[0:3], sums_df[0:1]], axis=0),
        "dec_gain": jnp.stack([sums_ds[3], sums_c[3], sums_df[1]]),
        "dec_shift": jnp.stack([sums_ds[4], sums_c[4], sums_df[2]]),
        "dec_ffn_bias": sums_df[4:8].reshape(-1),
    }
    return (decoded, source_grad, target_grad), grads, small_grads


GATHERS = (("enc_self",), ("enc_ffn",), ("dec_self", "cross"), ("dec_ffn",))


def simple(kernel, name, meta, inputs, outs, scratch=()):
    specs = [pl.BlockSpec(memory_space=pltpu.VMEM)] * len(inputs)
    return pl.pallas_call(
        kernel,
        in_specs=[pl.BlockSpec(memory_space=pltpu.SMEM)] + specs,
        out_specs=[pl.BlockSpec(memory_space=pltpu.VMEM)] * len(outs),
        out_shape=list(outs),
        scratch_shapes=list(scratch),
        compiler_params=pltpu.CompilerParams(vmem_limit_bytes=VMEM_LIMIT),
        cost_estimate=pl.CostEstimate(
            flops=0,
            bytes_accessed=int(sum(a.size * a.dtype.itemsize for a in list(inputs) + list(outs))),
            transcendentals=0,
        ),
        name=name,
    )(meta, *inputs)


SMALL_NAMES = (
    ("enc_bias", ENC_BIAS), ("enc_gain", ENC_GAIN), ("enc_shift", ENC_SHIFT),
    ("dec_bias", DEC_BIAS), ("dec_gain", DEC_GAIN), ("dec_shift", DEC_SHIFT),
)
LINE_NAMES = (("enc_ffn_bias", ENC_FFN_BIAS), ("dec_ffn_bias", DEC_FFN_BIAS))


def pack_kernel(plan, nz, meta, *refs):
    n_in = sum(len(p) for p in plan)
    shards = refs[:n_in]
    small_refs = refs[n_in : n_in + len(SMALL_NAMES) + len(LINE_NAMES)]
    outs = refs[n_in + len(small_refs) : -1]
    rows = refs[-1]
    at = 0
    for out, chunk in zip(outs, plan):
        for row in chunk:
            shard = shards[at]
            rd, cols = shard.shape
            for cb in range(cols // TILE):
                out[row + cb * rd : row + (cb + 1) * rd, :] = shard[:, cb * TILE : (cb + 1) * TILE]
            at += 1
    rank = meta[0] * nz + meta[1]
    rows[...] = jnp.zeros_like(rows)
    for ref, (_, row) in zip(small_refs, SMALL_NAMES + LINE_NAMES):
        lines, part = ref.shape
        lane = lax.broadcasted_iota(jnp.int32, (part, TILE), 1)
        spread = (lane % part == lax.broadcasted_iota(jnp.int32, (part, TILE), 0)).astype(BF16)
        tiled = nn(ref[...], spread)
        across = lax.broadcasted_iota(jnp.int32, (lines, TILE), 1)
        if row >= ENC_FFN_BIAS:
            per = TILE // part
            tiled = jnp.broadcast_to(tiled, (4, TILE))
            across = lax.broadcasted_iota(jnp.int32, (4, TILE), 1)
            down = lax.broadcasted_iota(jnp.int32, (4, TILE), 0)
            ok = (across // part == rank % per) & (down == rank // per)
            rows[row : row + 4, :] = jnp.where(ok, tiled, 0.0)
        else:
            rows[row : row + lines, :] = jnp.where(across // part == rank, tiled, 0.0)
    outs[0][outs[0].shape[0] - SMALL_ROWS :, :] = rows[...].astype(BF16)


def along_z_kernel(nz, rows, tail, meta, *refs):
    parts = refs[:nz]
    out = refs[nz]
    z = meta[1]
    for s in range(nz):
        out[(z + nz - s) % nz] = parts[s][:rows, :]
    if tail:
        total = parts[0][rows:, :].astype(F32)
        for s in range(1, nz):
            total = total + parts[s][rows:, :].astype(F32)
        refs[nz + 1][...] = total.astype(BF16)


def add_cores_kernel(tail, meta, *refs):
    own, other = refs[0], refs[1]
    outs = refs[2 + 2 * bool(tail) :]
    for k in range(own.shape[0]):
        flat = own.shape[1] * own.shape[2]
        for z in range(own.shape[1]):
            outs[k][z * own.shape[2] : (z + 1) * own.shape[2], :] = (
                own[k, z].astype(F32) + other[k, z].astype(F32)
            ).astype(BF16)
        if tail:
            outs[k][flat:, :] = (refs[2][...].astype(F32) + refs[3][...].astype(F32)).astype(BF16)


def add_chips_kernel(nz, rows, tail, n_parts, meta, *refs):
    parts, outs = refs[:n_parts], refs[n_parts:]
    z = meta[1]
    for s in range(nz):
        at = pl.multiple_of(((z + s) % nz) * rows, 16)
        total = parts[0][pl.ds(at, rows), :].astype(F32)
        for part in parts[1:]:
            total = total + part[pl.ds(at, rows), :].astype(F32)
        outs[s][:rows, :] = total.astype(outs[s].dtype)
    if tail:
        total = parts[0][nz * rows :, :].astype(F32)
        for part in parts[1:]:
            total = total + part[nz * rows :, :].astype(F32)
        for s in range(nz):
            outs[s][rows:, :] = total.astype(outs[s].dtype)


def add_z_kernel(nz, places, rows, tail, meta, *refs):
    parts, outs = refs[:nz], refs[nz:]
    for (row, rd, cols), out in zip(places, outs):
        for cb in range(cols // TILE):
            at = row + cb * rd
            total = parts[0][at : at + rd, :]
            for part in parts[1:]:
                total = total + part[at : at + rd, :].astype(F32)
            out[:, cb * TILE : (cb + 1) * TILE] = total
    if tail:
        rank = meta[0] * nz + meta[1]
        total = parts[0][rows:, :]
        for part in parts[1:]:
            total = total + part[rows:, :].astype(F32)
        for out, (_, row) in zip(outs[len(places) :], SMALL_NAMES + LINE_NAMES):
            lines, part = out.shape
            if row >= ENC_FFN_BIAS:
                per = TILE // part
                down = lax.broadcasted_iota(jnp.int32, (8, TILE), 0)
                base = total[24:32, :]
                picked = jnp.sum(
                    jnp.where(down == rank // per + (row - 24), base, 0.0), axis=0, keepdims=True
                )
                moved = pltpu.roll(jnp.broadcast_to(picked, (8, TILE)), TILE - (rank % per) * part, 1)
                out[...] = moved[0:1, :part]
            else:
                first = row // 8 * 8
                moved = pltpu.roll(total[first : first + 24 if first < 8 else 24, :], TILE - rank * part, 1)
                out[...] = moved[row - first : row - first + lines, :part]


def swap(v, axis, size, mask):
    return lax.ppermute(v, axis, [(i, i ^ mask) for i in range(size)])


def shift(v, axis, size, by):
    return lax.ppermute(v, axis, [(i, (i + by) % size) for i in range(size)])


def gather_all(layouts, shards, meta, nd, nz):
    plan, sizes, inputs = [], [], []
    for groups in GATHERS:
        rows, first = [], 0
        for g in groups:
            layouts[g].first = first
            for n, at in zip(layouts[g].names, layouts[g].offsets):
                rows.append(first + at)
                inputs.append(shards[n])
            first += layouts[g].rows
        plan.append(rows)
        sizes.append(first)
    for n, _ in SMALL_NAMES:
        inputs.append(shards[n])
    for n, _ in LINE_NAMES:
        inputs.append(shards[n].reshape(1, -1))
    tails = [SMALL_ROWS] + [0] * (len(GATHERS) - 1)
    packs = simple(
        functools.partial(pack_kernel, plan, nz), "pack_weights", meta, inputs,
        [jax.ShapeDtypeStruct((r + t, TILE), BF16) for r, t in zip(sizes, tails)],
        [pltpu.VMEM((SMALL_ROWS, TILE), F32)],
    )
    w, small = {}, None
    for groups, pack, rows, tail in zip(GATHERS, packs, sizes, tails):
        parts = [pack] + [shift(pack, "fsdp", nz, s) for s in range(1, nz)]
        outs = [jax.ShapeDtypeStruct((nz, rows, TILE), BF16)]
        if tail:
            outs.append(jax.ShapeDtypeStruct((tail, TILE), BF16))
        joined = simple(functools.partial(along_z_kernel, nz, rows, tail), "join_z", meta, parts, outs)
        def spread(v):
            pieces = []
            for k in range(nd // 2):
                piece = v if k == 0 else swap(v, "dp", nd, 2 * k)
                pieces += [piece, swap(piece, "dp", nd, 1)]
            return pieces
        pieces = spread(joined[0])
        if tail:
            small = sum(p.astype(F32) for p in spread(joined[1]))
        for g in groups:
            w[g] = pieces
    return w, small


def reduce_group(layout, grads, meta, nd, nz, tail=None):
    rows, ranks = layout.rows, nd * nz
    extra = SMALL_ROWS if tail is not None else 0
    inputs = [grads[0], swap(grads[1], "dp", nd, 1)]
    if extra:
        inputs += [tail, swap(tail, "dp", nd, 1)]
    flat = nz * rows + extra
    sums = simple(
        functools.partial(add_cores_kernel, extra), "add_cores", meta, inputs,
        [jax.ShapeDtypeStruct((flat, TILE), BF16)] * (nd // 2),
    )
    parts = [sums[0]] + [swap(sums[k], "dp", nd, 2 * k) for k in range(1, nd // 2)]
    sums = simple(
        functools.partial(add_chips_kernel, nz, rows, extra, len(parts)), "add_chips", meta, parts,
        [jax.ShapeDtypeStruct((rows + extra, TILE), F32 if s == 0 else BF16) for s in range(nz)],
    )
    parts = [sums[0]] + [shift(sums[s], "fsdp", nz, s) for s in range(1, nz)]
    places = [(at, r // ranks, c) for at, (r, c) in zip(layout.offsets, layout.shapes)]
    outs = [jax.ShapeDtypeStruct((rd, c), F32) for _, rd, c in places]
    if extra:
        wide = TILE // ranks
        counts = (4, 2, 2, 7, 3, 3)
        outs += [jax.ShapeDtypeStruct((c, wide), F32) for c in counts]
        outs += [jax.ShapeDtypeStruct((1, 4 * wide), F32)] * 2
    return simple(functools.partial(add_z_kernel, nz, places, rows, extra), "add_z", meta, parts, outs)


def local(nd, nz, source, target, cotangent, pair_order, source_lengths, target_lengths, *shards):
    shards = dict(zip(ARG_NAMES, shards))
    ranks = nd * nz
    matrices = [n for names in GROUPS.values() for n in names]
    shapes = {n: (shards[n].shape[0] * ranks, shards[n].shape[1]) for n in matrices}
    pieces = nd % 2 == 0 and nd & (nd - 1) == 0 and all(shards[n].shape[0] % 16 == 0 for n in matrices)
    layouts = {g: Layout(g, shapes, pieces, nd, nz) for g in GROUPS}
    meta = jnp.concatenate(
        [
            jnp.stack([lax.axis_index("dp"), lax.axis_index("fsdp")]).astype(jnp.int32),
            lookup(pair_order, source_lengths),
            lookup(pair_order, target_lengths),
        ]
    )
    if not pieces:
        return gathered_whole(layouts, source, target, cotangent, meta, shards)
    w, small = gather_all(layouts, shards, meta, nd, nz)
    outs, grads, sums = compute(layouts, source, target, cotangent, meta, small, w)
    result = {}
    for g in ("dec_ffn", "cross", "dec_self", "enc_ffn"):
        result.update(zip(layouts[g].names, reduce_group(layouts[g], grads[g], meta, nd, nz)))
    pad = jnp.zeros((3, sums["enc_bias"].shape[1]), F32)
    tail = jnp.concatenate(
        [sums[n] for n, _ in SMALL_NAMES] + [pad] + [sums[n].reshape(4, -1) for n, _ in LINE_NAMES], axis=0
    ).astype(BF16)
    last = reduce_group(layouts["enc_self"], grads["enc_self"], meta, nd, nz, tail)
    names = layouts["enc_self"].names + tuple(n for n, _ in SMALL_NAMES + LINE_NAMES)
    result.update(zip(names, last))
    for n, _ in LINE_NAMES:
        result[n] = result[n].reshape(-1)
    return outs + tuple(result[n] for n in ARG_NAMES)


def gathered_whole(layouts, source, target, cotangent, meta, shards):
    full = {}
    for n in ARG_NAMES:
        axis = 1 if n.endswith(("_bias", "_gain", "_shift")) and shards[n].ndim == 2 else 0
        full[n] = lax.all_gather(shards[n], AXES, axis=axis, tiled=True)
    width = source.shape[2]
    pad = jnp.zeros((3, width), BF16)
    small = jnp.concatenate(
        [full["enc_bias"], full["enc_gain"], full["enc_shift"], full["dec_bias"], full["dec_gain"],
         full["dec_shift"], pad, full["enc_ffn_bias"].reshape(-1, width), full["dec_ffn_bias"].reshape(-1, width)],
        axis=0,
    ).astype(F32)
    w = {g: [full[n] for n in names] for g, names in GROUPS.items()}
    outs, grads, small_grads = compute(layouts, source, target, cotangent, meta, small, w)
    summed = dict(small_grads)
    for g, names in GROUPS.items():
        for n, v in zip(names, grads[g]):
            summed[n] = v.astype(F32)
    result = []
    for n in ARG_NAMES:
        axis = 1 if n in small_grads and shards[n].ndim == 2 else 0
        result.append(lax.psum_scatter(summed[n], AXES, scatter_dimension=axis, tiled=True))
    return outs + tuple(result)


def specs():
    split, rows, cols = P(AXES, None, None), P(AXES, None), P(None, AXES)
    line = P(AXES)
    weights = (
        rows, rows, rows, rows, cols, line, cols, cols,
        rows, rows, rows, rows, rows, rows, rows, cols, line, cols, cols,
    )
    return (split, split, split, line, P(), P()) + weights, (split, split, split) + weights


def solution(mesh):
    in_specs, out_specs = specs()
    return jax.shard_map(
        functools.partial(local, mesh.shape["dp"], mesh.shape["fsdp"]),
        mesh=mesh, in_specs=in_specs, out_specs=out_specs, check_vma=False,
    )
```

```python
import functools

import jax
import jax.numpy as jnp
from jax import lax
from jax.experimental import pallas as pl
from jax.experimental.pallas import tpu as pltpu
from jax.sharding import PartitionSpec as P

F32 = jnp.float32
BF16 = jnp.bfloat16
DP, FSDP = "dp", "fsdp"
AXES = (DP, FSDP)
HEAD_DIM = 64
PAIR = 2 * HEAD_DIM
TILE = 512
epsilon = 1e-05
FORWARD_TILE = 256
COST = 1
VMEM_LIMIT = 56 * 1024 * 1024

ENC_BIAS, ENC_GAIN, ENC_SHIFT = 0, 4, 6
DEC_BIAS, DEC_GAIN, DEC_SHIFT = 8, 15, 18
ENC_FFN_BIAS, DEC_FFN_BIAS = 24, 28
SMALL_ROWS = 32

(A_ENC_QKV, A_ENC_OUT, A_ENC_IN, A_ENC_BACK, A_ENC_BIAS, A_ENC_FBIAS, A_ENC_GAIN, A_ENC_SHIFT, A_DEC_QKV, A_DEC_OUT,
 A_CROSS_Q, A_CROSS_KV, A_CROSS_OUT, A_DEC_IN, A_DEC_BACK, A_DEC_BIAS, A_DEC_FBIAS, A_DEC_GAIN, A_DEC_SHIFT) = range(19)
ENC_SELF, ENC_FFN, DEC_SELF, CROSS, DEC_FFN = range(5)
GROUPS = (
    (A_ENC_QKV, A_ENC_OUT),
    (A_ENC_IN, A_ENC_BACK),
    (A_DEC_QKV, A_DEC_OUT),
    (A_CROSS_Q, A_CROSS_KV, A_CROSS_OUT),
    (A_DEC_IN, A_DEC_BACK),
)
SMALLS = (
    (A_ENC_BIAS, ENC_BIAS, 4), (A_ENC_GAIN, ENC_GAIN, 2), (A_ENC_SHIFT, ENC_SHIFT, 2),
    (A_DEC_BIAS, DEC_BIAS, 7), (A_DEC_GAIN, DEC_GAIN, 3), (A_DEC_SHIFT, DEC_SHIFT, 3),
)
LINES = ((A_ENC_FBIAS, ENC_FFN_BIAS, 1), (A_DEC_FBIAS, DEC_FFN_BIAS, 1))
WHOLE, PIECES, RANKS = range(3)
GATHERS = ((ENC_SELF,), (ENC_FFN, DEC_SELF), (CROSS, DEC_FFN))


def nn(a, b):
    return lax.dot_general(a, b, (((1,), (0,)), ((), ())), preferred_element_type=F32)


def nt(a, b):
    return lax.dot_general(a, b, (((1,), (1,)), ((), ())), preferred_element_type=F32)


def tn(a, b):
    return lax.dot_general(a, b, (((0,), (0,)), ((), ())), preferred_element_type=F32)


def tokens_sum(v):
    return jnp.sum(v, axis=0, keepdims=True)


def normalize(h):
    c = h - jnp.mean(h, axis=-1, keepdims=True)
    r = lax.rsqrt(jnp.mean(c * c, axis=-1, keepdims=True) + epsilon)
    return c * r, r


def norm_back(dv, xh, r, g):
    hh = dv * g
    return r * (
        hh - jnp.mean(hh, axis=-1, keepdims=True) - xh * jnp.mean(hh * xh, axis=-1, keepdims=True)
    )


def gelu_parts(u):
    c = 0.7978845608028654
    sq = u * u
    t = jnp.tanh(u * (c + (c * 0.044715) * sq))
    half = 0.5 * (1.0 + t)
    slope = half + (0.5 * u) * (1.0 - t * t) * (c + (3.0 * c * 0.044715) * sq)
    return u * half, slope


class Layout:
    def __init__(self, group, shapes, mode, nd, nz):
        self.names = GROUPS[group]
        self.mode = mode
        self.shapes = [shapes[n] for n in self.names]
        self.span = 0
        self.nd, self.nz = nd, nz
        self.offsets, row = [], 0
        for rows, cols in self.shapes:
            self.offsets.append(row)
            row += (rows // (nd * nz)) * (cols // TILE)
        self.rows = row
        self.first = 0

    def n_sources(self):
        return len(self.names) if self.mode == WHOLE else self.nd

    def w_scratch(self):
        return [pltpu.VMEM(s, BF16) for s in self.shapes] + [
            pltpu.SemaphoreType.DMA((len(self.shapes),))
        ]

    def acc_scratch(self):
        return (
            [pltpu.VMEM(s, F32) for s in self.shapes]
            + [pltpu.VMEM(s, BF16) for s in self.shapes]
            + [pltpu.SemaphoreType.DMA((len(self.shapes),))]
        )

    def start_loads(self, sources, weights, sems, dp, order):
        for j in order:
            rows, cols = self.shapes[j]
            if self.mode == WHOLE:
                pltpu.make_async_copy(sources[j], weights[j], sems.at[j]).start()
                continue
            rd = rows // (self.nd * self.nz)
            view = weights[j].reshape(self.nd, self.nz, rd, cols)
            for m in range(self.nd):
                mask = self.masks(dp)[m]
                for cb in range(cols // TILE):
                    pltpu.make_async_copy(
                        sources[m]
                        .at[pl.ds(0, self.nz * self.span), :]
                        .reshape(self.nz, self.span, TILE)
                        .at[:, pl.ds(self.first + self.offsets[j] + cb * rd, rd), :],
                        view.at[dp ^ mask, :, :, pl.ds(cb * TILE, TILE)],
                        sems.at[j],
                    ).start()

    def masks(self, dp):
        first = jnp.where(dp % 2 == 0, 4, 2)
        return [0, 1, first, 7 - first, 6 - first, first + 1, 6, 7]

    def wait_load(self, weights, sems, j):
        pltpu.make_async_copy(weights[j], weights[j], sems.at[j]).wait()

    def grad_shapes(self):
        if self.mode == WHOLE:
            return [jax.ShapeDtypeStruct(s, BF16) for s in self.shapes]
        if self.mode == RANKS:
            return [jax.ShapeDtypeStruct((self.nd * self.nz, self.rows, TILE), BF16)]
        return [jax.ShapeDtypeStruct((self.nd // 2, self.nz, self.rows, TILE), BF16)] * 2

    def start_store(self, acc, stage, outs, sems, dp, j):
        rows, cols = self.shapes[j]
        stage[j][...] = acc[j][...].astype(BF16)
        if self.mode == WHOLE:
            pltpu.make_async_copy(stage[j], outs[j], sems.at[j]).start()
            return
        rd = rows // (self.nd * self.nz)
        if self.mode == RANKS:
            view = stage[j].reshape(self.nd * self.nz, rd, cols)
            for cb in range(cols // TILE):
                pltpu.make_async_copy(
                    view.at[:, :, pl.ds(cb * TILE, TILE)],
                    outs[0].at[:, pl.ds(self.offsets[j] + cb * rd, rd), :],
                    sems.at[j],
                ).start()
            return
        view = stage[j].reshape(self.nd, self.nz, rd, cols)
        for m, mask in enumerate(self.masks(dp)):
            for cb in range(cols // TILE):
                pltpu.make_async_copy(
                    view.at[dp ^ mask, :, :, pl.ds(cb * TILE, TILE)],
                    outs[m % 2].at[m // 2, :, pl.ds(self.offsets[j] + cb * rd, rd), :],
                    sems.at[j],
                ).start()

    def wait_store(self, stage, sems, j):
        pltpu.make_async_copy(stage[j], stage[j], sems.at[j]).wait()


class Use:
    def __init__(self, layout, step, dp, last, sources, weights, wsem):
        self.layout, self.step, self.dp, self.last = layout, step, dp, last
        self.sources, self.w, self.wsem = sources, weights, wsem
        self.acc = ()

    def add_sums(self, sg, grads, acc, stage, gsem):
        self.sg, self.grads, self.acc, self.stage, self.gsem = sg, grads, acc, stage, gsem

    def begin(self, order):
        @pl.when(self.step == 0)
        def _():
            self.layout.start_loads(self.sources, self.w, self.wsem, self.dp, order)
            if self.acc:
                for ref in self.acc:
                    ref[...] = jnp.zeros_like(ref)
                self.sg[...] = jnp.zeros_like(self.sg)

    def ready(self, *which):
        @pl.when(self.step == 0)
        def _():
            for j in which:
                self.layout.wait_load(self.w, self.wsem, j)

    def sums(self, row, v, at=0):
        self.sg[row : row + 1, at : at + v.shape[1]] += tokens_sum(v)

    def send(self, *which):
        @pl.when(self.last)
        def _():
            for j in which:
                self.layout.start_store(self.acc, self.stage, self.grads, self.gsem, self.dp, j)

    def end(self):
        @pl.when(self.last)
        def _():
            for j in range(len(self.layout.names)):
                self.layout.wait_store(self.stage, self.gsem, j)


def low_lanes(rows):
    return lax.broadcasted_iota(jnp.int32, (rows, PAIR), 1) < HEAD_DIM


def split_pair(v):
    low = low_lanes(v.shape[0])
    zero = jnp.zeros_like(v)
    return jnp.concatenate([jnp.where(low, v, zero), jnp.where(low, zero, v)], axis=0)


def allowed_keys(length, causal, size):
    col = lax.broadcasted_iota(jnp.int32, (size, size), 1)
    ok = col < length
    if causal:
        ok = ok & (col <= lax.broadcasted_iota(jnp.int32, (size, size), 0))
    return ok


def pair_forward(q, k, v, ok):
    size = q.shape[0]
    s = nt(split_pair(q), k)
    s = jnp.where(jnp.concatenate([ok, ok], axis=0), s, -1e30)
    e = jnp.exp(s - jnp.max(s, axis=-1, keepdims=True))
    a = (e * (1.0 / jnp.sum(e, axis=-1, keepdims=True))).astype(BF16)
    mixed = nn(jnp.concatenate([a[:size], a[size:]], axis=1), split_pair(v))
    return a, mixed


def pair_backward(q, k, v, a, g):
    size = q.shape[0]
    g2 = split_pair(g)
    af = a.astype(F32)
    da = nt(g2, v)
    ds = (af * (da - jnp.sum(af * da, axis=-1, keepdims=True))).astype(BF16)
    dv = tn(a, g2)
    dk = tn(ds, split_pair(q))
    dq = nn(jnp.concatenate([ds[:size], ds[size:]], axis=1), split_pair(k))
    return dq * (HEAD_DIM**-0.5), dk, dv


def row(small, at):
    return small[at : at + 1]


def attention_fwd(q, k, v, ok, a_ref, o_ref):
    for p in range(a_ref.shape[1]):
        at = p * PAIR
        a, mixed = pair_forward(q(at), k(at), v(at), ok)
        a_ref[0, p] = a
        o_ref[0, :, at : at + PAIR] = mixed.astype(BF16)


def self_fwd(use, small, x_ref, h_ref, qkv_ref, a_ref, o_ref, length, causal, bias):
    size, width = x_ref.shape[1:]
    w = use.w
    use.begin((0, 1))
    ok = allowed_keys(length, causal, size)
    use.ready(0)
    x = x_ref[0]
    q = (nn(x, w[0][:, :width]) + row(small, bias)) * (HEAD_DIM**-0.5)
    qkv_ref[0, :, :width] = q.astype(BF16)
    qkv_ref[0, :, width : 2 * width] = nn(x, w[0][:, width : 2 * width]).astype(BF16)
    qkv_ref[0, :, 2 * width :] = (nn(x, w[0][:, 2 * width :]) + row(small, bias + 1)).astype(BF16)

    def part(k):
        return lambda at: qkv_ref[0, :, k * width + at : k * width + at + PAIR]

    attention_fwd(part(0), part(1), part(2), ok, a_ref, o_ref)
    use.ready(1)
    h_ref[0] = x.astype(F32) + nn(o_ref[0], w[1][...]) + row(small, bias + 2)


def decoder_first(small, h3_ref):
    return normalize(h3_ref[0])[0] * row(small, DEC_GAIN) + row(small, DEC_SHIFT)


def memory_rows(small, h2_ref):
    return (normalize(h2_ref[0])[0] * row(small, ENC_GAIN + 1) + row(small, ENC_SHIFT + 1)).astype(BF16)


def cross_fwd(use, small, h3_ref, h2_ref, h_ref, q_ref, kv_ref, a_ref, o_ref, length):
    size, width = h3_ref.shape[1:]
    w = use.w
    use.begin((0, 1, 2))
    ok = allowed_keys(length, False, size)
    first = decoder_first(small, h3_ref)
    memory = memory_rows(small, h2_ref)
    use.ready(0)
    q = (nn(first.astype(BF16), w[0][...]) + row(small, DEC_BIAS + 3)) * (HEAD_DIM**-0.5)
    q_ref[0] = q.astype(BF16)
    use.ready(1)
    kv_ref[0, :, :width] = nn(memory, w[1][:, :width]).astype(BF16)
    kv_ref[0, :, width:] = (nn(memory, w[1][:, width:]) + row(small, DEC_BIAS + 4)).astype(BF16)
    attention_fwd(
        lambda at: q_ref[0, :, at : at + PAIR],
        lambda at: kv_ref[0, :, at : at + PAIR],
        lambda at: kv_ref[0, :, width + at : width + at + PAIR],
        ok, a_ref, o_ref,
    )
    use.ready(2)
    h_ref[0] = first + nn(o_ref[0], w[2][...]) + row(small, DEC_BIAS + 5)


def ffn_steps(use, small, low, total, ffn_bias, hid_put, slope_put):
    w = use.w
    hidden = w[0].shape[1]
    use.ready(0, 1)
    for at in range(0, hidden, FORWARD_TILE):
        cols = slice(at, at + FORWARD_TILE)
        lane = at % TILE
        bias = small[ffn_bias + at // TILE : ffn_bias + at // TILE + 1, lane : lane + FORWARD_TILE]
        hid, slope = gelu_parts(nn(low, w[0][:, cols]) + bias)
        hid = hid.astype(BF16)
        hid_put(cols, hid)
        slope_put(cols, slope.astype(BF16))
        total = total + nn(hid, w[1][cols, :])
    return total


def ffn_fwd(use, small, h1_ref, x_ref, h_ref, hid_ref, slope_ref):
    use.begin((0, 1))
    first = normalize(h1_ref[0])[0] * row(small, ENC_GAIN) + row(small, ENC_SHIFT)
    total = first + row(small, ENC_BIAS + 3) + x_ref[0].astype(F32)

    def hid_put(cols, v):
        hid_ref[0, :, cols] = v

    def slope_put(cols, v):
        slope_ref[0, :, cols] = v

    h_ref[0] = ffn_steps(use, small, first.astype(BF16), total, ENC_FFN_BIAS, hid_put, slope_put)


def ffn_back(use, low, hid, slope, g, wait=True):
    w, acc = use.w, use.acc
    acc[1][...] += nn(hid.T, g)
    use.send(1)
    if wait:
        use.ready(1)
    du = nt(g, w[1][...]) * slope.astype(F32)
    for t in range(du.shape[1] // TILE):
        use.sums(4 + t, du[:, t * TILE : (t + 1) * TILE])
    gu = du.astype(BF16)
    acc[0][...] += nn(low.T, gu)
    use.send(0)
    if wait:
        use.ready(0)
    return nt(gu, w[0][...])


def ffn_both(use, small, h4_ref, x_ref, cot_ref, out_ref, dd2_ref, dh5_ref, hid_s, slope_s, length):
    size, width = x_ref.shape[1:]
    use.begin((0, 1))
    second = normalize(h4_ref[0])[0] * row(small, DEC_GAIN + 1) + row(small, DEC_SHIFT + 1)
    low = second.astype(BF16)
    total = second + row(small, DEC_BIAS + 6) + x_ref[0].astype(F32)

    def hid_put(cols, v):
        hid_s[:, cols] = v

    def slope_put(cols, v):
        slope_s[:, cols] = v

    total = ffn_steps(use, small, low, total, DEC_FFN_BIAS, hid_put, slope_put)
    xh, r = normalize(total)
    gain = row(small, DEC_GAIN + 2)
    valid = lax.broadcasted_iota(jnp.int32, (size, width), 0) < length
    out_ref[0] = jnp.where(valid, xh * gain + row(small, DEC_SHIFT + 2), 0.0).astype(BF16)
    dv = jnp.where(valid, cot_ref[0].astype(F32), 0.0)
    dh = norm_back(dv, xh, r, gain)
    use.sums(0, dh)
    use.sums(1, dv * xh)
    use.sums(2, dv)
    dh5_ref[0] = dh
    dd2_ref[0] = dh + ffn_back(use, low, hid_s[...], slope_s[...], dh.astype(BF16), False)
    use.end()


def ffn_bwd(use, small, dm_ref, h2_ref, h1_ref, hid_ref, slope_ref, de1_ref, dh2_ref):
    use.begin((1, 0))
    low = (normalize(h1_ref[0])[0] * row(small, ENC_GAIN) + row(small, ENC_SHIFT)).astype(BF16)
    xh, r = normalize(h2_ref[0])
    dv = dm_ref[0]
    dh = norm_back(dv, xh, r, row(small, ENC_GAIN + 1))
    use.sums(0, dh)
    use.sums(1, dv * xh)
    use.sums(2, dv)
    dh2_ref[0] = dh
    de1_ref[0] = dh + ffn_back(use, low, hid_ref[0], slope_ref[0], dh.astype(BF16))
    use.end()


def attention_bwd(use, q, k, v, a_ref, go_s, put):
    for p in range(a_ref.shape[1]):
        at = p * PAIR
        dq, dk, dv = pair_backward(q(at), k(at), v(at), a_ref[0, p], go_s[:, at : at + PAIR])
        use.sums(0, dq, at)
        use.sums(1, dv, at)
        put(at, dq.astype(BF16), dk.astype(BF16), dv.astype(BF16))


def block_sums(use, dv, xh, dh):
    use.sums(2, dh)
    use.sums(3, dv * xh)
    use.sums(4, dv)


def self_bwd(use, small, dv, h_ref, x_ref, extra_ref, qkv_ref, a_ref, o_ref, dx_ref, go_s, g_s, gain_row):
    size, width = x_ref.shape[1:]
    w, acc = use.w, use.acc
    use.begin((1, 0))
    xh, r = normalize(h_ref[0])
    dh = norm_back(dv, xh, r, row(small, gain_row))
    block_sums(use, dv, xh, dh)
    g = dh.astype(BF16)
    acc[1][...] += nn(o_ref[0].T, g)
    use.send(1)
    use.ready(1)
    go_s[...] = nt(g, w[1][...]).astype(BF16)

    def part(k):
        return lambda at: qkv_ref[0, :, k * width + at : k * width + at + PAIR]

    def put(at, *parts):
        for k, v in enumerate(parts):
            g_s[:, k * width + at : k * width + at + PAIR] = v

    attention_bwd(use, part(0), part(1), part(2), a_ref, go_s, put)
    acc[0][...] += nn(x_ref[0].T, g_s[...])
    use.send(0)
    use.ready(0)
    dx_ref[0] = (dh + extra_ref[0] + nt(g_s[...], w[0][...])).astype(BF16)
    use.end()


def cross_bwd(use, small, dv, h4_ref, h3_ref, h2_ref, q_ref, kv_ref, a_ref, o_ref, dm_ref, go_s, gq_s, gkv_s):
    width = h4_ref.shape[2]
    w, acc = use.w, use.acc
    use.begin((2, 0, 1))
    first = decoder_first(small, h3_ref).astype(BF16)
    memory = memory_rows(small, h2_ref)
    xh, r = normalize(h4_ref[0])
    dh = norm_back(dv, xh, r, row(small, DEC_GAIN + 1))
    block_sums(use, dv, xh, dh)
    g = dh.astype(BF16)
    acc[2][...] += nn(o_ref[0].T, g)
    use.send(2)
    use.ready(2)
    go_s[...] = nt(g, w[2][...]).astype(BF16)

    def put(at, dq, dk, dvv):
        gq_s[:, at : at + PAIR] = dq
        gkv_s[:, at : at + PAIR] = dk
        gkv_s[:, width + at : width + at + PAIR] = dvv

    attention_bwd(
        use,
        lambda at: q_ref[0, :, at : at + PAIR],
        lambda at: kv_ref[0, :, at : at + PAIR],
        lambda at: kv_ref[0, :, width + at : width + at + PAIR],
        a_ref, go_s, put,
    )
    acc[0][...] += nn(first.T, gq_s[...])
    acc[1][...] += nn(memory.T, gkv_s[...])
    use.send(0, 1)
    use.ready(0, 1)
    dm_ref[0] = nt(gkv_s[...], w[1][...])
    out = dh + nt(gq_s[...], w[0][...])
    use.end()
    return out


def call(kernel, name, count, meta, rows, small, parts, after, out_rows, scratch):
    def by_row(shape):
        tail = tuple(shape[1:])
        return pl.BlockSpec((1,) + tail, lambda i, m, k=len(tail): (i,) + (0,) * k)

    def whole(shape):
        return pl.BlockSpec(tuple(shape), lambda i, m, k=len(shape): (0,) * k)

    width = small.shape[1]
    backs = [layout for layout, _, back in parts if back]
    shapes = list(out_rows) + [jax.ShapeDtypeStruct((8, width), F32)] * len(backs)
    for layout in backs:
        shapes += layout.grad_shapes()

    def body(meta, *refs):
        refs = list(refs)

        def next_refs(n):
            head = refs[:n]
            del refs[:n]
            return head

        ins = next_refs(len(rows))
        small_ref = next_refs(1)[0]
        sources = [next_refs(len(s)) for _, s, _ in parts]
        next_refs(len(after))
        outs = next_refs(len(out_rows))
        sums = next_refs(len(backs))
        grads = [next_refs(len(layout.grad_shapes())) for layout in backs]
        step = pl.program_id(0)
        last = step == count - 1
        uses, at = [], 0
        for (layout, _, back), src in zip(parts, sources):
            n = len(layout.names)
            use = Use(layout, step, meta[0], last, src, next_refs(n), next_refs(1)[0])
            if back:
                use.add_sums(sums[at], grads[at], next_refs(n), next_refs(n), next_refs(1)[0])
                at += 1
            uses.append(use)
        kernel(meta, step, small_ref, uses, ins, outs, refs)

    scratches = []
    for layout, _, back in parts:
        scratches += layout.w_scratch() + (layout.acc_scratch() if back else [])
    hbm = pl.BlockSpec(memory_space=pl.ANY)
    n_sources = sum(len(s) for _, s, _ in parts)
    out_specs = [by_row(v.shape) for v in out_rows] + [whole((8, width))] * len(backs)
    out_specs += [hbm] * (len(shapes) - len(out_specs))
    result = pl.pallas_call(
        body,
        grid_spec=pltpu.PrefetchScalarGridSpec(
            num_scalar_prefetch=1,
            grid=(count,),
            in_specs=[by_row(a.shape) for a in rows] + [whole(small.shape)] + [hbm] * (n_sources + len(after)),
            out_specs=out_specs,
            scratch_shapes=scratches + list(scratch),
        ),
        out_shape=shapes,
        compiler_params=pltpu.CompilerParams(dimension_semantics=("arbitrary",), vmem_limit_bytes=VMEM_LIMIT),
        cost_estimate=pl.CostEstimate(flops=COST, bytes_accessed=COST, transcendentals=0),
        name=name,
    )(meta, *rows, small, *[v for _, s, _ in parts for v in s], *after)
    n = len(out_rows)
    given, sums, rest = result[:n], result[n : n + len(backs)], list(result[n + len(backs) :])
    grads = []
    for layout in backs:
        k = len(layout.grad_shapes())
        grads.append(rest[:k])
        rest = rest[k:]
    return given, sums, grads


def lookup(pair_order, lengths):
    indices = jnp.arange(lengths.shape[0], dtype=jnp.int32)
    chosen = jnp.where(pair_order[:, None] == indices[None, :], lengths[None, :], 0)
    return jnp.sum(chosen, axis=1)


class Step:
    def __init__(self, layouts, source, target, cotangent, meta):
        self.layouts, self.meta = layouts, meta
        self.source, self.target, self.cotangent = source, target, cotangent
        self.count, self.size, self.width = source.shape
        self.hidden = layouts[ENC_FFN].shapes[0][1]
        pairs = self.width // PAIR
        self.shares = jax.ShapeDtypeStruct((self.count, pairs, 2 * self.size, self.size), BF16)
        self.small, self.w = None, {}

    def f32(self, cols):
        return jax.ShapeDtypeStruct((self.count, self.size, cols), F32)

    def bf16(self, cols):
        return jax.ShapeDtypeStruct((self.count, self.size, cols), BF16)

    def run(self, kernel, name, groups, rows, out_rows, back=(), scratch=(), after=()):
        parts = [(self.layouts[g], self.w[g], g in back) for g in groups]
        return call(kernel, name, self.count, self.meta, rows, self.small, parts, list(after), out_rows, scratch)

    def rows_of(self, *columns):
        return [pltpu.VMEM((self.size, c), BF16) for c in columns]

    def enc_self_fwd(self, after=()):
        d = self.width

        def kernel(meta, step, small, uses, ins, outs, scratch):
            self_fwd(uses[0], small, *ins, *outs, meta[2 + step], False, ENC_BIAS)

        (self.h1, self.enc_qkv, self.enc_a, self.enc_o), _, _ = self.run(
            kernel, "enc_self_fwd", (ENC_SELF,), [self.source],
            [self.f32(d), self.bf16(3 * d), self.shares, self.bf16(d)], after=after,
        )

    def dec_self_fwd(self, after=()):
        d = self.width

        def kernel(meta, step, small, uses, ins, outs, scratch):
            self_fwd(uses[0], small, *ins, *outs, meta[2 + self.count + step], True, DEC_BIAS)

        (self.h3, self.dec_qkv, self.dec_a, self.dec_o), _, _ = self.run(
            kernel, "dec_self_fwd", (DEC_SELF,), [self.target],
            [self.f32(d), self.bf16(3 * d), self.shares, self.bf16(d)], after=after,
        )

    def enc_ffn_fwd(self, after=()):
        def kernel(meta, step, small, uses, ins, outs, scratch):
            ffn_fwd(uses[0], small, *ins, *outs)

        (self.h2, self.hid, self.slope), _, _ = self.run(
            kernel, "enc_ffn_fwd", (ENC_FFN,), [self.h1, self.source],
            [self.f32(self.width), self.bf16(self.hidden), self.bf16(self.hidden)], after=after,
        )

    def dec_middle(self, after=()):
        d = self.width

        def kernel(meta, step, small, uses, ins, outs, scratch):
            cross_fwd(uses[0], small, *ins[:2], *outs[:5], meta[2 + step])
            ffn_both(uses[1], small, outs[0], *ins[2:], *outs[5:], *scratch, meta[2 + self.count + step])

        rows, sums, grads = self.run(
            kernel, "dec_middle", (CROSS, DEC_FFN), [self.h3, self.h2, self.target, self.cotangent],
            [self.f32(d), self.bf16(d), self.bf16(2 * d), self.shares, self.bf16(d), self.bf16(d), self.f32(d),
             self.f32(d)],
            (DEC_FFN,), self.rows_of(self.hidden, self.hidden), after,
        )
        self.h4, self.q, self.kv, self.cross_a, self.cross_o, self.decoded, self.dd2, self.dh5 = rows
        self.sums_df = sums[0]
        return grads[0]

    def dec_bwd(self, after=()):
        d = self.width

        def kernel(meta, step, small, uses, ins, outs, scratch):
            dd2, h4, h3, h2, q, kv, cross_a, cross_o, target, dh5, qkv, a, o = ins
            go, gq, gkv, g = scratch
            dd1 = cross_bwd(uses[0], small, dd2[0], h4, h3, h2, q, kv, cross_a, cross_o, outs[0], go, gq, gkv)
            self_bwd(uses[1], small, dd1, h3, target, dh5, qkv, a, o, outs[1], go, g, DEC_GAIN)

        rows, (self.sums_c, self.sums_ds), grads = self.run(
            kernel, "dec_bwd", (CROSS, DEC_SELF),
            [self.dd2, self.h4, self.h3, self.h2, self.q, self.kv, self.cross_a, self.cross_o, self.target, self.dh5,
             self.dec_qkv, self.dec_a, self.dec_o],
            [self.f32(d), self.bf16(d)], (CROSS, DEC_SELF), self.rows_of(d, d, 2 * d, 3 * d), after,
        )
        self.dm, self.target_grad = rows
        return grads

    def enc_ffn_bwd(self, after=()):
        d = self.width

        def kernel(meta, step, small, uses, ins, outs, scratch):
            ffn_bwd(uses[0], small, *ins, *outs)

        (self.de1, self.dh2), (self.sums_ef,), grads = self.run(
            kernel, "enc_ffn_bwd", (ENC_FFN,), [self.dm, self.h2, self.h1, self.hid, self.slope],
            [self.f32(d), self.f32(d)], (ENC_FFN,), (), after,
        )
        return grads[0]

    def enc_self_bwd(self, after=()):
        d = self.width

        def kernel(meta, step, small, uses, ins, outs, scratch):
            self_bwd(uses[0], small, ins[0][0], *ins[1:], *outs, *scratch, ENC_GAIN)

        (self.source_grad,), (self.sums_es,), grads = self.run(
            kernel, "enc_self_bwd", (ENC_SELF,),
            [self.de1, self.h1, self.source, self.dh2, self.enc_qkv, self.enc_a, self.enc_o], [self.bf16(d)],
            (ENC_SELF,), self.rows_of(d, 3 * d), after,
        )
        return grads[0]

    def small_sums(self):
        es, ef, ds, c, df = self.sums_es, self.sums_ef, self.sums_ds, self.sums_c, self.sums_df
        return jnp.concatenate(
            [es[0:3], ef[0:1], es[3:4], ef[1:2], es[4:5], ef[2:3], ds[0:3], c[0:3], df[0:1], ds[3:4], c[3:4], df[1:2],
             ds[4:5], c[4:5], df[2:3], jnp.zeros((3, self.width), F32), ef[4:8], df[4:8]], axis=0,
        )


def simple(kernel, name, meta, inputs, outs, scratch=(), after=()):
    specs = [pl.BlockSpec(memory_space=pltpu.VMEM)] * len(inputs)
    specs += [pl.BlockSpec(memory_space=pl.ANY)] * len(after)

    def body(meta, *refs):
        return kernel(meta, *refs[: len(inputs)], *refs[len(inputs) + len(after) :])

    return pl.pallas_call(
        body,
        in_specs=[pl.BlockSpec(memory_space=pltpu.SMEM)] + specs,
        out_specs=[pl.BlockSpec(memory_space=pltpu.VMEM)] * len(outs),
        out_shape=list(outs),
        scratch_shapes=list(scratch),
        compiler_params=pltpu.CompilerParams(vmem_limit_bytes=VMEM_LIMIT),
        cost_estimate=pl.CostEstimate(flops=COST, bytes_accessed=COST, transcendentals=0),
        name=name,
    )(meta, *inputs, *after)


def pack_kernel(plan, nz, meta, *refs):
    n_in = sum(len(p) for p in plan)
    shards = refs[:n_in]
    small_refs = refs[n_in : n_in + len(SMALLS) + len(LINES)]
    outs = refs[n_in + len(small_refs) : -1]
    rows = refs[-1]
    at = 0
    for out, chunk in zip(outs, plan):
        for row in chunk:
            shard = shards[at]
            rd, cols = shard.shape
            for cb in range(cols // TILE):
                out[row + cb * rd : row + (cb + 1) * rd, :] = shard[:, cb * TILE : (cb + 1) * TILE]
            at += 1
    rank = meta[0] * nz + meta[1]
    rows[...] = jnp.zeros_like(rows)
    for ref, (_, row, _) in zip(small_refs, SMALLS + LINES):
        lines, part = ref.shape
        lane = lax.broadcasted_iota(jnp.int32, (part, TILE), 1)
        spread = (lane % part == lax.broadcasted_iota(jnp.int32, (part, TILE), 0)).astype(BF16)
        tiled = nn(ref[...], spread)
        across = lax.broadcasted_iota(jnp.int32, (lines, TILE), 1)
        if row >= ENC_FFN_BIAS:
            per = TILE // part
            tiled = jnp.broadcast_to(tiled, (4, TILE))
            across = lax.broadcasted_iota(jnp.int32, (4, TILE), 1)
            down = lax.broadcasted_iota(jnp.int32, (4, TILE), 0)
            ok = (across // part == rank % per) & (down == rank // per)
            rows[row : row + 4, :] = jnp.where(ok, tiled, 0.0)
        else:
            rows[row : row + lines, :] = jnp.where(across // part == rank, tiled, 0.0)
    outs[0][outs[0].shape[0] - SMALL_ROWS :, :] = rows[...].astype(BF16)


def along_z_kernel(nz, rows, tail, meta, *refs):
    parts = refs[:nz]
    out = refs[nz]
    z = meta[1]
    for s in range(nz):
        at = pl.multiple_of(((z + nz - s) % nz) * rows, 16)
        out[pl.ds(at, rows), :] = parts[s][:rows, :]
    if tail:
        total = parts[0][rows:, :].astype(F32)
        for s in range(1, nz):
            total = total + parts[s][rows:, :].astype(F32)
        out[nz * rows :, :] = total.astype(BF16)


def add_cores_kernel(counts, tail, halves, meta, *refs):
    n = len(counts)
    outs = refs[2 * n + 2 * bool(tail) :]
    chips, nz = refs[0].shape[:2]
    total = sum(counts)
    for k in range(chips):
        out = outs[k % 2].at[k // 2] if halves else outs[k]
        for z in range(nz):
            at = z * total
            for g, rows in enumerate(counts):
                out[at : at + rows, :] = (
                    refs[2 * g][k, z].astype(F32) + refs[2 * g + 1][k, z].astype(F32)
                ).astype(BF16)
                at += rows
        if tail:
            out[nz * total :, :] = (refs[2 * n][...].astype(F32) + refs[2 * n + 1][...].astype(F32)).astype(BF16)


def add_half_kernel(meta, kept, got, own, second):
    own[...] = (kept[0].astype(F32) + got[0].astype(F32)).astype(BF16)
    second[...] = (kept[1].astype(F32) + got[1].astype(F32)).astype(BF16)


def add_chips_kernel(nz, rows, tail, n_parts, meta, *refs):
    parts, outs = refs[:n_parts], refs[n_parts:]
    z = meta[1]
    for s in range(nz):
        at = pl.multiple_of(((z + s) % nz) * rows, 16)
        total = parts[0][pl.ds(at, rows), :].astype(F32)
        for part in parts[1:]:
            total = total + part[pl.ds(at, rows), :].astype(F32)
        outs[s][:rows, :] = total.astype(outs[s].dtype)
    if tail:
        total = parts[0][nz * rows :, :].astype(F32)
        for part in parts[1:]:
            total = total + part[nz * rows :, :].astype(F32)
        for s in range(nz):
            outs[s][rows:, :] = total.astype(outs[s].dtype)


def add_z_kernel(nz, places, rows, tail, meta, *refs):
    parts, outs = refs[:nz], refs[nz:]
    for (row, rd, cols), out in zip(places, outs):
        for cb in range(cols // TILE):
            at = row + cb * rd
            total = parts[0][at : at + rd, :].astype(F32)
            for part in parts[1:]:
                total = total + part[at : at + rd, :].astype(F32)
            out[:, cb * TILE : (cb + 1) * TILE] = total
    if tail:
        rank = meta[0] * nz + meta[1]
        total = parts[0][rows:, :]
        for part in parts[1:]:
            total = total + part[rows:, :].astype(F32)
        for out, (_, row, _) in zip(outs[len(places) :], SMALLS + LINES):
            lines, part = out.shape
            if row >= ENC_FFN_BIAS:
                per = TILE // part
                down = lax.broadcasted_iota(jnp.int32, (8, TILE), 0)
                base = total[24:32, :]
                picked = jnp.sum(
                    jnp.where(down == rank // per + (row - 24), base, 0.0), axis=0, keepdims=True
                )
                moved = pltpu.roll(jnp.broadcast_to(picked, (8, TILE)), TILE - (rank % per) * part, 1)
                out[...] = moved[0:1, :part]
            else:
                first = row // 8 * 8
                moved = pltpu.roll(total[first : first + 24 if first < 8 else 24, :], TILE - rank * part, 1)
                out[...] = moved[row - first : row - first + lines, :part]


def swap(v, size, mask):
    return lax.ppermute(v, DP, [(i, i ^ mask) for i in range(size)])


def shift(v, size, by):
    return lax.ppermute(v, FSDP, [(i, (i + by) % size) for i in range(size)])


def across(v, size, own, other):
    return lax.ppermute(v, DP, [(i, i ^ (other if i % 2 else own)) for i in range(size)])


def hold(values, *first):
    return lax.optimization_barrier((values, first))[0]


class Exchange:
    def __init__(self, layouts, meta, nd, nz):
        self.layouts, self.meta, self.nd, self.nz = layouts, meta, nd, nz

    def pack(self, shards):
        plan, sizes, inputs = [], [], []
        for groups in GATHERS:
            rows, first = [], 0
            for g in groups:
                self.layouts[g].first = first
                for n, at in zip(self.layouts[g].names, self.layouts[g].offsets):
                    rows.append(first + at)
                    inputs.append(shards[n])
                first += self.layouts[g].rows
            for g in groups:
                self.layouts[g].span = first
            plan.append(rows)
            sizes.append(first)
        inputs += [shards[n] for n, _, _ in SMALLS] + [shards[n].reshape(1, -1) for n, _, _ in LINES]
        self.sizes = sizes
        self.tails = [SMALL_ROWS] + [0] * (len(GATHERS) - 1)
        return simple(
            functools.partial(pack_kernel, plan, self.nz), "pack", self.meta, inputs,
            [jax.ShapeDtypeStruct((r + t, TILE), BF16) for r, t in zip(sizes, self.tails)],
            [pltpu.VMEM((SMALL_ROWS, TILE), F32)],
        )

    def gather_z(self, pack):
        return [pack] + [shift(pack, self.nz, s) for s in range(1, self.nz)]

    def join_z(self, c, parts):
        rows, tail = self.sizes[c], self.tails[c]
        return simple(
            functools.partial(along_z_kernel, self.nz, rows, tail), "join", self.meta, parts,
            [jax.ShapeDtypeStruct((self.nz * rows + tail, TILE), BF16)],
        )[0]

    def gather_chips(self, joined, *before):
        first = across(joined, self.nd, 4, 2)
        second = across(joined, self.nd, 2, 4)
        if before:
            first = hold(first, *before)
        return [joined, first, second, across(first, self.nd, 2, 4)]

    def gather_cores(self, pieces):
        return [v for piece in pieces for v in (piece, swap(piece, self.nd, 1))]

    def to_cores(self, grads):
        return [grads[0], swap(grads[1], self.nd, 1)]

    def add_cores(self, groups, parts, tail=None, halves=False):
        counts = [self.layouts[g].rows for g in groups]
        extra = 0 if tail is None else SMALL_ROWS
        if extra:
            parts = parts + [tail, swap(tail, self.nd, 1)]
        return simple(
            functools.partial(add_cores_kernel, counts, extra, halves), "add_cores", self.meta, parts,
            [jax.ShapeDtypeStruct(((2,) if halves else ()) + (self.nz * sum(counts) + extra, TILE), BF16)]
            * (2 if halves else self.nd // 2),
        )

    def add_half(self, kept, got):
        shape = jax.ShapeDtypeStruct(kept.shape[1:], BF16)
        return simple(add_half_kernel, "add_half", self.meta, [kept, got], [shape, shape])

    def to_first(self, v):
        return across(v, self.nd, 4, 2)

    def to_second(self, v):
        return across(v, self.nd, 2, 4)

    def to_chips(self, sums):
        return [sums[0], self.to_first(sums[1]), self.to_second(sums[2]), swap(sums[3], self.nd, 6)]

    def add_chips(self, groups, parts, extra=0):
        rows = sum(self.layouts[g].rows for g in groups)
        return simple(
            functools.partial(add_chips_kernel, self.nz, rows, extra, len(parts)), "add_chips", self.meta, parts,
            [jax.ShapeDtypeStruct((rows + extra, TILE), F32 if s == 0 else BF16) for s in range(self.nz)],
        )

    def to_z(self, sums):
        return [sums[0]] + [shift(sums[s], self.nz, s) for s in range(1, self.nz)]

    def add_z(self, groups, parts, extra=0):
        ranks, first, places = self.nd * self.nz, 0, []
        for g in groups:
            layout = self.layouts[g]
            places += [(first + at, r // ranks, c) for at, (r, c) in zip(layout.offsets, layout.shapes)]
            first += layout.rows
        outs = [jax.ShapeDtypeStruct((rd, c), F32) for _, rd, c in places]
        if extra:
            wide = TILE // ranks
            outs += [jax.ShapeDtypeStruct((lines, wide), F32) for _, _, lines in SMALLS]
            outs += [jax.ShapeDtypeStruct((1, 4 * wide), F32)] * 2
        return simple(
            functools.partial(add_z_kernel, len(parts), places, first, extra), "add_z", self.meta, parts, outs
        )


def by_pieces(layouts, source, target, cotangent, meta, shards, nd, nz):
    ex = Exchange(layouts, meta, nd, nz)
    st = Step(layouts, source, target, cotangent, meta)
    packs = ex.pack(shards)
    joined0 = ex.join_z(0, ex.gather_z(packs[0]))
    along1 = ex.gather_z(hold(packs[1], joined0))
    pieces = ex.gather_cores(hold(ex.gather_chips(joined0), along1))
    st.w[ENC_SELF] = pieces
    st.small = sum(p[p.shape[0] - SMALL_ROWS :].astype(F32) for p in pieces)
    joined1 = ex.join_z(1, along1)
    along2 = ex.gather_z(hold(packs[2], joined1))
    st.enc_self_fwd(after=[joined1])
    along2 = hold(along2, st.h1)
    chips1 = ex.gather_chips(joined1, along2)
    joined2 = ex.join_z(2, hold(along2, chips1[1]))
    st.w[ENC_FFN] = st.w[DEC_SELF] = ex.gather_cores(hold(chips1, joined2))
    st.dec_self_fwd(after=[joined2])
    chips2 = ex.gather_chips(joined2, st.h3)
    st.enc_ffn_fwd(after=[chips2[1]])
    st.w[CROSS] = st.w[DEC_FFN] = ex.gather_cores(hold(chips2, st.h2))
    result = [None] * len(shards)

    def put(groups, outs):
        names = [n for g in groups for n in GROUPS[g]]
        names += [n for n, _, _ in SMALLS + LINES]
        for n, v in zip(names, outs):
            result[n] = v.reshape(shards[n].shape)

    df = st.dec_middle()[0]
    df = lax.psum_scatter(df.reshape(nd, nz, *df.shape[1:]), DP, scatter_dimension=0, tiled=True)
    both = (CROSS, DEC_SELF)
    cr, ds = st.dec_bwd()
    cr = ex.to_chips(ex.add_cores(both, ex.to_cores(cr) + ex.to_cores(ds)))
    ef = st.enc_ffn_bwd(after=[cr[0]])
    cr, df = hold((cr, df), st.de1)
    ef = ex.to_cores(hold(ef, cr))
    cr = ex.add_chips(both, cr)
    df = lax.psum_scatter(hold(df, cr[0]), FSDP, scatter_dimension=1, tiled=True)
    cr = ex.to_z(cr)
    ef_kept, ef = ex.add_cores((ENC_FFN,), hold(ef, cr[0]), halves=True)
    ef = ex.to_first(ef)
    es = st.enc_self_bwd(after=[cr[0], ef_kept])
    cr, ef = hold((cr, ef), st.source_grad)
    es = ex.to_cores(hold(es, cr, ef))
    tail = hold(st.small_sums().astype(BF16), cr, ef)
    ef_own, ef = ex.add_half(ef_kept, ef)
    ef = ex.to_second(ef)
    es = ex.to_chips(ex.add_cores((ENC_SELF,), hold(es, ef_own), tail))
    put(both, ex.add_z(both, hold(cr, es[0])))
    ef = ex.to_z(ex.add_chips((ENC_FFN,), hold([ef_own, ef], es[0])))
    es = ex.to_z(ex.add_chips((ENC_SELF,), hold(es, ef[0]), SMALL_ROWS))
    put((ENC_FFN,), ex.add_z((ENC_FFN,), hold(ef, es[0])))
    df = hold(df, es[0])
    put((DEC_FFN,), ex.add_z((DEC_FFN,), [df.reshape(df.shape[2:])]))
    es = hold(es, result[A_DEC_IN])
    put((ENC_SELF,), ex.add_z((ENC_SELF,), es, SMALL_ROWS))
    return (st.decoded, st.source_grad, st.target_grad) + tuple(result)


def whole(layouts, source, target, cotangent, meta, shards):
    small_names = [n for n, _, _ in SMALLS]
    full = [
        lax.all_gather(v, AXES, axis=1 if n in small_names else 0, tiled=True) for n, v in enumerate(shards)
    ]
    width = source.shape[2]
    st = Step(layouts, source, target, cotangent, meta)
    st.small = jnp.concatenate(
        [full[n] for n in small_names]
        + [jnp.zeros((3, width), BF16)]
        + [full[n].reshape(-1, width) for n, _, _ in LINES],
        axis=0,
    ).astype(F32)
    st.w = {g: [full[n] for n in names] for g, names in enumerate(GROUPS)}
    st.enc_self_fwd()
    st.enc_ffn_fwd()
    st.dec_self_fwd()
    grads = [None] * len(GROUPS)
    grads[DEC_FFN] = st.dec_middle()
    grads[CROSS], grads[DEC_SELF] = st.dec_bwd()
    grads[ENC_FFN] = st.enc_ffn_bwd()
    grads[ENC_SELF] = st.enc_self_bwd()
    sums = st.small_sums()
    result = [None] * len(shards)
    for g, names in enumerate(GROUPS):
        for n, v in zip(names, grads[g]):
            result[n] = v.astype(F32)
    for n, row, lines in SMALLS:
        result[n] = sums[row : row + lines]
    for n, row, _ in LINES:
        result[n] = sums[row : row + 4].reshape(-1)
    result = [
        lax.psum_scatter(v, AXES, scatter_dimension=1 if n in small_names else 0, tiled=True)
        for n, v in enumerate(result)
    ]
    return (st.decoded, st.source_grad, st.target_grad) + tuple(result)


def local(nd, nz, source, target, cotangent, pair_order, source_lengths, target_lengths, *shards):
    ranks = nd * nz
    matrices = [n for names in GROUPS for n in names]
    shapes = {n: (shards[n].shape[0] * ranks, shards[n].shape[1]) for n in matrices}
    pieces = nd == 8 and all(shards[n].shape[0] % 16 == 0 for n in matrices)
    modes = (PIECES, PIECES, PIECES, PIECES, RANKS) if pieces else (WHOLE,) * len(GROUPS)
    layouts = [Layout(g, shapes, modes[g], nd, nz) for g in range(len(GROUPS))]
    meta = jnp.concatenate(
        [
            jnp.stack([lax.axis_index(DP), lax.axis_index(FSDP)]).astype(jnp.int32),
            lookup(pair_order, source_lengths),
            lookup(pair_order, target_lengths),
        ]
    )
    if pieces:
        return by_pieces(layouts, source, target, cotangent, meta, shards, nd, nz)
    return whole(layouts, source, target, cotangent, meta, shards)


def specs():
    split, rows, cols = P(AXES, None, None), P(AXES, None), P(None, AXES)
    line = P(AXES)
    weights = (
        rows, rows, rows, rows, cols, line, cols, cols,
        rows, rows, rows, rows, rows, rows, rows, cols, line, cols, cols,
    )
    return (split, split, split, line, P(), P()) + weights, (split, split, split) + weights


def solution(mesh):
    in_specs, out_specs = specs()
    return jax.shard_map(
        functools.partial(local, mesh.shape[DP], mesh.shape[FSDP]),
        mesh=mesh, in_specs=in_specs, out_specs=out_specs, check_vma=False,
    )
```

```python
import functools

import jax
import jax.numpy as jnp
from jax import lax
from jax.experimental import pallas as pl
from jax.experimental.pallas import tpu as pltpu
from jax.sharding import PartitionSpec as P

F32 = jnp.float32
BF16 = jnp.bfloat16
DP, FSDP = "dp", "fsdp"
AXES = (DP, FSDP)
HEAD_DIM = 64
PAIR = 2 * HEAD_DIM
TILE = 512
epsilon = 1e-05
FORWARD_TILE = 256
COST = 1
SIMPLE_LIMIT = 16 * 1024 * 1024
VMEM_LIMIT = 56 * 1024 * 1024

ENC_BIAS, ENC_GAIN, ENC_SHIFT = 0, 4, 6
DEC_BIAS, DEC_GAIN, DEC_SHIFT = 8, 15, 18
ENC_FFN_BIAS, DEC_FFN_BIAS = 24, 28
SMALL_ROWS = 32

(A_ENC_QKV, A_ENC_OUT, A_ENC_IN, A_ENC_BACK, A_ENC_BIAS, A_ENC_FBIAS, A_ENC_GAIN, A_ENC_SHIFT, A_DEC_QKV, A_DEC_OUT,
 A_CROSS_Q, A_CROSS_KV, A_CROSS_OUT, A_DEC_IN, A_DEC_BACK, A_DEC_BIAS, A_DEC_FBIAS, A_DEC_GAIN, A_DEC_SHIFT) = range(19)
ENC_SELF, ENC_FFN, DEC_SELF, CROSS, DEC_FFN = range(5)
GROUPS = (
    (A_ENC_QKV, A_ENC_OUT),
    (A_ENC_IN, A_ENC_BACK),
    (A_DEC_QKV, A_DEC_OUT),
    (A_CROSS_Q, A_CROSS_KV, A_CROSS_OUT),
    (A_DEC_IN, A_DEC_BACK),
)
SMALLS = (
    (A_ENC_BIAS, ENC_BIAS, 4), (A_ENC_GAIN, ENC_GAIN, 2), (A_ENC_SHIFT, ENC_SHIFT, 2),
    (A_DEC_BIAS, DEC_BIAS, 7), (A_DEC_GAIN, DEC_GAIN, 3), (A_DEC_SHIFT, DEC_SHIFT, 3),
)
LINES = ((A_ENC_FBIAS, ENC_FFN_BIAS, 1), (A_DEC_FBIAS, DEC_FFN_BIAS, 1))
WHOLE, PIECES, RANKS = range(3)
GATHERS = ((ENC_SELF,), (ENC_FFN, DEC_SELF), (CROSS, DEC_FFN))


def nn(a, b):
    return lax.dot_general(a, b, (((1,), (0,)), ((), ())), preferred_element_type=F32)


def nt(a, b):
    return lax.dot_general(a, b, (((1,), (1,)), ((), ())), preferred_element_type=F32)


def tn(a, b):
    return lax.dot_general(a, b, (((0,), (0,)), ((), ())), preferred_element_type=F32)


def tokens_sum(v):
    return jnp.sum(v, axis=0, keepdims=True)


def normalize(h):
    c = h - jnp.mean(h, axis=-1, keepdims=True)
    r = lax.rsqrt(jnp.mean(c * c, axis=-1, keepdims=True) + epsilon)
    return c * r, r


def norm_back(dv, xh, r, g):
    hh = dv * g
    return r * (
        hh - jnp.mean(hh, axis=-1, keepdims=True) - xh * jnp.mean(hh * xh, axis=-1, keepdims=True)
    )


def gelu_parts(u):
    c = 0.7978845608028654
    sq = u * u
    t = jnp.tanh(u * (c + (c * 0.044715) * sq))
    half = 0.5 * (1.0 + t)
    slope = half + (0.5 * u) * (1.0 - t * t) * (c + (3.0 * c * 0.044715) * sq)
    return u * half, slope


class Layout:
    def __init__(self, group, shapes, mode, nd, nz):
        self.names = GROUPS[group]
        self.mode = mode
        self.shapes = [shapes[n] for n in self.names]
        self.span = 0
        self.nd, self.nz = nd, nz
        self.offsets, row = [], 0
        for rows, cols in self.shapes:
            self.offsets.append(row)
            row += (rows // (nd * nz)) * (cols // TILE)
        self.rows = row
        self.first = 0

    def n_sources(self):
        return len(self.names) if self.mode == WHOLE else self.nd

    def w_scratch(self):
        return [pltpu.VMEM(s, BF16) for s in self.shapes] + [
            pltpu.SemaphoreType.DMA((len(self.shapes),))
        ]

    def acc_scratch(self):
        return (
            [pltpu.VMEM(s, F32) for s in self.shapes]
            + [pltpu.VMEM(s, BF16) for s in self.shapes]
            + [pltpu.SemaphoreType.DMA((len(self.shapes),))]
        )

    def start_loads(self, sources, weights, sems, dp, order):
        for j in order:
            rows, cols = self.shapes[j]
            if self.mode == WHOLE:
                pltpu.make_async_copy(sources[j], weights[j], sems.at[j]).start()
                continue
            rd = rows // (self.nd * self.nz)
            view = weights[j].reshape(self.nd, self.nz, rd, cols)
            for m in range(self.nd):
                mask = self.masks(dp)[m]
                for cb in range(cols // TILE):
                    pltpu.make_async_copy(
                        sources[m]
                        .at[pl.ds(0, self.nz * self.span), :]
                        .reshape(self.nz, self.span, TILE)
                        .at[:, pl.ds(self.first + self.offsets[j] + cb * rd, rd), :],
                        view.at[dp ^ mask, :, :, pl.ds(cb * TILE, TILE)],
                        sems.at[j],
                    ).start()

    def masks(self, dp):
        first = jnp.where(dp % 2 == 0, 4, 2)
        return [0, 1, first, 7 - first, 6 - first, first + 1, 6, 7]

    def wait_load(self, weights, sems, j):
        pltpu.make_async_copy(weights[j], weights[j], sems.at[j]).wait()

    def grad_shapes(self):
        if self.mode == WHOLE:
            return [jax.ShapeDtypeStruct(s, BF16) for s in self.shapes]
        if self.mode == RANKS:
            return [jax.ShapeDtypeStruct((self.nd * self.nz, self.rows, TILE), BF16)]
        return [jax.ShapeDtypeStruct((self.nd // 2, self.nz, self.rows, TILE), BF16)] * 2

    def start_store(self, acc, stage, outs, sems, dp, j):
        rows, cols = self.shapes[j]
        stage[j][...] = acc[j][...].astype(BF16)
        if self.mode == WHOLE:
            pltpu.make_async_copy(stage[j], outs[j], sems.at[j]).start()
            return
        rd = rows // (self.nd * self.nz)
        if self.mode == RANKS:
            view = stage[j].reshape(self.nd * self.nz, rd, cols)
            for cb in range(cols // TILE):
                pltpu.make_async_copy(
                    view.at[:, :, pl.ds(cb * TILE, TILE)],
                    outs[0].at[:, pl.ds(self.offsets[j] + cb * rd, rd), :],
                    sems.at[j],
                ).start()
            return
        view = stage[j].reshape(self.nd, self.nz, rd, cols)
        for m, mask in enumerate(self.masks(dp)):
            for cb in range(cols // TILE):
                pltpu.make_async_copy(
                    view.at[dp ^ mask, :, :, pl.ds(cb * TILE, TILE)],
                    outs[m % 2].at[m // 2, :, pl.ds(self.offsets[j] + cb * rd, rd), :],
                    sems.at[j],
                ).start()

    def wait_store(self, stage, sems, j):
        pltpu.make_async_copy(stage[j], stage[j], sems.at[j]).wait()


class Use:
    def __init__(self, layout, step, dp, last, sources, weights, wsem):
        self.layout, self.step, self.dp, self.last = layout, step, dp, last
        self.sources, self.w, self.wsem = sources, weights, wsem
        self.acc = ()

    def add_sums(self, sg, grads, acc, stage, gsem):
        self.sg, self.grads, self.acc, self.stage, self.gsem = sg, grads, acc, stage, gsem

    def begin(self, order):
        @pl.when(self.step == 0)
        def _():
            self.layout.start_loads(self.sources, self.w, self.wsem, self.dp, order)
            if self.acc:
                for ref in self.acc:
                    ref[...] = jnp.zeros_like(ref)
                self.sg[...] = jnp.zeros_like(self.sg)

    def ready(self, *which):
        @pl.when(self.step == 0)
        def _():
            for j in which:
                self.layout.wait_load(self.w, self.wsem, j)

    def sums(self, row, v, at=0):
        self.sg[row : row + 1, at : at + v.shape[1]] += tokens_sum(v)

    def send(self, *which):
        @pl.when(self.last)
        def _():
            for j in which:
                self.layout.start_store(self.acc, self.stage, self.grads, self.gsem, self.dp, j)

    def end(self):
        @pl.when(self.last)
        def _():
            for j in range(len(self.layout.names)):
                self.layout.wait_store(self.stage, self.gsem, j)


def low_lanes(rows):
    return lax.broadcasted_iota(jnp.int32, (rows, PAIR), 1) < HEAD_DIM


def split_pair(v):
    low = low_lanes(v.shape[0])
    zero = jnp.zeros_like(v)
    return jnp.concatenate([jnp.where(low, v, zero), jnp.where(low, zero, v)], axis=0)


def allowed_keys(length, causal, size):
    col = lax.broadcasted_iota(jnp.int32, (size, size), 1)
    ok = col < length
    if causal:
        ok = ok & (col <= lax.broadcasted_iota(jnp.int32, (size, size), 0))
    return ok


def pair_forward(q, k, v, ok):
    size = q.shape[0]
    s = nt(split_pair(q), k)
    s = jnp.where(jnp.concatenate([ok, ok], axis=0), s, -1e30)
    e = jnp.exp(s - jnp.max(s, axis=-1, keepdims=True))
    a = (e * (1.0 / jnp.sum(e, axis=-1, keepdims=True))).astype(BF16)
    mixed = nn(jnp.concatenate([a[:size], a[size:]], axis=1), split_pair(v))
    return a, mixed


def pair_backward(q, k, v, a, g):
    size = q.shape[0]
    g2 = split_pair(g)
    af = a.astype(F32)
    da = nt(g2, v)
    ds = (af * (da - jnp.sum(af * da, axis=-1, keepdims=True))).astype(BF16)
    dv = tn(g2, a).T
    dk = tn(split_pair(q), ds).T
    dq = nn(jnp.concatenate([ds[:size], ds[size:]], axis=1), split_pair(k))
    return dq * (HEAD_DIM**-0.5), dk, dv


def row(small, at):
    return small[at : at + 1]


def attention_fwd(q, k, v, ok, a_ref, o_ref):
    for p in range(a_ref.shape[1]):
        at = p * PAIR
        a, mixed = pair_forward(q(at), k(at), v(at), ok)
        a_ref[0, p] = a
        o_ref[0, :, at : at + PAIR] = mixed.astype(BF16)


def self_fwd(use, small, x_ref, h_ref, qkv_ref, a_ref, o_ref, length, causal, bias):
    size, width = x_ref.shape[1:]
    w = use.w
    use.begin((0, 1))
    ok = allowed_keys(length, causal, size)
    use.ready(0)
    x = x_ref[0]
    q = (nn(x, w[0][:, :width]) + row(small, bias)) * (HEAD_DIM**-0.5)
    qkv_ref[0, :, :width] = q.astype(BF16)
    qkv_ref[0, :, width : 2 * width] = nn(x, w[0][:, width : 2 * width]).astype(BF16)
    qkv_ref[0, :, 2 * width :] = (nn(x, w[0][:, 2 * width :]) + row(small, bias + 1)).astype(BF16)

    def part(k):
        return lambda at: qkv_ref[0, :, k * width + at : k * width + at + PAIR]

    attention_fwd(part(0), part(1), part(2), ok, a_ref, o_ref)
    use.ready(1)
    h_ref[0] = x.astype(F32) + nn(o_ref[0], w[1][...]) + row(small, bias + 2)


def decoder_first(small, h3_ref):
    return normalize(h3_ref[0])[0] * row(small, DEC_GAIN) + row(small, DEC_SHIFT)


def memory_rows(small, h2_ref):
    return (normalize(h2_ref[0])[0] * row(small, ENC_GAIN + 1) + row(small, ENC_SHIFT + 1)).astype(BF16)


def cross_fwd(use, small, h3_ref, h2_ref, h_ref, q_ref, kv_ref, a_ref, o_ref, length):
    size, width = h3_ref.shape[1:]
    w = use.w
    use.begin((0, 1, 2))
    ok = allowed_keys(length, False, size)
    first = decoder_first(small, h3_ref)
    memory = memory_rows(small, h2_ref)
    use.ready(0)
    q = (nn(first.astype(BF16), w[0][...]) + row(small, DEC_BIAS + 3)) * (HEAD_DIM**-0.5)
    q_ref[0] = q.astype(BF16)
    use.ready(1)
    kv_ref[0, :, :width] = nn(memory, w[1][:, :width]).astype(BF16)
    kv_ref[0, :, width:] = (nn(memory, w[1][:, width:]) + row(small, DEC_BIAS + 4)).astype(BF16)
    attention_fwd(
        lambda at: q_ref[0, :, at : at + PAIR],
        lambda at: kv_ref[0, :, at : at + PAIR],
        lambda at: kv_ref[0, :, width + at : width + at + PAIR],
        ok, a_ref, o_ref,
    )
    use.ready(2)
    h_ref[0] = first + nn(o_ref[0], w[2][...]) + row(small, DEC_BIAS + 5)


def ffn_steps(use, small, low, total, ffn_bias, hid_put, slope_put):
    w = use.w
    hidden = w[0].shape[1]
    use.ready(0, 1)
    for at in range(0, hidden, FORWARD_TILE):
        cols = slice(at, at + FORWARD_TILE)
        lane = at % TILE
        bias = small[ffn_bias + at // TILE : ffn_bias + at // TILE + 1, lane : lane + FORWARD_TILE]
        hid, slope = gelu_parts(nn(low, w[0][:, cols]) + bias)
        hid = hid.astype(BF16)
        hid_put(cols, hid)
        slope_put(cols, slope.astype(BF16))
        total = total + nn(hid, w[1][cols, :])
    return total


def ffn_fwd(use, small, h1_ref, x_ref, h_ref, hid_ref, slope_ref):
    use.begin((0, 1))
    first = normalize(h1_ref[0])[0] * row(small, ENC_GAIN) + row(small, ENC_SHIFT)
    total = first + row(small, ENC_BIAS + 3) + x_ref[0].astype(F32)

    def hid_put(cols, v):
        hid_ref[0, :, cols] = v

    def slope_put(cols, v):
        slope_ref[0, :, cols] = v

    h_ref[0] = ffn_steps(use, small, first.astype(BF16), total, ENC_FFN_BIAS, hid_put, slope_put)


def ffn_back(use, low, hid, slope, g, wait=True):
    w, acc = use.w, use.acc
    acc[1][...] += nn(hid.T, g)
    use.send(1)
    if wait:
        use.ready(1)
    du = nt(g, w[1][...]) * slope.astype(F32)
    for t in range(du.shape[1] // TILE):
        use.sums(4 + t, du[:, t * TILE : (t + 1) * TILE])
    gu = du.astype(BF16)
    acc[0][...] += nn(low.T, gu)
    use.send(0)
    if wait:
        use.ready(0)
    return nt(gu, w[0][...])


def ffn_both(use, small, h4_ref, x_ref, cot_ref, out_ref, dd2_ref, dh5_ref, hid_s, slope_s, length):
    size, width = x_ref.shape[1:]
    use.begin((0, 1))
    second = normalize(h4_ref[0])[0] * row(small, DEC_GAIN + 1) + row(small, DEC_SHIFT + 1)
    low = second.astype(BF16)
    total = second + row(small, DEC_BIAS + 6) + x_ref[0].astype(F32)

    def hid_put(cols, v):
        hid_s[:, cols] = v

    def slope_put(cols, v):
        slope_s[:, cols] = v

    total = ffn_steps(use, small, low, total, DEC_FFN_BIAS, hid_put, slope_put)
    xh, r = normalize(total)
    gain = row(small, DEC_GAIN + 2)
    valid = lax.broadcasted_iota(jnp.int32, (size, width), 0) < length
    out_ref[0] = jnp.where(valid, xh * gain + row(small, DEC_SHIFT + 2), 0.0).astype(BF16)
    dv = jnp.where(valid, cot_ref[0].astype(F32), 0.0)
    dh = norm_back(dv, xh, r, gain)
    use.sums(0, dh)
    use.sums(1, dv * xh)
    use.sums(2, dv)
    dh5_ref[0] = dh
    dd2_ref[0] = dh + ffn_back(use, low, hid_s[...], slope_s[...], dh.astype(BF16), False)
    use.end()


def ffn_bwd(use, small, dm_ref, h2_ref, h1_ref, hid_ref, slope_ref, de1_ref, dh2_ref):
    use.begin((1, 0))
    low = (normalize(h1_ref[0])[0] * row(small, ENC_GAIN) + row(small, ENC_SHIFT)).astype(BF16)
    xh, r = normalize(h2_ref[0])
    dv = dm_ref[0]
    dh = norm_back(dv, xh, r, row(small, ENC_GAIN + 1))
    use.sums(0, dh)
    use.sums(1, dv * xh)
    use.sums(2, dv)
    dh2_ref[0] = dh
    de1_ref[0] = dh + ffn_back(use, low, hid_ref[0], slope_ref[0], dh.astype(BF16))
    use.end()


def attention_bwd(use, q, k, v, a_ref, go_s, put):
    for p in range(a_ref.shape[1]):
        at = p * PAIR
        dq, dk, dv = pair_backward(q(at), k(at), v(at), a_ref[0, p], go_s[:, at : at + PAIR])
        use.sums(0, dq, at)
        use.sums(1, dv, at)
        put(at, dq.astype(BF16), dk.astype(BF16), dv.astype(BF16))


def block_sums(use, dv, xh, dh):
    use.sums(2, dh)
    use.sums(3, dv * xh)
    use.sums(4, dv)


def self_bwd(use, small, dv, h_ref, x_ref, extra_ref, qkv_ref, a_ref, o_ref, dx_ref, go_s, g_s, gain_row):
    size, width = x_ref.shape[1:]
    w, acc = use.w, use.acc
    use.begin((1, 0))
    xh, r = normalize(h_ref[0])
    dh = norm_back(dv, xh, r, row(small, gain_row))
    block_sums(use, dv, xh, dh)
    g = dh.astype(BF16)
    acc[1][...] += nn(o_ref[0].T, g)
    use.send(1)
    use.ready(1)
    go_s[...] = nt(g, w[1][...]).astype(BF16)

    def part(k):
        return lambda at: qkv_ref[0, :, k * width + at : k * width + at + PAIR]

    def put(at, *parts):
        for k, v in enumerate(parts):
            g_s[:, k * width + at : k * width + at + PAIR] = v

    attention_bwd(use, part(0), part(1), part(2), a_ref, go_s, put)
    acc[0][...] += nn(x_ref[0].T, g_s[...])
    use.send(0)
    use.ready(0)
    dx_ref[0] = (dh + extra_ref[0] + nt(g_s[...], w[0][...])).astype(BF16)
    use.end()


def cross_bwd(use, small, dv, h4_ref, h3_ref, h2_ref, q_ref, kv_ref, a_ref, o_ref, dm_ref, go_s, gq_s, gkv_s):
    width = h4_ref.shape[2]
    w, acc = use.w, use.acc
    use.begin((2, 0, 1))
    first = decoder_first(small, h3_ref).astype(BF16)
    memory = memory_rows(small, h2_ref)
    xh, r = normalize(h4_ref[0])
    dh = norm_back(dv, xh, r, row(small, DEC_GAIN + 1))
    block_sums(use, dv, xh, dh)
    g = dh.astype(BF16)
    acc[2][...] += nn(o_ref[0].T, g)
    use.send(2)
    use.ready(2)
    go_s[...] = nt(g, w[2][...]).astype(BF16)

    def put(at, dq, dk, dvv):
        gq_s[:, at : at + PAIR] = dq
        gkv_s[:, at : at + PAIR] = dk
        gkv_s[:, width + at : width + at + PAIR] = dvv

    attention_bwd(
        use,
        lambda at: q_ref[0, :, at : at + PAIR],
        lambda at: kv_ref[0, :, at : at + PAIR],
        lambda at: kv_ref[0, :, width + at : width + at + PAIR],
        a_ref, go_s, put,
    )
    acc[0][...] += nn(first.T, gq_s[...])
    acc[1][...] += nn(memory.T, gkv_s[...])
    use.send(0, 1)
    use.ready(0, 1)
    dm_ref[0] = nt(gkv_s[...], w[1][...])
    out = dh + nt(gq_s[...], w[0][...])
    use.end()
    return out


def call(kernel, name, count, meta, rows, small, parts, after, out_rows, scratch):
    def by_row(shape):
        tail = tuple(shape[1:])
        return pl.BlockSpec((1,) + tail, lambda i, m, k=len(tail): (i,) + (0,) * k)

    def whole(shape):
        return pl.BlockSpec(tuple(shape), lambda i, m, k=len(shape): (0,) * k)

    width = small.shape[1]
    backs = [layout for layout, _, back in parts if back]
    shapes = list(out_rows) + [jax.ShapeDtypeStruct((8, width), F32)] * len(backs)
    for layout in backs:
        shapes += layout.grad_shapes()

    def body(meta, *refs):
        refs = list(refs)

        def next_refs(n):
            head = refs[:n]
            del refs[:n]
            return head

        ins = next_refs(len(rows))
        small_ref = next_refs(1)[0]
        sources = [next_refs(len(s)) for _, s, _ in parts]
        next_refs(len(after))
        outs = next_refs(len(out_rows))
        sums = next_refs(len(backs))
        grads = [next_refs(len(layout.grad_shapes())) for layout in backs]
        step = pl.program_id(0)
        last = step == count - 1
        uses, at = [], 0
        for (layout, _, back), src in zip(parts, sources):
            n = len(layout.names)
            use = Use(layout, step, meta[0], last, src, next_refs(n), next_refs(1)[0])
            if back:
                use.add_sums(sums[at], grads[at], next_refs(n), next_refs(n), next_refs(1)[0])
                at += 1
            uses.append(use)
        kernel(meta, step, small_ref, uses, ins, outs, refs)

    scratches = []
    for layout, _, back in parts:
        scratches += layout.w_scratch() + (layout.acc_scratch() if back else [])
    hbm = pl.BlockSpec(memory_space=pl.ANY)
    n_sources = sum(len(s) for _, s, _ in parts)
    out_specs = [by_row(v.shape) for v in out_rows] + [whole((8, width))] * len(backs)
    out_specs += [hbm] * (len(shapes) - len(out_specs))
    result = pl.pallas_call(
        body,
        grid_spec=pltpu.PrefetchScalarGridSpec(
            num_scalar_prefetch=1,
            grid=(count,),
            in_specs=[by_row(a.shape) for a in rows] + [whole(small.shape)] + [hbm] * (n_sources + len(after)),
            out_specs=out_specs,
            scratch_shapes=scratches + list(scratch),
        ),
        out_shape=shapes,
        compiler_params=pltpu.CompilerParams(dimension_semantics=("arbitrary",), vmem_limit_bytes=VMEM_LIMIT),
        cost_estimate=pl.CostEstimate(flops=COST, bytes_accessed=COST, transcendentals=0),
        name=name,
    )(meta, *rows, small, *[v for _, s, _ in parts for v in s], *after)
    n = len(out_rows)
    given, sums, rest = result[:n], result[n : n + len(backs)], list(result[n + len(backs) :])
    grads = []
    for layout in backs:
        k = len(layout.grad_shapes())
        grads.append(rest[:k])
        rest = rest[k:]
    return given, sums, grads


def lookup(pair_order, lengths):
    indices = jnp.arange(lengths.shape[0], dtype=jnp.int32)
    chosen = jnp.where(pair_order[:, None] == indices[None, :], lengths[None, :], 0)
    return jnp.sum(chosen, axis=1)


class Step:
    def __init__(self, layouts, source, target, cotangent, meta):
        self.layouts, self.meta = layouts, meta
        self.source, self.target, self.cotangent = source, target, cotangent
        self.count, self.size, self.width = source.shape
        self.hidden = layouts[ENC_FFN].shapes[0][1]
        pairs = self.width // PAIR
        self.shares = jax.ShapeDtypeStruct((self.count, pairs, 2 * self.size, self.size), BF16)
        self.small, self.w = None, {}

    def f32(self, cols):
        return jax.ShapeDtypeStruct((self.count, self.size, cols), F32)

    def bf16(self, cols):
        return jax.ShapeDtypeStruct((self.count, self.size, cols), BF16)

    def run(self, kernel, name, groups, rows, out_rows, back=(), scratch=(), after=()):
        parts = [(self.layouts[g], self.w[g], g in back) for g in groups]
        return call(kernel, name, self.count, self.meta, rows, self.small, parts, list(after), out_rows, scratch)

    def rows_of(self, *columns):
        return [pltpu.VMEM((self.size, c), BF16) for c in columns]

    def enc_self_fwd(self, after=()):
        d = self.width

        def kernel(meta, step, small, uses, ins, outs, scratch):
            self_fwd(uses[0], small, *ins, *outs, meta[2 + step], False, ENC_BIAS)

        (self.h1, self.enc_qkv, self.enc_a, self.enc_o), _, _ = self.run(
            kernel, "enc_self_fwd", (ENC_SELF,), [self.source],
            [self.f32(d), self.bf16(3 * d), self.shares, self.bf16(d)], after=after,
        )

    def dec_self_fwd(self, after=()):
        d = self.width

        def kernel(meta, step, small, uses, ins, outs, scratch):
            self_fwd(uses[0], small, *ins, *outs, meta[2 + self.count + step], True, DEC_BIAS)

        (self.h3, self.dec_qkv, self.dec_a, self.dec_o), _, _ = self.run(
            kernel, "dec_self_fwd", (DEC_SELF,), [self.target],
            [self.f32(d), self.bf16(3 * d), self.shares, self.bf16(d)], after=after,
        )

    def enc_ffn_fwd(self, after=()):
        def kernel(meta, step, small, uses, ins, outs, scratch):
            ffn_fwd(uses[0], small, *ins, *outs)

        (self.h2, self.hid, self.slope), _, _ = self.run(
            kernel, "enc_ffn_fwd", (ENC_FFN,), [self.h1, self.source],
            [self.f32(self.width), self.bf16(self.hidden), self.bf16(self.hidden)], after=after,
        )

    def dec_middle(self, after=()):
        d = self.width

        def kernel(meta, step, small, uses, ins, outs, scratch):
            cross_fwd(uses[0], small, *ins[:2], *outs[:5], meta[2 + step])
            ffn_both(uses[1], small, outs[0], *ins[2:], *outs[5:], *scratch, meta[2 + self.count + step])

        rows, sums, grads = self.run(
            kernel, "dec_middle", (CROSS, DEC_FFN), [self.h3, self.h2, self.target, self.cotangent],
            [self.f32(d), self.bf16(d), self.bf16(2 * d), self.shares, self.bf16(d), self.bf16(d), self.f32(d),
             self.f32(d)],
            (DEC_FFN,), self.rows_of(self.hidden, self.hidden), after,
        )
        self.h4, self.q, self.kv, self.cross_a, self.cross_o, self.decoded, self.dd2, self.dh5 = rows
        self.sums_df = sums[0]
        return grads[0]

    def dec_bwd(self, after=()):
        d = self.width

        def kernel(meta, step, small, uses, ins, outs, scratch):
            dd2, h4, h3, h2, q, kv, cross_a, cross_o, target, dh5, qkv, a, o = ins
            go, gq, gkv, g = scratch
            dd1 = cross_bwd(uses[0], small, dd2[0], h4, h3, h2, q, kv, cross_a, cross_o, outs[0], go, gq, gkv)
            self_bwd(uses[1], small, dd1, h3, target, dh5, qkv, a, o, outs[1], go, g, DEC_GAIN)

        rows, (self.sums_c, self.sums_ds), grads = self.run(
            kernel, "dec_bwd", (CROSS, DEC_SELF),
            [self.dd2, self.h4, self.h3, self.h2, self.q, self.kv, self.cross_a, self.cross_o, self.target, self.dh5,
             self.dec_qkv, self.dec_a, self.dec_o],
            [self.f32(d), self.bf16(d)], (CROSS, DEC_SELF), self.rows_of(d, d, 2 * d, 3 * d), after,
        )
        self.dm, self.target_grad = rows
        return grads

    def enc_ffn_bwd(self, after=()):
        d = self.width

        def kernel(meta, step, small, uses, ins, outs, scratch):
            ffn_bwd(uses[0], small, *ins, *outs)

        (self.de1, self.dh2), (self.sums_ef,), grads = self.run(
            kernel, "enc_ffn_bwd", (ENC_FFN,), [self.dm, self.h2, self.h1, self.hid, self.slope],
            [self.f32(d), self.f32(d)], (ENC_FFN,), (), after,
        )
        return grads[0]

    def enc_self_bwd(self, after=()):
        d = self.width

        def kernel(meta, step, small, uses, ins, outs, scratch):
            self_bwd(uses[0], small, ins[0][0], *ins[1:], *outs, *scratch, ENC_GAIN)

        (self.source_grad,), (self.sums_es,), grads = self.run(
            kernel, "enc_self_bwd", (ENC_SELF,),
            [self.de1, self.h1, self.source, self.dh2, self.enc_qkv, self.enc_a, self.enc_o], [self.bf16(d)],
            (ENC_SELF,), self.rows_of(d, 3 * d), after,
        )
        return grads[0]

    def small_sums(self):
        es, ef, ds, c, df = self.sums_es, self.sums_ef, self.sums_ds, self.sums_c, self.sums_df
        return jnp.concatenate(
            [es[0:3], ef[0:1], es[3:4], ef[1:2], es[4:5], ef[2:3], ds[0:3], c[0:3], df[0:1], ds[3:4], c[3:4], df[1:2],
             ds[4:5], c[4:5], df[2:3], jnp.zeros((3, self.width), F32), ef[4:8], df[4:8]], axis=0,
        )


def simple(kernel, name, meta, inputs, outs, scratch=(), after=(), limit=SIMPLE_LIMIT):
    specs = [pl.BlockSpec(memory_space=pltpu.VMEM)] * len(inputs)
    specs += [pl.BlockSpec(memory_space=pl.ANY)] * len(after)

    def body(meta, *refs):
        return kernel(meta, *refs[: len(inputs)], *refs[len(inputs) + len(after) :])

    return pl.pallas_call(
        body,
        in_specs=[pl.BlockSpec(memory_space=pltpu.SMEM)] + specs,
        out_specs=[pl.BlockSpec(memory_space=pltpu.VMEM)] * len(outs),
        out_shape=list(outs),
        scratch_shapes=list(scratch),
        compiler_params=pltpu.CompilerParams(vmem_limit_bytes=limit),
        cost_estimate=pl.CostEstimate(flops=COST, bytes_accessed=COST, transcendentals=0),
        name=name,
    )(meta, *inputs, *after)


def pack_kernel(plan, nz, meta, *refs):
    n_in = sum(len(p) for p in plan)
    shards = refs[:n_in]
    small_refs = refs[n_in : n_in + len(SMALLS) + len(LINES)]
    outs = refs[n_in + len(small_refs) : -1]
    rows = refs[-1]
    at = 0
    for out, chunk in zip(outs, plan):
        for row in chunk:
            shard = shards[at]
            rd, cols = shard.shape
            for cb in range(cols // TILE):
                out[row + cb * rd : row + (cb + 1) * rd, :] = shard[:, cb * TILE : (cb + 1) * TILE]
            at += 1
    rank = meta[0] * nz + meta[1]
    rows[...] = jnp.zeros_like(rows)
    for ref, (_, row, _) in zip(small_refs, SMALLS + LINES):
        lines, part = ref.shape
        lane = lax.broadcasted_iota(jnp.int32, (part, TILE), 1)
        spread = (lane % part == lax.broadcasted_iota(jnp.int32, (part, TILE), 0)).astype(BF16)
        tiled = nn(ref[...], spread)
        across = lax.broadcasted_iota(jnp.int32, (lines, TILE), 1)
        if row >= ENC_FFN_BIAS:
            per = TILE // part
            tiled = jnp.broadcast_to(tiled, (4, TILE))
            across = lax.broadcasted_iota(jnp.int32, (4, TILE), 1)
            down = lax.broadcasted_iota(jnp.int32, (4, TILE), 0)
            ok = (across // part == rank % per) & (down == rank // per)
            rows[row : row + 4, :] = jnp.where(ok, tiled, 0.0)
        else:
            rows[row : row + lines, :] = jnp.where(across // part == rank, tiled, 0.0)
    outs[0][outs[0].shape[0] - SMALL_ROWS :, :] = rows[...].astype(BF16)


def along_z_kernel(nz, rows, tail, meta, *refs):
    parts = refs[:nz]
    out = refs[nz]
    z = meta[1]
    for s in range(nz):
        at = pl.multiple_of(((z + nz - s) % nz) * rows, 16)
        out[pl.ds(at, rows), :] = parts[s][:rows, :]
    if tail:
        total = parts[0][rows:, :].astype(F32)
        for s in range(1, nz):
            total = total + parts[s][rows:, :].astype(F32)
        out[nz * rows :, :] = total.astype(BF16)


def add_cores_kernel(counts, tail, halves, meta, *refs):
    n = len(counts)
    outs = refs[2 * n + 2 * bool(tail) :]
    chips, nz = refs[0].shape[:2]
    total = sum(counts)
    for k in range(chips):
        out = outs[k % 2].at[k // 2] if halves else outs[k]
        for z in range(nz):
            at = z * total
            for g, rows in enumerate(counts):
                out[at : at + rows, :] = (
                    refs[2 * g][k, z].astype(F32) + refs[2 * g + 1][k, z].astype(F32)
                ).astype(BF16)
                at += rows
        if tail:
            out[nz * total :, :] = (refs[2 * n][...].astype(F32) + refs[2 * n + 1][...].astype(F32)).astype(BF16)


def add_half_kernel(meta, kept, got, own, second):
    own[...] = (kept[0].astype(F32) + got[0].astype(F32)).astype(BF16)
    second[...] = (kept[1].astype(F32) + got[1].astype(F32)).astype(BF16)


def add_two_kernel(meta, one, two, out):
    out[...] = (one[...].astype(F32) + two[...].astype(F32)).astype(BF16)


def add_chips_kernel(nz, rows, tail, n_parts, meta, *refs):
    parts, outs = refs[:n_parts], refs[n_parts:]
    z = meta[1]
    for s in range(nz):
        at = pl.multiple_of(((z + s) % nz) * rows, 16)
        total = parts[0][pl.ds(at, rows), :].astype(F32)
        for part in parts[1:]:
            total = total + part[pl.ds(at, rows), :].astype(F32)
        outs[s][:rows, :] = total.astype(outs[s].dtype)
    if tail:
        total = parts[0][nz * rows :, :].astype(F32)
        for part in parts[1:]:
            total = total + part[nz * rows :, :].astype(F32)
        for s in range(nz):
            outs[s][rows:, :] = total.astype(outs[s].dtype)


def add_z_kernel(nz, places, rows, tail, meta, *refs):
    parts, outs = refs[:nz], refs[nz:]
    for (row, rd, cols), out in zip(places, outs):
        for cb in range(cols // TILE):
            at = row + cb * rd
            total = parts[0][at : at + rd, :].astype(F32)
            for part in parts[1:]:
                total = total + part[at : at + rd, :].astype(F32)
            out[:, cb * TILE : (cb + 1) * TILE] = total
    if tail:
        rank = meta[0] * nz + meta[1]
        total = parts[0][rows:, :]
        for part in parts[1:]:
            total = total + part[rows:, :].astype(F32)
        for out, (_, row, _) in zip(outs[len(places) :], SMALLS + LINES):
            lines, part = out.shape
            if row >= ENC_FFN_BIAS:
                per = TILE // part
                down = lax.broadcasted_iota(jnp.int32, (8, TILE), 0)
                base = total[24:32, :]
                picked = jnp.sum(
                    jnp.where(down == rank // per + (row - 24), base, 0.0), axis=0, keepdims=True
                )
                moved = pltpu.roll(jnp.broadcast_to(picked, (8, TILE)), TILE - (rank % per) * part, 1)
                out[...] = moved[0:1, :part]
            else:
                first = row // 8 * 8
                moved = pltpu.roll(total[first : first + 24 if first < 8 else 24, :], TILE - rank * part, 1)
                out[...] = moved[row - first : row - first + lines, :part]


def swap(v, size, mask):
    return lax.ppermute(v, DP, [(i, i ^ mask) for i in range(size)])


def shift(v, size, by):
    return lax.ppermute(v, FSDP, [(i, (i + by) % size) for i in range(size)])


def across(v, size, own, other):
    return lax.ppermute(v, DP, [(i, i ^ (other if i % 2 else own)) for i in range(size)])


def hold(values, *first):
    return lax.optimization_barrier((values, first))[0]


class Exchange:
    def __init__(self, layouts, meta, nd, nz):
        self.layouts, self.meta, self.nd, self.nz = layouts, meta, nd, nz

    def pack(self, shards):
        plan, sizes, inputs = [], [], []
        for groups in GATHERS:
            rows, first = [], 0
            for g in groups:
                self.layouts[g].first = first
                for n, at in zip(self.layouts[g].names, self.layouts[g].offsets):
                    rows.append(first + at)
                    inputs.append(shards[n])
                first += self.layouts[g].rows
            for g in groups:
                self.layouts[g].span = first
            plan.append(rows)
            sizes.append(first)
        inputs += [shards[n] for n, _, _ in SMALLS] + [shards[n].reshape(1, -1) for n, _, _ in LINES]
        self.sizes = sizes
        self.tails = [SMALL_ROWS] + [0] * (len(GATHERS) - 1)
        return simple(
            functools.partial(pack_kernel, plan, self.nz), "pack", self.meta, inputs,
            [jax.ShapeDtypeStruct((r + t, TILE), BF16) for r, t in zip(sizes, self.tails)],
            [pltpu.VMEM((SMALL_ROWS, TILE), F32)], limit=VMEM_LIMIT,
        )

    def gather_z(self, pack):
        return [pack] + [shift(pack, self.nz, s) for s in range(1, self.nz)]

    def join_z(self, c, parts):
        rows, tail = self.sizes[c], self.tails[c]
        return simple(
            functools.partial(along_z_kernel, self.nz, rows, tail), "join", self.meta, parts,
            [jax.ShapeDtypeStruct((self.nz * rows + tail, TILE), BF16)],
        )[0]

    def gather_chips(self, joined, *before):
        first = across(joined, self.nd, 4, 2)
        second = across(joined, self.nd, 2, 4)
        if before:
            first = hold(first, *before)
        return [joined, first, second, across(first, self.nd, 2, 4)]

    def gather_cores(self, pieces):
        return [v for piece in pieces for v in (piece, swap(piece, self.nd, 1))]

    def to_cores(self, grads):
        return [grads[0], swap(grads[1], self.nd, 1)]

    def add_cores(self, groups, parts, tail=None, halves=False):
        counts = [self.layouts[g].rows for g in groups]
        extra = 0 if tail is None else SMALL_ROWS
        if extra:
            parts = parts + [tail, swap(tail, self.nd, 1)]
        return simple(
            functools.partial(add_cores_kernel, counts, extra, halves), "add_cores", self.meta, parts,
            [jax.ShapeDtypeStruct(((2,) if halves else ()) + (self.nz * sum(counts) + extra, TILE), BF16)]
            * (2 if halves else self.nd // 2),
        )

    def add_half(self, kept, got):
        shape = jax.ShapeDtypeStruct(kept.shape[1:], BF16)
        return simple(add_half_kernel, "add_half", self.meta, [kept, got], [shape, shape])

    def to_first(self, v):
        return across(v, self.nd, 4, 2)

    def to_second(self, v):
        return across(v, self.nd, 2, 4)

    def to_chips(self, sums):
        return [sums[0], self.to_first(sums[1]), self.to_second(sums[2]), swap(sums[3], self.nd, 6)]

    def add_chips(self, groups, parts, extra=0):
        rows = sum(self.layouts[g].rows for g in groups)
        return simple(
            functools.partial(add_chips_kernel, self.nz, rows, extra, len(parts)), "add_chips", self.meta, parts,
            [jax.ShapeDtypeStruct((rows + extra, TILE), F32 if s == 0 else BF16) for s in range(self.nz)],
        )

    def add_chips_flat(self, parts):
        shape = jax.ShapeDtypeStruct(parts[0].shape, BF16)
        return simple(add_two_kernel, "add_two", self.meta, parts, [shape])[0]

    def to_z(self, sums):
        return [sums[0]] + [shift(sums[s], self.nz, s) for s in range(1, self.nz)]

    def add_z(self, groups, parts, extra=0):
        ranks, first, places = self.nd * self.nz, 0, []
        for g in groups:
            layout = self.layouts[g]
            places += [(first + at, r // ranks, c) for at, (r, c) in zip(layout.offsets, layout.shapes)]
            first += layout.rows
        outs = [jax.ShapeDtypeStruct((rd, c), F32) for _, rd, c in places]
        if extra:
            wide = TILE // ranks
            outs += [jax.ShapeDtypeStruct((lines, wide), F32) for _, _, lines in SMALLS]
            outs += [jax.ShapeDtypeStruct((1, 4 * wide), F32)] * 2
        return simple(
            functools.partial(add_z_kernel, len(parts), places, first, extra), "add_z", self.meta, parts, outs
        )


def by_pieces(layouts, source, target, cotangent, place, meta, shards, nd, nz):
    ex = Exchange(layouts, place, nd, nz)
    packs = ex.pack(shards)
    st = Step(layouts, source, target, cotangent, hold(meta, packs))
    along0 = ex.gather_z(packs[0])
    joined0 = ex.join_z(0, along0)
    along1 = ex.gather_z(hold(packs[1], joined0))
    pieces = ex.gather_cores(hold(ex.gather_chips(joined0), along1))
    st.w[ENC_SELF] = pieces
    st.small = sum(p[p.shape[0] - SMALL_ROWS :].astype(F32) for p in pieces)
    joined1 = ex.join_z(1, along1)
    along2 = ex.gather_z(hold(packs[2], joined1))
    st.enc_self_fwd(after=[joined1])
    along2 = hold(along2, st.h1)
    chips1 = ex.gather_chips(joined1, along2)
    joined2 = ex.join_z(2, hold(along2, chips1[1]))
    st.w[ENC_FFN] = st.w[DEC_SELF] = ex.gather_cores(hold(chips1, joined2))
    st.dec_self_fwd(after=[joined2])
    chips2 = ex.gather_chips(joined2, st.h3)
    early2 = ex.gather_cores(hold(chips2[:3], st.h3))
    st.enc_ffn_fwd(after=[chips2[1], chips2[2]])
    st.w[CROSS] = st.w[DEC_FFN] = hold(early2, st.h2) + ex.gather_cores(hold(chips2[3:], st.h2))
    result = [None] * len(shards)

    def put(groups, outs):
        names = [n for g in groups for n in GROUPS[g]]
        names += [n for n, _, _ in SMALLS + LINES]
        for n, v in zip(names, outs):
            result[n] = v.reshape(shards[n].shape)

    df = st.dec_middle()[0]
    df = lax.psum_scatter(df.reshape(nd, nz, *df.shape[1:]), DP, scatter_dimension=0, tiled=True)
    both = (CROSS, DEC_SELF)
    cr, ds = st.dec_bwd()
    cr_kept, cr = ex.add_cores(both, ex.to_cores(cr) + ex.to_cores(ds), halves=True)
    cr = ex.to_first(cr)
    ef = st.enc_ffn_bwd(after=[cr_kept])
    cr, df = hold((cr, df), st.de1)
    ef = ex.to_cores(hold(ef, cr))
    cr_own, cr = ex.add_half(cr_kept, cr)
    cr = ex.to_second(cr)
    ef_kept, ef = ex.add_cores((ENC_FFN,), hold(ef, cr_own), halves=True)
    cr = ex.add_chips_flat([cr_own, hold(cr, ef_kept)])
    ef = ex.to_first(ef)
    late = jnp.concatenate([df[0], cr.reshape(nz, -1, TILE)], axis=1)
    late = lax.psum_scatter(late, FSDP, scatter_dimension=0, tiled=True)[0]
    es = st.enc_self_bwd(after=[cr, ef_kept])
    ef = hold(ef, st.source_grad)
    es = ex.to_cores(hold(es, ef))
    tail = st.small_sums().astype(BF16)
    ef_own, ef = ex.add_half(ef_kept, ef)
    ef = ex.to_second(ef)
    es = ex.to_chips(ex.add_cores((ENC_SELF,), hold(es, ef_own), tail))
    ef = ex.to_z(ex.add_chips((ENC_FFN,), hold([ef_own, ef], es[0])))
    es = ex.to_z(ex.add_chips((ENC_SELF,), hold(es, ef[0]), SMALL_ROWS))
    put((ENC_FFN,), ex.add_z((ENC_FFN,), hold(ef, es[0])))
    late = hold(late, result[A_ENC_IN])
    put((DEC_FFN,) + both, ex.add_z((DEC_FFN,) + both, [late]))
    es = hold(es, result[A_DEC_IN])
    put((ENC_SELF,), ex.add_z((ENC_SELF,), es, SMALL_ROWS))
    return (st.decoded, st.source_grad, st.target_grad) + tuple(result)


def whole(layouts, source, target, cotangent, meta, shards):
    small_names = [n for n, _, _ in SMALLS]
    full = [
        lax.all_gather(v, AXES, axis=1 if n in small_names else 0, tiled=True) for n, v in enumerate(shards)
    ]
    width = source.shape[2]
    st = Step(layouts, source, target, cotangent, meta)
    st.small = jnp.concatenate(
        [full[n] for n in small_names]
        + [jnp.zeros((3, width), BF16)]
        + [full[n].reshape(-1, width) for n, _, _ in LINES],
        axis=0,
    ).astype(F32)
    st.w = {g: [full[n] for n in names] for g, names in enumerate(GROUPS)}
    st.enc_self_fwd()
    st.enc_ffn_fwd()
    st.dec_self_fwd()
    grads = [None] * len(GROUPS)
    grads[DEC_FFN] = st.dec_middle()
    grads[CROSS], grads[DEC_SELF] = st.dec_bwd()
    grads[ENC_FFN] = st.enc_ffn_bwd()
    grads[ENC_SELF] = st.enc_self_bwd()
    sums = st.small_sums()
    result = [None] * len(shards)
    for g, names in enumerate(GROUPS):
        for n, v in zip(names, grads[g]):
            result[n] = v.astype(F32)
    for n, row, lines in SMALLS:
        result[n] = sums[row : row + lines]
    for n, row, _ in LINES:
        result[n] = sums[row : row + 4].reshape(-1)
    result = [
        lax.psum_scatter(v, AXES, scatter_dimension=1 if n in small_names else 0, tiled=True)
        for n, v in enumerate(result)
    ]
    return (st.decoded, st.source_grad, st.target_grad) + tuple(result)


def local(nd, nz, source, target, cotangent, pair_order, source_lengths, target_lengths, *shards):
    ranks = nd * nz
    matrices = [n for names in GROUPS for n in names]
    shapes = {n: (shards[n].shape[0] * ranks, shards[n].shape[1]) for n in matrices}
    pieces = nd == 8 and all(shards[n].shape[0] % 16 == 0 for n in matrices)
    modes = (PIECES, PIECES, PIECES, PIECES, RANKS) if pieces else (WHOLE,) * len(GROUPS)
    layouts = [Layout(g, shapes, modes[g], nd, nz) for g in range(len(GROUPS))]
    place = jnp.stack([lax.axis_index(DP), lax.axis_index(FSDP)]).astype(jnp.int32)
    meta = jnp.concatenate([place, lookup(pair_order, source_lengths), lookup(pair_order, target_lengths)])
    if pieces:
        return by_pieces(layouts, source, target, cotangent, place, meta, shards, nd, nz)
    return whole(layouts, source, target, cotangent, meta, shards)


def specs():
    split, rows, cols = P(AXES, None, None), P(AXES, None), P(None, AXES)
    line = P(AXES)
    weights = (
        rows, rows, rows, rows, cols, line, cols, cols,
        rows, rows, rows, rows, rows, rows, rows, cols, line, cols, cols,
    )
    return (split, split, split, line, P(), P()) + weights, (split, split, split) + weights


def solution(mesh):
    in_specs, out_specs = specs()
    return jax.shard_map(
        functools.partial(local, mesh.shape[DP], mesh.shape[FSDP]),
        mesh=mesh, in_specs=in_specs, out_specs=out_specs, check_vma=False,
    )
```

```python
import functools

import jax
import jax.numpy as jnp
from jax import lax
from jax.experimental import pallas as pl
from jax.experimental.pallas import tpu as pltpu
from jax.sharding import PartitionSpec as P

F32 = jnp.float32
BF16 = jnp.bfloat16
DP, FSDP = "dp", "fsdp"
AXES = (DP, FSDP)
HEAD_DIM = 64
PAIR = 2 * HEAD_DIM
TILE = 512
epsilon = 1e-05
FORWARD_TILE = 256
COST = 1
SIMPLE_LIMIT = 16 * 1024 * 1024
VMEM_LIMIT = 56 * 1024 * 1024

ENC_BIAS, ENC_GAIN, ENC_SHIFT = 0, 4, 6
DEC_BIAS, DEC_GAIN, DEC_SHIFT = 8, 15, 18
ENC_FFN_BIAS, DEC_FFN_BIAS = 24, 28
SMALL_ROWS = 32

(A_ENC_QKV, A_ENC_OUT, A_ENC_IN, A_ENC_BACK, A_ENC_BIAS, A_ENC_FBIAS, A_ENC_GAIN, A_ENC_SHIFT, A_DEC_QKV, A_DEC_OUT,
 A_CROSS_Q, A_CROSS_KV, A_CROSS_OUT, A_DEC_IN, A_DEC_BACK, A_DEC_BIAS, A_DEC_FBIAS, A_DEC_GAIN, A_DEC_SHIFT) = range(19)
ENC_SELF, ENC_FFN, DEC_SELF, CROSS, DEC_FFN = range(5)
GROUPS = (
    (A_ENC_QKV, A_ENC_OUT),
    (A_ENC_IN, A_ENC_BACK),
    (A_DEC_QKV, A_DEC_OUT),
    (A_CROSS_Q, A_CROSS_KV, A_CROSS_OUT),
    (A_DEC_IN, A_DEC_BACK),
)
SMALLS = (
    (A_ENC_BIAS, ENC_BIAS, 4), (A_ENC_GAIN, ENC_GAIN, 2), (A_ENC_SHIFT, ENC_SHIFT, 2),
    (A_DEC_BIAS, DEC_BIAS, 7), (A_DEC_GAIN, DEC_GAIN, 3), (A_DEC_SHIFT, DEC_SHIFT, 3),
)
LINES = ((A_ENC_FBIAS, ENC_FFN_BIAS, 1), (A_DEC_FBIAS, DEC_FFN_BIAS, 1))
WHOLE, PIECES, RANKS = range(3)
GATHERS = ((ENC_SELF,), (ENC_FFN, DEC_SELF), (CROSS, DEC_FFN))


def nn(a, b):
    return lax.dot_general(a, b, (((1,), (0,)), ((), ())), preferred_element_type=F32)


def nt(a, b):
    return lax.dot_general(a, b, (((1,), (1,)), ((), ())), preferred_element_type=F32)


def tn(a, b):
    return lax.dot_general(a, b, (((0,), (0,)), ((), ())), preferred_element_type=F32)


def tokens_sum(v):
    return jnp.sum(v, axis=0, keepdims=True)


def normalize(h):
    c = h - jnp.mean(h, axis=-1, keepdims=True)
    r = lax.rsqrt(jnp.mean(c * c, axis=-1, keepdims=True) + epsilon)
    return c * r, r


def norm_back(dv, xh, r, g):
    hh = dv * g
    return r * (
        hh - jnp.mean(hh, axis=-1, keepdims=True) - xh * jnp.mean(hh * xh, axis=-1, keepdims=True)
    )


def gelu_parts(u):
    c = 0.7978845608028654
    sq = u * u
    half = 0.5 + 0.5 * jnp.tanh(u * (c + (c * 0.044715) * sq))
    gelu = u * half
    return gelu, half + gelu * (1.0 - half) * (2.0 * c + (6.0 * c * 0.044715) * sq)


class Layout:
    def __init__(self, group, shapes, mode, nd, nz):
        self.names = GROUPS[group]
        self.mode = mode
        self.shapes = [shapes[n] for n in self.names]
        self.span = 0
        self.nd, self.nz = nd, nz
        self.offsets, row = [], 0
        for rows, cols in self.shapes:
            self.offsets.append(row)
            row += (rows // (nd * nz)) * (cols // TILE)
        self.rows = row
        self.first = 0

    def n_sources(self):
        return len(self.names) if self.mode == WHOLE else self.nd

    def w_scratch(self):
        return [pltpu.VMEM(s, BF16) for s in self.shapes] + [
            pltpu.SemaphoreType.DMA((len(self.shapes),))
        ]

    def acc_scratch(self):
        return (
            [pltpu.VMEM(s, F32) for s in self.shapes]
            + [pltpu.VMEM(s, BF16) for s in self.shapes]
            + [pltpu.SemaphoreType.DMA((len(self.shapes),))]
        )

    def start_loads(self, sources, weights, sems, dp, order):
        for j in order:
            rows, cols = self.shapes[j]
            if self.mode == WHOLE:
                pltpu.make_async_copy(sources[j], weights[j], sems.at[j]).start()
                continue
            rd = rows // (self.nd * self.nz)
            view = weights[j].reshape(self.nd, self.nz, rd, cols)
            for m in range(self.nd):
                mask = self.masks(dp)[m]
                for cb in range(cols // TILE):
                    pltpu.make_async_copy(
                        sources[m]
                        .at[pl.ds(0, self.nz * self.span), :]
                        .reshape(self.nz, self.span, TILE)
                        .at[:, pl.ds(self.first + self.offsets[j] + cb * rd, rd), :],
                        view.at[dp ^ mask, :, :, pl.ds(cb * TILE, TILE)],
                        sems.at[j],
                    ).start()

    def masks(self, dp):
        first = jnp.where(dp % 2 == 0, 4, 2)
        return [0, 1, first, 7 - first, 6 - first, first + 1, 6, 7]

    def wait_load(self, weights, sems, j):
        pltpu.make_async_copy(weights[j], weights[j], sems.at[j]).wait()

    def grad_shapes(self):
        if self.mode == WHOLE:
            return [jax.ShapeDtypeStruct(s, BF16) for s in self.shapes]
        if self.mode == RANKS:
            return [jax.ShapeDtypeStruct((self.nd * self.nz, self.rows, TILE), BF16)]
        return [jax.ShapeDtypeStruct((self.nd // 2, self.nz, self.rows, TILE), BF16)] * 2

    def start_store(self, acc, stage, outs, sems, dp, j):
        rows, cols = self.shapes[j]
        stage[j][...] = acc[j][...].astype(BF16)
        if self.mode == WHOLE:
            pltpu.make_async_copy(stage[j], outs[j], sems.at[j]).start()
            return
        rd = rows // (self.nd * self.nz)
        if self.mode == RANKS:
            view = stage[j].reshape(self.nd * self.nz, rd, cols)
            for cb in range(cols // TILE):
                pltpu.make_async_copy(
                    view.at[:, :, pl.ds(cb * TILE, TILE)],
                    outs[0].at[:, pl.ds(self.offsets[j] + cb * rd, rd), :],
                    sems.at[j],
                ).start()
            return
        view = stage[j].reshape(self.nd, self.nz, rd, cols)
        for m, mask in enumerate(self.masks(dp)):
            for cb in range(cols // TILE):
                pltpu.make_async_copy(
                    view.at[dp ^ mask, :, :, pl.ds(cb * TILE, TILE)],
                    outs[m % 2].at[m // 2, :, pl.ds(self.offsets[j] + cb * rd, rd), :],
                    sems.at[j],
                ).start()

    def wait_store(self, stage, sems, j):
        pltpu.make_async_copy(stage[j], stage[j], sems.at[j]).wait()


class Use:
    def __init__(self, layout, dp, sources, weights, wsem):
        self.layout, self.dp = layout, dp
        self.sources, self.w, self.wsem = sources, weights, wsem
        self.acc = ()

    def add_sums(self, sg, grads, acc, stage, gsem):
        self.sg, self.grads, self.acc, self.stage, self.gsem = sg, grads, acc, stage, gsem

    def begin(self, order):
        self.layout.start_loads(self.sources, self.w, self.wsem, self.dp, order)

    def clear(self):
        if self.acc:
            for ref in self.acc:
                ref[...] = jnp.zeros_like(ref)
            self.sg[...] = jnp.zeros_like(self.sg)

    def ready(self, *which):
        @pl.when(self.step == 0)
        def _():
            for j in which:
                self.layout.wait_load(self.w, self.wsem, j)

    def sums(self, row, v, at=0):
        self.sg[row : row + 1, at : at + v.shape[1]] += tokens_sum(v)

    def send(self, *which):
        @pl.when(self.last)
        def _():
            for j in which:
                self.layout.start_store(self.acc, self.stage, self.grads, self.gsem, self.dp, j)

    def end(self):
        if self.acc:
            for j in range(len(self.layout.names)):
                self.layout.wait_store(self.stage, self.gsem, j)


def low_lanes(rows):
    return lax.broadcasted_iota(jnp.int32, (rows, PAIR), 1) < HEAD_DIM


def split_pair(v):
    low = low_lanes(v.shape[0])
    zero = jnp.zeros_like(v)
    return jnp.concatenate([jnp.where(low, v, zero), jnp.where(low, zero, v)], axis=0)


def allowed_keys(length, causal, size):
    col = lax.broadcasted_iota(jnp.int32, (size, size), 1)
    ok = col < length
    if causal:
        ok = ok & (col <= lax.broadcasted_iota(jnp.int32, (size, size), 0))
    return ok


def pair_forward(q, k, v, ok):
    size = q.shape[0]
    s = nt(split_pair(q), k)
    s = jnp.where(jnp.concatenate([ok, ok], axis=0), s, -1e30)
    e = jnp.exp(s - jnp.max(s, axis=-1, keepdims=True))
    a = (e * (1.0 / jnp.sum(e, axis=-1, keepdims=True))).astype(BF16)
    mixed = nn(jnp.concatenate([a[:size], a[size:]], axis=1), split_pair(v))
    return a, mixed


def pair_backward(q, k, v, a, g):
    size = q.shape[0]
    g2 = split_pair(g)
    af = a.astype(F32)
    da = nt(g2, v)
    ds = (af * (da - jnp.sum(af * da, axis=-1, keepdims=True))).astype(BF16)
    dv = tn(g2, a).T
    dk = tn(split_pair(q), ds).T
    dq = nn(jnp.concatenate([ds[:size], ds[size:]], axis=1), split_pair(k))
    return dq * (HEAD_DIM**-0.5), dk, dv


def row(small, at):
    return small[at : at + 1]


def attention_fwd(q, k, v, ok, a_ref, o_ref):
    for p in range(a_ref.shape[1]):
        at = p * PAIR
        a, mixed = pair_forward(q(at), k(at), v(at), ok)
        a_ref[0, p] = a
        o_ref[0, :, at : at + PAIR] = mixed.astype(BF16)


def self_fwd(use, small, x_ref, h_ref, qkv_ref, a_ref, o_ref, length, causal, bias):
    size, width = x_ref.shape[1:]
    w = use.w
    ok = allowed_keys(length, causal, size)
    use.ready(0)
    x = x_ref[0]
    q = (nn(x, w[0][:, :width]) + row(small, bias)) * (HEAD_DIM**-0.5)
    qkv_ref[0, :, :width] = q.astype(BF16)
    qkv_ref[0, :, width : 2 * width] = nn(x, w[0][:, width : 2 * width]).astype(BF16)
    qkv_ref[0, :, 2 * width :] = (nn(x, w[0][:, 2 * width :]) + row(small, bias + 1)).astype(BF16)

    def part(k):
        return lambda at: qkv_ref[0, :, k * width + at : k * width + at + PAIR]

    attention_fwd(part(0), part(1), part(2), ok, a_ref, o_ref)
    use.ready(1)
    h_ref[0] = x.astype(F32) + nn(o_ref[0], w[1][...]) + row(small, bias + 2)


def decoder_first(small, h3_ref):
    return normalize(h3_ref[0])[0] * row(small, DEC_GAIN) + row(small, DEC_SHIFT)


def memory_rows(small, h2_ref):
    return (normalize(h2_ref[0])[0] * row(small, ENC_GAIN + 1) + row(small, ENC_SHIFT + 1)).astype(BF16)


def cross_fwd(use, small, h3_ref, h2_ref, h_ref, q_ref, kv_ref, a_ref, o_ref, length):
    size, width = h3_ref.shape[1:]
    w = use.w
    ok = allowed_keys(length, False, size)
    first = decoder_first(small, h3_ref)
    memory = memory_rows(small, h2_ref)
    use.ready(0)
    q = (nn(first.astype(BF16), w[0][...]) + row(small, DEC_BIAS + 3)) * (HEAD_DIM**-0.5)
    q_ref[0] = q.astype(BF16)
    use.ready(1)
    kv_ref[0, :, :width] = nn(memory, w[1][:, :width]).astype(BF16)
    kv_ref[0, :, width:] = (nn(memory, w[1][:, width:]) + row(small, DEC_BIAS + 4)).astype(BF16)
    attention_fwd(
        lambda at: q_ref[0, :, at : at + PAIR],
        lambda at: kv_ref[0, :, at : at + PAIR],
        lambda at: kv_ref[0, :, width + at : width + at + PAIR],
        ok, a_ref, o_ref,
    )
    use.ready(2)
    h_ref[0] = first + nn(o_ref[0], w[2][...]) + row(small, DEC_BIAS + 5)


def ffn_steps(use, small, low, total, ffn_bias, hid_put, slope_put):
    w = use.w
    hidden = w[0].shape[1]
    use.ready(0, 1)
    for at in range(0, hidden, FORWARD_TILE):
        cols = slice(at, at + FORWARD_TILE)
        lane = at % TILE
        bias = small[ffn_bias + at // TILE : ffn_bias + at // TILE + 1, lane : lane + FORWARD_TILE]
        hid, slope = gelu_parts(nn(low, w[0][:, cols]) + bias)
        hid = hid.astype(BF16)
        hid_put(cols, hid)
        slope_put(cols, slope.astype(BF16))
        total = total + nn(hid, w[1][cols, :])
    return total


def ffn_fwd(use, small, h1_ref, x_ref, h_ref, hid_ref, slope_ref):
    first = normalize(h1_ref[0])[0] * row(small, ENC_GAIN) + row(small, ENC_SHIFT)
    total = first + row(small, ENC_BIAS + 3) + x_ref[0].astype(F32)

    def hid_put(cols, v):
        hid_ref[0, :, cols] = v

    def slope_put(cols, v):
        slope_ref[0, :, cols] = v

    h_ref[0] = ffn_steps(use, small, first.astype(BF16), total, ENC_FFN_BIAS, hid_put, slope_put)


def ffn_back(use, low, hid, slope, g, wait=True):
    w, acc = use.w, use.acc
    acc[1][...] += nn(hid.T, g)
    use.send(1)
    if wait:
        use.ready(1)
    du = nt(g, w[1][...]) * slope.astype(F32)
    for t in range(du.shape[1] // TILE):
        use.sums(4 + t, du[:, t * TILE : (t + 1) * TILE])
    gu = du.astype(BF16)
    acc[0][...] += nn(low.T, gu)
    use.send(0)
    if wait:
        use.ready(0)
    return nt(gu, w[0][...])


def ffn_both(use, small, h4_ref, x_ref, cot_ref, out_ref, dd2_ref, dh5_ref, hid_s, slope_s, length):
    size, width = x_ref.shape[1:]
    second = normalize(h4_ref[0])[0] * row(small, DEC_GAIN + 1) + row(small, DEC_SHIFT + 1)
    low = second.astype(BF16)
    total = second + row(small, DEC_BIAS + 6) + x_ref[0].astype(F32)

    def hid_put(cols, v):
        hid_s[:, cols] = v

    def slope_put(cols, v):
        slope_s[:, cols] = v

    total = ffn_steps(use, small, low, total, DEC_FFN_BIAS, hid_put, slope_put)
    xh, r = normalize(total)
    gain = row(small, DEC_GAIN + 2)
    valid = lax.broadcasted_iota(jnp.int32, (size, width), 0) < length
    out_ref[0] = jnp.where(valid, xh * gain + row(small, DEC_SHIFT + 2), 0.0).astype(BF16)
    dv = jnp.where(valid, cot_ref[0].astype(F32), 0.0)
    dh = norm_back(dv, xh, r, gain)
    use.sums(0, dh)
    use.sums(1, dv * xh)
    use.sums(2, dv)
    dh5_ref[0] = dh
    dd2_ref[0] = dh + ffn_back(use, low, hid_s[...], slope_s[...], dh.astype(BF16), False)


def ffn_bwd(use, small, dm_ref, h2_ref, h1_ref, hid_ref, slope_ref, de1_ref, dh2_ref):
    low = (normalize(h1_ref[0])[0] * row(small, ENC_GAIN) + row(small, ENC_SHIFT)).astype(BF16)
    xh, r = normalize(h2_ref[0])
    dv = dm_ref[0]
    dh = norm_back(dv, xh, r, row(small, ENC_GAIN + 1))
    use.sums(0, dh)
    use.sums(1, dv * xh)
    use.sums(2, dv)
    dh2_ref[0] = dh
    de1_ref[0] = dh + ffn_back(use, low, hid_ref[0], slope_ref[0], dh.astype(BF16))


def attention_bwd(use, q, k, v, a_ref, go_s, put):
    for p in range(a_ref.shape[1]):
        at = p * PAIR
        dq, dk, dv = pair_backward(q(at), k(at), v(at), a_ref[0, p], go_s[:, at : at + PAIR])
        use.sums(0, dq, at)
        use.sums(1, dv, at)
        put(at, dq.astype(BF16), dk.astype(BF16), dv.astype(BF16))


def block_sums(use, dv, xh, dh):
    use.sums(2, dh)
    use.sums(3, dv * xh)
    use.sums(4, dv)


def self_bwd(use, small, dv, h_ref, x_ref, extra_ref, qkv_ref, a_ref, o_ref, dx_ref, go_s, g_s, gain_row):
    size, width = x_ref.shape[1:]
    w, acc = use.w, use.acc
    xh, r = normalize(h_ref[0])
    dh = norm_back(dv, xh, r, row(small, gain_row))
    block_sums(use, dv, xh, dh)
    g = dh.astype(BF16)
    acc[1][...] += nn(o_ref[0].T, g)
    use.send(1)
    use.ready(1)
    go_s[...] = nt(g, w[1][...]).astype(BF16)

    def part(k):
        return lambda at: qkv_ref[0, :, k * width + at : k * width + at + PAIR]

    def put(at, *parts):
        for k, v in enumerate(parts):
            g_s[:, k * width + at : k * width + at + PAIR] = v

    attention_bwd(use, part(0), part(1), part(2), a_ref, go_s, put)
    acc[0][...] += nn(x_ref[0].T, g_s[...])
    use.send(0)
    use.ready(0)
    dx_ref[0] = (dh + extra_ref[0] + nt(g_s[...], w[0][...])).astype(BF16)


def cross_bwd(use, small, dv, h4_ref, h3_ref, h2_ref, q_ref, kv_ref, a_ref, o_ref, dm_ref, go_s, gq_s, gkv_s):
    width = h4_ref.shape[2]
    w, acc = use.w, use.acc
    first = decoder_first(small, h3_ref).astype(BF16)
    memory = memory_rows(small, h2_ref)
    xh, r = normalize(h4_ref[0])
    dh = norm_back(dv, xh, r, row(small, DEC_GAIN + 1))
    block_sums(use, dv, xh, dh)
    g = dh.astype(BF16)
    acc[2][...] += nn(o_ref[0].T, g)
    use.send(2)
    use.ready(2)
    go_s[...] = nt(g, w[2][...]).astype(BF16)

    def put(at, dq, dk, dvv):
        gq_s[:, at : at + PAIR] = dq
        gkv_s[:, at : at + PAIR] = dk
        gkv_s[:, width + at : width + at + PAIR] = dvv

    attention_bwd(
        use,
        lambda at: q_ref[0, :, at : at + PAIR],
        lambda at: kv_ref[0, :, at : at + PAIR],
        lambda at: kv_ref[0, :, width + at : width + at + PAIR],
        a_ref, go_s, put,
    )
    acc[0][...] += nn(first.T, gq_s[...])
    acc[1][...] += nn(memory.T, gkv_s[...])
    use.send(0, 1)
    use.ready(0, 1)
    dm_ref[0] = nt(gkv_s[...], w[1][...])
    out = dh + nt(gq_s[...], w[0][...])
    return out


def call(kernel, name, count, meta, rows, small, parts, after, out_rows, scratch):
    def by_row(shape):
        tail = tuple(shape[1:])
        return pl.BlockSpec((1,) + tail, lambda i, k=len(tail): (i,) + (0,) * k)

    width = small.shape[1]
    backs = [layout for layout, _, _, back in parts if back]
    shapes = list(out_rows) + [jax.ShapeDtypeStruct((8, width), F32)] * len(backs)
    for layout in backs:
        shapes += layout.grad_shapes()

    def body(meta, *refs):
        refs = list(refs)

        def next_refs(n):
            head = refs[:n]
            del refs[:n]
            return head

        ins = next_refs(len(rows))
        small_ref = next_refs(1)[0]
        sources = [next_refs(len(part[1])) for part in parts]
        next_refs(len(after))
        outs = next_refs(len(out_rows))
        sums = next_refs(len(backs))
        grads = [next_refs(len(layout.grad_shapes())) for layout in backs]
        uses, at = [], 0
        for (layout, _, order, back), src in zip(parts, sources):
            n = len(layout.names)
            use = Use(layout, meta[0], src, next_refs(n), next_refs(1)[0])
            use.begin(order)
            if back:
                use.add_sums(sums[at], grads[at], next_refs(n), next_refs(n), next_refs(1)[0])
                at += 1
            uses.append(use)
        for use in uses:
            use.clear()

        def sentence(*blocks):
            step = pl.program_id(0)
            for use in uses:
                use.step, use.last = step, step == count - 1
            kernel(meta, step, small_ref, uses, blocks[: len(rows)], blocks[len(rows) :], refs)

        pltpu.emit_pipeline(
            sentence, grid=(count,), in_specs=[by_row(v.shape) for v in rows], out_specs=[by_row(v.shape) for v in out_rows]
        )(*ins, *outs)
        for use in uses:
            use.end()

    scratches = []
    for layout, _, _, back in parts:
        scratches += layout.w_scratch() + (layout.acc_scratch() if back else [])
    hbm = pl.BlockSpec(memory_space=pl.ANY)
    vmem = pl.BlockSpec(memory_space=pltpu.VMEM)
    n_sources = sum(len(part[1]) for part in parts)
    result = pl.pallas_call(
        body,
        in_specs=[pl.BlockSpec(memory_space=pltpu.SMEM)] + [hbm] * len(rows) + [vmem] + [hbm] * (n_sources + len(after)),
        out_specs=[hbm] * len(out_rows) + [vmem] * len(backs) + [hbm] * (len(shapes) - len(out_rows) - len(backs)),
        out_shape=shapes,
        scratch_shapes=scratches + list(scratch),
        compiler_params=pltpu.CompilerParams(vmem_limit_bytes=VMEM_LIMIT),
        cost_estimate=pl.CostEstimate(flops=COST, bytes_accessed=COST, transcendentals=0),
        name=name,
    )(meta, *rows, small, *[v for part in parts for v in part[1]], *after)
    n = len(out_rows)
    given, sums, rest = result[:n], result[n : n + len(backs)], list(result[n + len(backs) :])
    grads = []
    for layout in backs:
        k = len(layout.grad_shapes())
        grads.append(rest[:k])
        rest = rest[k:]
    return given, sums, grads


def lookup(pair_order, lengths):
    indices = jnp.arange(lengths.shape[0], dtype=jnp.int32)
    chosen = jnp.where(pair_order[:, None] == indices[None, :], lengths[None, :], 0)
    return jnp.sum(chosen, axis=1)


class Step:
    def __init__(self, layouts, source, target, cotangent, meta):
        self.layouts, self.meta = layouts, meta
        self.source, self.target, self.cotangent = source, target, cotangent
        self.count, self.size, self.width = source.shape
        self.hidden = layouts[ENC_FFN].shapes[0][1]
        pairs = self.width // PAIR
        self.shares = jax.ShapeDtypeStruct((self.count, pairs, 2 * self.size, self.size), BF16)
        self.small, self.w = None, {}

    def f32(self, cols):
        return jax.ShapeDtypeStruct((self.count, self.size, cols), F32)

    def bf16(self, cols):
        return jax.ShapeDtypeStruct((self.count, self.size, cols), BF16)

    def run(self, kernel, name, groups, rows, out_rows, back=(), scratch=(), after=()):
        parts = [(self.layouts[g], self.w[g], order, g in back) for g, order in groups]
        return call(kernel, name, self.count, self.meta, rows, self.small, parts, list(after), out_rows, scratch)

    def rows_of(self, *columns):
        return [pltpu.VMEM((self.size, c), BF16) for c in columns]

    def enc_self_fwd(self, after=()):
        d = self.width

        def kernel(meta, step, small, uses, ins, outs, scratch):
            self_fwd(uses[0], small, *ins, *outs, meta[2 + step], False, ENC_BIAS)

        (self.h1, self.enc_qkv, self.enc_a, self.enc_o), _, _ = self.run(
            kernel, "enc_self_fwd", ((ENC_SELF, (0, 1)),), [self.source],
            [self.f32(d), self.bf16(3 * d), self.shares, self.bf16(d)], after=after,
        )

    def dec_self_fwd(self, after=()):
        d = self.width

        def kernel(meta, step, small, uses, ins, outs, scratch):
            self_fwd(uses[0], small, *ins, *outs, meta[2 + self.count + step], True, DEC_BIAS)

        (self.h3, self.dec_qkv, self.dec_a, self.dec_o), _, _ = self.run(
            kernel, "dec_self_fwd", ((DEC_SELF, (0, 1)),), [self.target],
            [self.f32(d), self.bf16(3 * d), self.shares, self.bf16(d)], after=after,
        )

    def enc_ffn_fwd(self, after=()):
        def kernel(meta, step, small, uses, ins, outs, scratch):
            ffn_fwd(uses[0], small, *ins, *outs)

        (self.h2, self.hid, self.slope), _, _ = self.run(
            kernel, "enc_ffn_fwd", ((ENC_FFN, (0, 1)),), [self.h1, self.source],
            [self.f32(self.width), self.bf16(self.hidden), self.bf16(self.hidden)], after=after,
        )

    def dec_middle(self, after=()):
        d = self.width

        def kernel(meta, step, small, uses, ins, outs, scratch):
            cross_fwd(uses[0], small, *ins[:2], *outs[:5], meta[2 + step])
            ffn_both(uses[1], small, outs[0], *ins[2:], *outs[5:], *scratch, meta[2 + self.count + step])

        rows, sums, grads = self.run(
            kernel, "dec_middle", ((CROSS, (0, 1, 2)), (DEC_FFN, (0, 1))), [self.h3, self.h2, self.target, self.cotangent],
            [self.f32(d), self.bf16(d), self.bf16(2 * d), self.shares, self.bf16(d), self.bf16(d), self.f32(d),
             self.f32(d)],
            (DEC_FFN,), self.rows_of(self.hidden, self.hidden), after,
        )
        self.h4, self.q, self.kv, self.cross_a, self.cross_o, self.decoded, self.dd2, self.dh5 = rows
        self.sums_df = sums[0]
        return grads[0]

    def dec_bwd(self, after=()):
        d = self.width

        def kernel(meta, step, small, uses, ins, outs, scratch):
            dd2, h4, h3, h2, q, kv, cross_a, cross_o, target, dh5, qkv, a, o = ins
            go, gq, gkv, g = scratch
            dd1 = cross_bwd(uses[0], small, dd2[0], h4, h3, h2, q, kv, cross_a, cross_o, outs[0], go, gq, gkv)
            self_bwd(uses[1], small, dd1, h3, target, dh5, qkv, a, o, outs[1], go, g, DEC_GAIN)

        rows, (self.sums_c, self.sums_ds), grads = self.run(
            kernel, "dec_bwd", ((CROSS, (2, 0, 1)), (DEC_SELF, (1, 0))),
            [self.dd2, self.h4, self.h3, self.h2, self.q, self.kv, self.cross_a, self.cross_o, self.target, self.dh5,
             self.dec_qkv, self.dec_a, self.dec_o],
            [self.f32(d), self.bf16(d)], (CROSS, DEC_SELF), self.rows_of(d, d, 2 * d, 3 * d), after,
        )
        self.dm, self.target_grad = rows
        return grads

    def enc_ffn_bwd(self, after=()):
        d = self.width

        def kernel(meta, step, small, uses, ins, outs, scratch):
            ffn_bwd(uses[0], small, *ins, *outs)

        (self.de1, self.dh2), (self.sums_ef,), grads = self.run(
            kernel, "enc_ffn_bwd", ((ENC_FFN, (1, 0)),), [self.dm, self.h2, self.h1, self.hid, self.slope],
            [self.f32(d), self.f32(d)], (ENC_FFN,), (), after,
        )
        return grads[0]

    def enc_self_bwd(self, after=()):
        d = self.width

        def kernel(meta, step, small, uses, ins, outs, scratch):
            self_bwd(uses[0], small, ins[0][0], *ins[1:], *outs, *scratch, ENC_GAIN)

        (self.source_grad,), (self.sums_es,), grads = self.run(
            kernel, "enc_self_bwd", ((ENC_SELF, (1, 0)),),
            [self.de1, self.h1, self.source, self.dh2, self.enc_qkv, self.enc_a, self.enc_o], [self.bf16(d)],
            (ENC_SELF,), self.rows_of(d, 3 * d), after,
        )
        return grads[0]

    def small_sums(self):
        es, ef, ds, c, df = self.sums_es, self.sums_ef, self.sums_ds, self.sums_c, self.sums_df
        return jnp.concatenate(
            [es[0:3], ef[0:1], es[3:4], ef[1:2], es[4:5], ef[2:3], ds[0:3], c[0:3], df[0:1], ds[3:4], c[3:4], df[1:2],
             ds[4:5], c[4:5], df[2:3], jnp.zeros((3, self.width), F32), ef[4:8], df[4:8]], axis=0,
        )


def simple(kernel, name, meta, inputs, outs, scratch=(), after=(), limit=SIMPLE_LIMIT):
    specs = [pl.BlockSpec(memory_space=pltpu.VMEM)] * len(inputs)
    specs += [pl.BlockSpec(memory_space=pl.ANY)] * len(after)

    def body(meta, *refs):
        return kernel(meta, *refs[: len(inputs)], *refs[len(inputs) + len(after) :])

    return pl.pallas_call(
        body,
        in_specs=[pl.BlockSpec(memory_space=pltpu.SMEM)] + specs,
        out_specs=[pl.BlockSpec(memory_space=pltpu.VMEM)] * len(outs),
        out_shape=list(outs),
        scratch_shapes=list(scratch),
        compiler_params=pltpu.CompilerParams(vmem_limit_bytes=limit),
        cost_estimate=pl.CostEstimate(flops=COST, bytes_accessed=COST, transcendentals=0),
        name=name,
    )(meta, *inputs, *after)


def pack_kernel(plan, nz, meta, *refs):
    n_in = sum(len(p) for p in plan)
    shards = refs[:n_in]
    small_refs = refs[n_in : n_in + len(SMALLS) + len(LINES)]
    outs = refs[n_in + len(small_refs) : -1]
    rows = refs[-1]
    at = 0
    for out, chunk in zip(outs, plan):
        for row in chunk:
            shard = shards[at]
            rd, cols = shard.shape
            for cb in range(cols // TILE):
                out[row + cb * rd : row + (cb + 1) * rd, :] = shard[:, cb * TILE : (cb + 1) * TILE]
            at += 1
    rank = meta[0] * nz + meta[1]
    rows[...] = jnp.zeros_like(rows)
    for ref, (_, row, _) in zip(small_refs, SMALLS + LINES):
        lines, part = ref.shape
        lane = lax.broadcasted_iota(jnp.int32, (part, TILE), 1)
        spread = (lane % part == lax.broadcasted_iota(jnp.int32, (part, TILE), 0)).astype(BF16)
        tiled = nn(ref[...], spread)
        across = lax.broadcasted_iota(jnp.int32, (lines, TILE), 1)
        if row >= ENC_FFN_BIAS:
            per = TILE // part
            tiled = jnp.broadcast_to(tiled, (4, TILE))
            across = lax.broadcasted_iota(jnp.int32, (4, TILE), 1)
            down = lax.broadcasted_iota(jnp.int32, (4, TILE), 0)
            ok = (across // part == rank % per) & (down == rank // per)
            rows[row : row + 4, :] = jnp.where(ok, tiled, 0.0)
        else:
            rows[row : row + lines, :] = jnp.where(across // part == rank, tiled, 0.0)
    outs[0][outs[0].shape[0] - SMALL_ROWS :, :] = rows[...].astype(BF16)


def along_z_kernel(nz, rows, tail, meta, *refs):
    parts = refs[:nz]
    out = refs[nz]
    z = meta[1]
    for s in range(nz):
        at = pl.multiple_of(((z + nz - s) % nz) * rows, 16)
        out[pl.ds(at, rows), :] = parts[s][:rows, :]
    if tail:
        total = parts[0][rows:, :].astype(F32)
        for s in range(1, nz):
            total = total + parts[s][rows:, :].astype(F32)
        out[nz * rows :, :] = total.astype(BF16)


def add_cores_kernel(counts, tail, halves, meta, *refs):
    n = len(counts)
    outs = refs[2 * n + 2 * bool(tail) :]
    chips, nz = refs[0].shape[:2]
    total = sum(counts)
    for k in range(chips):
        out = outs[k % 2].at[k // 2] if halves else outs[k]
        for z in range(nz):
            at = z * total
            for g, rows in enumerate(counts):
                out[at : at + rows, :] = (
                    refs[2 * g][k, z].astype(F32) + refs[2 * g + 1][k, z].astype(F32)
                ).astype(BF16)
                at += rows
        if tail:
            out[nz * total :, :] = (refs[2 * n][...].astype(F32) + refs[2 * n + 1][...].astype(F32)).astype(BF16)


def add_half_kernel(meta, kept, got, own, second):
    own[...] = (kept[0].astype(F32) + got[0].astype(F32)).astype(BF16)
    second[...] = (kept[1].astype(F32) + got[1].astype(F32)).astype(BF16)


def add_two_kernel(meta, one, two, out):
    out[...] = (one[...].astype(F32) + two[...].astype(F32)).astype(BF16)


def add_chips_kernel(nz, rows, tail, n_parts, meta, *refs):
    parts, outs = refs[:n_parts], refs[n_parts:]
    z = meta[1]
    for s in range(nz):
        at = pl.multiple_of(((z + s) % nz) * rows, 16)
        total = parts[0][pl.ds(at, rows), :].astype(F32)
        for part in parts[1:]:
            total = total + part[pl.ds(at, rows), :].astype(F32)
        outs[s][:rows, :] = total.astype(outs[s].dtype)
    if tail:
        total = parts[0][nz * rows :, :].astype(F32)
        for part in parts[1:]:
            total = total + part[nz * rows :, :].astype(F32)
        for s in range(nz):
            outs[s][rows:, :] = total.astype(outs[s].dtype)


def add_z_kernel(nz, places, rows, tail, meta, *refs):
    parts, outs = refs[:nz], refs[nz:]
    for (row, rd, cols), out in zip(places, outs):
        for cb in range(cols // TILE):
            at = row + cb * rd
            total = parts[0][at : at + rd, :].astype(F32)
            for part in parts[1:]:
                total = total + part[at : at + rd, :].astype(F32)
            out[:, cb * TILE : (cb + 1) * TILE] = total
    if tail:
        rank = meta[0] * nz + meta[1]
        total = parts[0][rows:, :]
        for part in parts[1:]:
            total = total + part[rows:, :].astype(F32)
        for out, (_, row, _) in zip(outs[len(places) :], SMALLS + LINES):
            lines, part = out.shape
            if row >= ENC_FFN_BIAS:
                per = TILE // part
                down = lax.broadcasted_iota(jnp.int32, (8, TILE), 0)
                base = total[24:32, :]
                picked = jnp.sum(
                    jnp.where(down == rank // per + (row - 24), base, 0.0), axis=0, keepdims=True
                )
                moved = pltpu.roll(jnp.broadcast_to(picked, (8, TILE)), TILE - (rank % per) * part, 1)
                out[...] = moved[0:1, :part]
            else:
                first = row // 8 * 8
                moved = pltpu.roll(total[first : first + 24 if first < 8 else 24, :], TILE - rank * part, 1)
                out[...] = moved[row - first : row - first + lines, :part]


def swap(v, size, mask):
    return lax.ppermute(v, DP, [(i, i ^ mask) for i in range(size)])


def shift(v, size, by):
    return lax.ppermute(v, FSDP, [(i, (i + by) % size) for i in range(size)])


def across(v, size, own, other):
    return lax.ppermute(v, DP, [(i, i ^ (other if i % 2 else own)) for i in range(size)])


def hold(values, *first):
    return lax.optimization_barrier((values, first))[0]


class Exchange:
    def __init__(self, layouts, meta, nd, nz):
        self.layouts, self.meta, self.nd, self.nz = layouts, meta, nd, nz

    def pack(self, shards):
        plan, sizes, inputs = [], [], []
        for groups in GATHERS:
            rows, first = [], 0
            for g in groups:
                self.layouts[g].first = first
                for n, at in zip(self.layouts[g].names, self.layouts[g].offsets):
                    rows.append(first + at)
                    inputs.append(shards[n])
                first += self.layouts[g].rows
            for g in groups:
                self.layouts[g].span = first
            plan.append(rows)
            sizes.append(first)
        inputs += [shards[n] for n, _, _ in SMALLS] + [shards[n].reshape(1, -1) for n, _, _ in LINES]
        self.sizes = sizes
        self.tails = [SMALL_ROWS] + [0] * (len(GATHERS) - 1)
        return simple(
            functools.partial(pack_kernel, plan, self.nz), "pack", self.meta, inputs,
            [jax.ShapeDtypeStruct((r + t, TILE), BF16) for r, t in zip(sizes, self.tails)],
            [pltpu.VMEM((SMALL_ROWS, TILE), F32)], limit=VMEM_LIMIT,
        )

    def gather_z(self, pack):
        return [pack] + [shift(pack, self.nz, s) for s in range(1, self.nz)]

    def join_z(self, c, parts):
        rows, tail = self.sizes[c], self.tails[c]
        return simple(
            functools.partial(along_z_kernel, self.nz, rows, tail), "join", self.meta, parts,
            [jax.ShapeDtypeStruct((self.nz * rows + tail, TILE), BF16)],
        )[0]

    def gather_chips(self, joined, *before):
        first = across(joined, self.nd, 4, 2)
        second = across(joined, self.nd, 2, 4)
        if before:
            first = hold(first, *before)
        return [joined, first, second, across(first, self.nd, 2, 4)]

    def gather_cores(self, pieces):
        return [v for piece in pieces for v in (piece, swap(piece, self.nd, 1))]

    def to_cores(self, grads):
        return [grads[0], swap(grads[1], self.nd, 1)]

    def add_cores(self, groups, parts, tail=None, halves=False):
        counts = [self.layouts[g].rows for g in groups]
        extra = 0 if tail is None else SMALL_ROWS
        if extra:
            parts = parts + [tail, swap(tail, self.nd, 1)]
        return simple(
            functools.partial(add_cores_kernel, counts, extra, halves), "add_cores", self.meta, parts,
            [jax.ShapeDtypeStruct(((2,) if halves else ()) + (self.nz * sum(counts) + extra, TILE), BF16)]
            * (2 if halves else self.nd // 2),
        )

    def add_half(self, kept, got):
        shape = jax.ShapeDtypeStruct(kept.shape[1:], BF16)
        return simple(add_half_kernel, "add_half", self.meta, [kept, got], [shape, shape])

    def to_first(self, v):
        return across(v, self.nd, 4, 2)

    def to_second(self, v):
        return across(v, self.nd, 2, 4)

    def to_chips(self, sums):
        return [sums[0], self.to_first(sums[1]), self.to_second(sums[2]), swap(sums[3], self.nd, 6)]

    def add_chips(self, groups, parts, extra=0):
        rows = sum(self.layouts[g].rows for g in groups)
        return simple(
            functools.partial(add_chips_kernel, self.nz, rows, extra, len(parts)), "add_chips", self.meta, parts,
            [jax.ShapeDtypeStruct((rows + extra, TILE), F32 if s == 0 else BF16) for s in range(self.nz)],
        )

    def add_chips_flat(self, parts):
        shape = jax.ShapeDtypeStruct(parts[0].shape, BF16)
        return simple(add_two_kernel, "add_two", self.meta, parts, [shape])[0]

    def to_z(self, sums):
        return [sums[0]] + [shift(sums[s], self.nz, s) for s in range(1, self.nz)]

    def add_z(self, groups, parts, extra=0):
        ranks, first, places = self.nd * self.nz, 0, []
        for g in groups:
            layout = self.layouts[g]
            places += [(first + at, r // ranks, c) for at, (r, c) in zip(layout.offsets, layout.shapes)]
            first += layout.rows
        outs = [jax.ShapeDtypeStruct((rd, c), F32) for _, rd, c in places]
        if extra:
            wide = TILE // ranks
            outs += [jax.ShapeDtypeStruct((lines, wide), F32) for _, _, lines in SMALLS]
            outs += [jax.ShapeDtypeStruct((1, 4 * wide), F32)] * 2
        return simple(
            functools.partial(add_z_kernel, len(parts), places, first, extra), "add_z", self.meta, parts, outs
        )


def by_pieces(layouts, source, target, cotangent, place, meta, shards, nd, nz):
    ex = Exchange(layouts, place, nd, nz)
    packs = ex.pack(shards)
    st = Step(layouts, source, target, cotangent, hold(meta, packs))
    along0 = ex.gather_z(packs[0])
    joined0 = ex.join_z(0, along0)
    along1 = ex.gather_z(hold(packs[1], joined0))
    pieces = ex.gather_cores(hold(ex.gather_chips(joined0), along1))
    st.w[ENC_SELF] = pieces
    st.small = sum(p[p.shape[0] - SMALL_ROWS :].astype(F32) for p in pieces)
    joined1 = ex.join_z(1, along1)
    along2 = ex.gather_z(hold(packs[2], joined1))
    st.enc_self_fwd(after=[joined1])
    along2 = hold(along2, st.h1)
    chips1 = ex.gather_chips(joined1, along2)
    joined2 = ex.join_z(2, hold(along2, chips1[1]))
    st.w[ENC_FFN] = st.w[DEC_SELF] = ex.gather_cores(hold(chips1, joined2))
    st.dec_self_fwd(after=[joined2])
    chips2 = ex.gather_chips(joined2, st.h3)
    early2 = ex.gather_cores(hold(chips2[:3], st.h3))
    st.enc_ffn_fwd(after=[chips2[1], chips2[2]])
    st.w[CROSS] = st.w[DEC_FFN] = hold(early2, st.h2) + ex.gather_cores(hold(chips2[3:], st.h2))
    result = [None] * len(shards)

    def put(groups, outs):
        names = [n for g in groups for n in GROUPS[g]]
        names += [n for n, _, _ in SMALLS + LINES]
        for n, v in zip(names, outs):
            result[n] = v.reshape(shards[n].shape)

    df = st.dec_middle()[0]
    df = lax.psum_scatter(df.reshape(nd, nz, *df.shape[1:]), DP, scatter_dimension=0, tiled=True)
    both = (CROSS, DEC_SELF)
    cr, ds = st.dec_bwd()
    cr_kept, cr = ex.add_cores(both, ex.to_cores(cr) + ex.to_cores(ds), halves=True)
    cr = ex.to_first(cr)
    ef = st.enc_ffn_bwd(after=[cr_kept])
    cr, df = hold((cr, df), st.de1)
    ef = ex.to_cores(hold(ef, cr))
    cr_own, cr = ex.add_half(cr_kept, cr)
    cr = ex.to_second(cr)
    ef_kept, ef = ex.add_cores((ENC_FFN,), hold(ef, cr_own), halves=True)
    cr = ex.add_chips_flat([cr_own, hold(cr, ef_kept)])
    ef = ex.to_first(ef)
    late = jnp.concatenate([df[0], cr.reshape(nz, -1, TILE)], axis=1)
    late = lax.psum_scatter(late, FSDP, scatter_dimension=0, tiled=True)[0]
    es = st.enc_self_bwd(after=[cr, ef_kept])
    ef = hold(ef, st.source_grad)
    es = ex.to_cores(hold(es, ef))
    tail = st.small_sums().astype(BF16)
    ef_own, ef = ex.add_half(ef_kept, ef)
    ef = ex.to_second(ef)
    es = ex.to_chips(ex.add_cores((ENC_SELF,), hold(es, ef_own), tail))
    ef = ex.to_z(ex.add_chips((ENC_FFN,), hold([ef_own, ef], es[0])))
    es = ex.to_z(ex.add_chips((ENC_SELF,), hold(es, ef[0]), SMALL_ROWS))
    put((ENC_FFN,), ex.add_z((ENC_FFN,), hold(ef, es[0])))
    late = hold(late, result[A_ENC_IN])
    put((DEC_FFN,) + both, ex.add_z((DEC_FFN,) + both, [late]))
    es = hold(es, result[A_DEC_IN])
    put((ENC_SELF,), ex.add_z((ENC_SELF,), es, SMALL_ROWS))
    return (st.decoded, st.source_grad, st.target_grad) + tuple(result)


def whole(layouts, source, target, cotangent, meta, shards):
    small_names = [n for n, _, _ in SMALLS]
    full = [
        lax.all_gather(v, AXES, axis=1 if n in small_names else 0, tiled=True) for n, v in enumerate(shards)
    ]
    width = source.shape[2]
    st = Step(layouts, source, target, cotangent, meta)
    st.small = jnp.concatenate(
        [full[n] for n in small_names]
        + [jnp.zeros((3, width), BF16)]
        + [full[n].reshape(-1, width) for n, _, _ in LINES],
        axis=0,
    ).astype(F32)
    st.w = {g: [full[n] for n in names] for g, names in enumerate(GROUPS)}
    st.enc_self_fwd()
    st.enc_ffn_fwd()
    st.dec_self_fwd()
    grads = [None] * len(GROUPS)
    grads[DEC_FFN] = st.dec_middle()
    grads[CROSS], grads[DEC_SELF] = st.dec_bwd()
    grads[ENC_FFN] = st.enc_ffn_bwd()
    grads[ENC_SELF] = st.enc_self_bwd()
    sums = st.small_sums()
    result = [None] * len(shards)
    for g, names in enumerate(GROUPS):
        for n, v in zip(names, grads[g]):
            result[n] = v.astype(F32)
    for n, row, lines in SMALLS:
        result[n] = sums[row : row + lines]
    for n, row, _ in LINES:
        result[n] = sums[row : row + 4].reshape(-1)
    result = [
        lax.psum_scatter(v, AXES, scatter_dimension=1 if n in small_names else 0, tiled=True)
        for n, v in enumerate(result)
    ]
    return (st.decoded, st.source_grad, st.target_grad) + tuple(result)


def local(nd, nz, source, target, cotangent, pair_order, source_lengths, target_lengths, *shards):
    ranks = nd * nz
    matrices = [n for names in GROUPS for n in names]
    shapes = {n: (shards[n].shape[0] * ranks, shards[n].shape[1]) for n in matrices}
    pieces = nd == 8 and all(shards[n].shape[0] % 16 == 0 for n in matrices)
    modes = (PIECES, PIECES, PIECES, PIECES, RANKS) if pieces else (WHOLE,) * len(GROUPS)
    layouts = [Layout(g, shapes, modes[g], nd, nz) for g in range(len(GROUPS))]
    place = jnp.stack([lax.axis_index(DP), lax.axis_index(FSDP)]).astype(jnp.int32)
    meta = jnp.concatenate([place, lookup(pair_order, source_lengths), lookup(pair_order, target_lengths)])
    if pieces:
        return by_pieces(layouts, source, target, cotangent, place, meta, shards, nd, nz)
    return whole(layouts, source, target, cotangent, meta, shards)


def specs():
    split, rows, cols = P(AXES, None, None), P(AXES, None), P(None, AXES)
    line = P(AXES)
    weights = (
        rows, rows, rows, rows, cols, line, cols, cols,
        rows, rows, rows, rows, rows, rows, rows, cols, line, cols, cols,
    )
    return (split, split, split, line, P(), P()) + weights, (split, split, split) + weights


def solution(mesh):
    in_specs, out_specs = specs()
    return jax.shard_map(
        functools.partial(local, mesh.shape[DP], mesh.shape[FSDP]),
        mesh=mesh, in_specs=in_specs, out_specs=out_specs, check_vma=False,
    )
```

```python
import functools

import jax
import jax.numpy as jnp
from jax import lax
from jax.experimental import pallas as pl
from jax.experimental.pallas import tpu as pltpu
from jax.sharding import PartitionSpec as P

F32 = jnp.float32
BF16 = jnp.bfloat16
DP, FSDP = "dp", "fsdp"
AXES = (DP, FSDP)
HEAD_DIM = 64
PAIR = 2 * HEAD_DIM
TILE = 512
epsilon = 1e-05
FORWARD_TILE = 256
COST = 1
SIMPLE_LIMIT = 16 * 1024 * 1024
VMEM_LIMIT = 56 * 1024 * 1024

ENC_BIAS, ENC_GAIN, ENC_SHIFT = 0, 4, 6
DEC_BIAS, DEC_GAIN, DEC_SHIFT = 8, 15, 18
ENC_FFN_BIAS, DEC_FFN_BIAS = 24, 28
SMALL_ROWS = 32

(A_ENC_QKV, A_ENC_OUT, A_ENC_IN, A_ENC_BACK, A_ENC_BIAS, A_ENC_FBIAS, A_ENC_GAIN, A_ENC_SHIFT, A_DEC_QKV, A_DEC_OUT,
 A_CROSS_Q, A_CROSS_KV, A_CROSS_OUT, A_DEC_IN, A_DEC_BACK, A_DEC_BIAS, A_DEC_FBIAS, A_DEC_GAIN, A_DEC_SHIFT) = range(19)
ENC_SELF, ENC_FFN, DEC_SELF, CROSS, DEC_FFN = range(5)
GROUPS = (
    (A_ENC_QKV, A_ENC_OUT),
    (A_ENC_IN, A_ENC_BACK),
    (A_DEC_QKV, A_DEC_OUT),
    (A_CROSS_Q, A_CROSS_KV, A_CROSS_OUT),
    (A_DEC_IN, A_DEC_BACK),
)
SMALLS = (
    (A_ENC_BIAS, ENC_BIAS, 4), (A_ENC_GAIN, ENC_GAIN, 2), (A_ENC_SHIFT, ENC_SHIFT, 2),
    (A_DEC_BIAS, DEC_BIAS, 7), (A_DEC_GAIN, DEC_GAIN, 3), (A_DEC_SHIFT, DEC_SHIFT, 3),
)
LINES = ((A_ENC_FBIAS, ENC_FFN_BIAS, 1), (A_DEC_FBIAS, DEC_FFN_BIAS, 1))
WHOLE, PIECES, RANKS = range(3)
GATHERS = ((ENC_SELF,), (ENC_FFN, DEC_SELF), (CROSS, DEC_FFN))


def nn(a, b):
    return lax.dot_general(a, b, (((1,), (0,)), ((), ())), preferred_element_type=F32)


def nt(a, b):
    return lax.dot_general(a, b, (((1,), (1,)), ((), ())), preferred_element_type=F32)


def tn(a, b):
    return lax.dot_general(a, b, (((0,), (0,)), ((), ())), preferred_element_type=F32)


def tokens_sum(v):
    return jnp.sum(v, axis=0, keepdims=True)


def normalize(h):
    c = h - jnp.mean(h, axis=-1, keepdims=True)
    r = lax.rsqrt(jnp.mean(c * c, axis=-1, keepdims=True) + epsilon)
    return c * r, r


def norm_back(dv, xh, r, g):
    hh = dv * g
    return r * (
        hh - jnp.mean(hh, axis=-1, keepdims=True) - xh * jnp.mean(hh * xh, axis=-1, keepdims=True)
    )


def gelu_parts(u):
    c = 0.7978845608028654
    sq = u * u
    half = 0.5 + 0.5 * jnp.tanh(u * (c + (c * 0.044715) * sq))
    gelu = u * half
    return gelu, half + gelu * (1.0 - half) * (2.0 * c + (6.0 * c * 0.044715) * sq)


class Layout:
    def __init__(self, group, shapes, mode, nd, nz):
        self.names = GROUPS[group]
        self.mode = mode
        self.shapes = [shapes[n] for n in self.names]
        self.span = 0
        self.nd, self.nz = nd, nz
        self.offsets, row = [], 0
        for rows, cols in self.shapes:
            self.offsets.append(row)
            row += (rows // (nd * nz)) * (cols // TILE)
        self.rows = row
        self.first = 0

    def n_sources(self):
        return len(self.names) if self.mode == WHOLE else self.nd

    def w_scratch(self):
        return [pltpu.VMEM(s, BF16) for s in self.shapes] + [
            pltpu.SemaphoreType.DMA((len(self.shapes),))
        ]

    def acc_scratch(self):
        return (
            [pltpu.VMEM(s, F32) for s in self.shapes]
            + [pltpu.VMEM(s, BF16) for s in self.shapes]
            + [pltpu.SemaphoreType.DMA((len(self.shapes),))]
        )

    def start_loads(self, sources, weights, sems, dp, order):
        for j in order:
            rows, cols = self.shapes[j]
            if self.mode == WHOLE:
                pltpu.make_async_copy(sources[j], weights[j], sems.at[j]).start()
                continue
            rd = rows // (self.nd * self.nz)
            view = weights[j].reshape(self.nd, self.nz, rd, cols)
            for m in range(self.nd):
                mask = self.masks(dp)[m]
                for cb in range(cols // TILE):
                    pltpu.make_async_copy(
                        sources[m]
                        .at[pl.ds(0, self.nz * self.span), :]
                        .reshape(self.nz, self.span, TILE)
                        .at[:, pl.ds(self.first + self.offsets[j] + cb * rd, rd), :],
                        view.at[dp ^ mask, :, :, pl.ds(cb * TILE, TILE)],
                        sems.at[j],
                    ).start()

    def masks(self, dp):
        first = jnp.where(dp % 2 == 0, 4, 2)
        return [0, 1, first, 7 - first, 6 - first, first + 1, 6, 7]

    def wait_load(self, weights, sems, j):
        pltpu.make_async_copy(weights[j], weights[j], sems.at[j]).wait()

    def grad_shapes(self):
        if self.mode == WHOLE:
            return [jax.ShapeDtypeStruct(s, BF16) for s in self.shapes]
        if self.mode == RANKS:
            return [jax.ShapeDtypeStruct((self.nd * self.nz, self.rows, TILE), BF16)]
        return [jax.ShapeDtypeStruct((self.nd // 2, self.nz, self.rows, TILE), BF16)] * 2

    def start_store(self, acc, stage, outs, sems, dp, j):
        rows, cols = self.shapes[j]
        stage[j][...] = acc[j][...].astype(BF16)
        if self.mode == WHOLE:
            pltpu.make_async_copy(stage[j], outs[j], sems.at[j]).start()
            return
        rd = rows // (self.nd * self.nz)
        if self.mode == RANKS:
            view = stage[j].reshape(self.nd * self.nz, rd, cols)
            for cb in range(cols // TILE):
                pltpu.make_async_copy(
                    view.at[:, :, pl.ds(cb * TILE, TILE)],
                    outs[0].at[:, pl.ds(self.offsets[j] + cb * rd, rd), :],
                    sems.at[j],
                ).start()
            return
        view = stage[j].reshape(self.nd, self.nz, rd, cols)
        for m, mask in enumerate(self.masks(dp)):
            for cb in range(cols // TILE):
                pltpu.make_async_copy(
                    view.at[dp ^ mask, :, :, pl.ds(cb * TILE, TILE)],
                    outs[m % 2].at[m // 2, :, pl.ds(self.offsets[j] + cb * rd, rd), :],
                    sems.at[j],
                ).start()

    def wait_store(self, stage, sems, j):
        pltpu.make_async_copy(stage[j], stage[j], sems.at[j]).wait()


class Use:
    def __init__(self, layout, dp, sources, weights, wsem):
        self.layout, self.dp = layout, dp
        self.sources, self.w, self.wsem = sources, weights, wsem
        self.acc = ()

    def add_sums(self, sg, grads, acc, stage, gsem):
        self.sg, self.grads, self.acc, self.stage, self.gsem = sg, grads, acc, stage, gsem

    def begin(self, order):
        self.layout.start_loads(self.sources, self.w, self.wsem, self.dp, order)

    def clear(self):
        if self.acc:
            for ref in self.acc:
                ref[...] = jnp.zeros_like(ref)
            self.sg[...] = jnp.zeros_like(self.sg)

    def ready(self, *which):
        @pl.when(self.step == 0)
        def _():
            for j in which:
                self.layout.wait_load(self.w, self.wsem, j)

    def sums(self, row, v, at=0):
        self.sg[row : row + 1, at : at + v.shape[1]] += tokens_sum(v)

    def send(self, *which):
        @pl.when(self.last)
        def _():
            for j in which:
                self.layout.start_store(self.acc, self.stage, self.grads, self.gsem, self.dp, j)

    def end(self):
        if self.acc:
            for j in range(len(self.layout.names)):
                self.layout.wait_store(self.stage, self.gsem, j)


def low_lanes(rows):
    return lax.broadcasted_iota(jnp.int32, (rows, PAIR), 1) < HEAD_DIM


def split_pair(v):
    low = low_lanes(v.shape[0])
    zero = jnp.zeros_like(v)
    return jnp.concatenate([jnp.where(low, v, zero), jnp.where(low, zero, v)], axis=0)


def allowed_keys(length, causal, size):
    col = lax.broadcasted_iota(jnp.int32, (size, size), 1)
    ok = col < length
    if causal:
        ok = ok & (col <= lax.broadcasted_iota(jnp.int32, (size, size), 0))
    return ok


def pair_forward(q, k, v, ok):
    size = q.shape[0]
    s = nt(split_pair(q), k)
    s = jnp.where(jnp.concatenate([ok, ok], axis=0), s, -1e30)
    e = jnp.exp(s - jnp.max(s, axis=-1, keepdims=True))
    a = (e * (1.0 / jnp.sum(e, axis=-1, keepdims=True))).astype(BF16)
    mixed = nn(jnp.concatenate([a[:size], a[size:]], axis=1), split_pair(v))
    return a, mixed


def pair_backward(q, k, v, a, g):
    size = q.shape[0]
    g2 = split_pair(g)
    af = a.astype(F32)
    da = nt(g2, v)
    ds = (af * (da - jnp.sum(af * da, axis=-1, keepdims=True))).astype(BF16)
    dv = tn(g2, a).T
    dk = tn(split_pair(q), ds).T
    dq = nn(jnp.concatenate([ds[:size], ds[size:]], axis=1), split_pair(k))
    return dq * (HEAD_DIM**-0.5), dk, dv


def row(small, at):
    return small[at : at + 1]


def attention_fwd(q, k, v, ok, a_ref, o_ref):
    for p in range(a_ref.shape[1]):
        at = p * PAIR
        a, mixed = pair_forward(q(at), k(at), v(at), ok)
        a_ref[0, p] = a
        o_ref[0, :, at : at + PAIR] = mixed.astype(BF16)


def self_fwd(use, small, x_ref, h_ref, qkv_ref, a_ref, o_ref, length, causal, bias):
    size, width = x_ref.shape[1:]
    w = use.w
    ok = allowed_keys(length, causal, size)
    use.ready(0)
    x = x_ref[0]
    q = (nn(x, w[0][:, :width]) + row(small, bias)) * (HEAD_DIM**-0.5)
    qkv_ref[0, :, :width] = q.astype(BF16)
    qkv_ref[0, :, width : 2 * width] = nn(x, w[0][:, width : 2 * width]).astype(BF16)
    qkv_ref[0, :, 2 * width :] = (nn(x, w[0][:, 2 * width :]) + row(small, bias + 1)).astype(BF16)

    def part(k):
        return lambda at: qkv_ref[0, :, k * width + at : k * width + at + PAIR]

    attention_fwd(part(0), part(1), part(2), ok, a_ref, o_ref)
    use.ready(1)
    h_ref[0] = x.astype(F32) + nn(o_ref[0], w[1][...]) + row(small, bias + 2)


def decoder_first(small, h3_ref):
    return normalize(h3_ref[0])[0] * row(small, DEC_GAIN) + row(small, DEC_SHIFT)


def memory_rows(small, h2_ref):
    return (normalize(h2_ref[0])[0] * row(small, ENC_GAIN + 1) + row(small, ENC_SHIFT + 1)).astype(BF16)


def cross_fwd(use, small, h3_ref, h2_ref, h_ref, q_ref, kv_ref, a_ref, o_ref, length):
    size, width = h3_ref.shape[1:]
    w = use.w
    ok = allowed_keys(length, False, size)
    first = decoder_first(small, h3_ref)
    memory = memory_rows(small, h2_ref)
    use.ready(0)
    q = (nn(first.astype(BF16), w[0][...]) + row(small, DEC_BIAS + 3)) * (HEAD_DIM**-0.5)
    q_ref[0] = q.astype(BF16)
    use.ready(1)
    kv_ref[0, :, :width] = nn(memory, w[1][:, :width]).astype(BF16)
    kv_ref[0, :, width:] = (nn(memory, w[1][:, width:]) + row(small, DEC_BIAS + 4)).astype(BF16)
    attention_fwd(
        lambda at: q_ref[0, :, at : at + PAIR],
        lambda at: kv_ref[0, :, at : at + PAIR],
        lambda at: kv_ref[0, :, width + at : width + at + PAIR],
        ok, a_ref, o_ref,
    )
    use.ready(2)
    h_ref[0] = first + nn(o_ref[0], w[2][...]) + row(small, DEC_BIAS + 5)


def ffn_steps(use, small, low, total, ffn_bias, hid_put, slope_put):
    w = use.w
    hidden = w[0].shape[1]
    use.ready(0, 1)
    for at in range(0, hidden, FORWARD_TILE):
        cols = slice(at, at + FORWARD_TILE)
        lane = at % TILE
        bias = small[ffn_bias + at // TILE : ffn_bias + at // TILE + 1, lane : lane + FORWARD_TILE]
        hid, slope = gelu_parts(nn(low, w[0][:, cols]) + bias)
        hid = hid.astype(BF16)
        hid_put(cols, hid)
        slope_put(cols, slope.astype(BF16))
        total = total + nn(hid, w[1][cols, :])
    return total


def ffn_fwd(use, small, h1_ref, x_ref, h_ref, hid_ref, slope_ref):
    first = normalize(h1_ref[0])[0] * row(small, ENC_GAIN) + row(small, ENC_SHIFT)
    total = first + row(small, ENC_BIAS + 3) + x_ref[0].astype(F32)

    def hid_put(cols, v):
        hid_ref[0, :, cols] = v

    def slope_put(cols, v):
        slope_ref[0, :, cols] = v

    h_ref[0] = ffn_steps(use, small, first.astype(BF16), total, ENC_FFN_BIAS, hid_put, slope_put)


def ffn_back(use, low, hid, slope, g, wait=True):
    w, acc = use.w, use.acc
    acc[1][...] += nn(hid.T, g)
    use.send(1)
    if wait:
        use.ready(1)
    du = nt(g, w[1][...]) * slope.astype(F32)
    for t in range(du.shape[1] // TILE):
        use.sums(4 + t, du[:, t * TILE : (t + 1) * TILE])
    gu = du.astype(BF16)
    acc[0][...] += nn(low.T, gu)
    use.send(0)
    if wait:
        use.ready(0)
    return nt(gu, w[0][...])


def ffn_both(use, small, h4_ref, x_ref, cot_ref, out_ref, dd2_ref, dh5_ref, hid_s, slope_s, length):
    size, width = x_ref.shape[1:]
    second = normalize(h4_ref[0])[0] * row(small, DEC_GAIN + 1) + row(small, DEC_SHIFT + 1)
    low = second.astype(BF16)
    total = second + row(small, DEC_BIAS + 6) + x_ref[0].astype(F32)

    def hid_put(cols, v):
        hid_s[:, cols] = v

    def slope_put(cols, v):
        slope_s[:, cols] = v

    total = ffn_steps(use, small, low, total, DEC_FFN_BIAS, hid_put, slope_put)
    xh, r = normalize(total)
    gain = row(small, DEC_GAIN + 2)
    valid = lax.broadcasted_iota(jnp.int32, (size, width), 0) < length
    out_ref[0] = jnp.where(valid, xh * gain + row(small, DEC_SHIFT + 2), 0.0).astype(BF16)
    dv = jnp.where(valid, cot_ref[0].astype(F32), 0.0)
    dh = norm_back(dv, xh, r, gain)
    use.sums(0, dh)
    use.sums(1, dv * xh)
    use.sums(2, dv)
    dh5_ref[0] = dh
    dd2_ref[0] = dh + ffn_back(use, low, hid_s[...], slope_s[...], dh.astype(BF16), False)


def ffn_bwd(use, small, dm_ref, h2_ref, h1_ref, hid_ref, slope_ref, de1_ref, dh2_ref):
    low = (normalize(h1_ref[0])[0] * row(small, ENC_GAIN) + row(small, ENC_SHIFT)).astype(BF16)
    xh, r = normalize(h2_ref[0])
    dv = dm_ref[0]
    dh = norm_back(dv, xh, r, row(small, ENC_GAIN + 1))
    use.sums(0, dh)
    use.sums(1, dv * xh)
    use.sums(2, dv)
    dh2_ref[0] = dh
    de1_ref[0] = dh + ffn_back(use, low, hid_ref[0], slope_ref[0], dh.astype(BF16))


def attention_bwd(use, q, k, v, a_ref, go_s, put):
    for p in range(a_ref.shape[1]):
        at = p * PAIR
        dq, dk, dv = pair_backward(q(at), k(at), v(at), a_ref[0, p], go_s[:, at : at + PAIR])
        use.sums(0, dq, at)
        use.sums(1, dv, at)
        put(at, dq.astype(BF16), dk.astype(BF16), dv.astype(BF16))


def block_sums(use, dv, xh, dh):
    use.sums(2, dh)
    use.sums(3, dv * xh)
    use.sums(4, dv)


def self_bwd(use, small, dv, h_ref, x_ref, extra_ref, qkv_ref, a_ref, o_ref, dx_ref, go_s, g_s, gain_row):
    size, width = x_ref.shape[1:]
    w, acc = use.w, use.acc
    xh, r = normalize(h_ref[0])
    dh = norm_back(dv, xh, r, row(small, gain_row))
    block_sums(use, dv, xh, dh)
    g = dh.astype(BF16)
    acc[1][...] += nn(o_ref[0].T, g)
    use.send(1)
    use.ready(1)
    go_s[...] = nt(g, w[1][...]).astype(BF16)

    def part(k):
        return lambda at: qkv_ref[0, :, k * width + at : k * width + at + PAIR]

    def put(at, *parts):
        for k, v in enumerate(parts):
            g_s[:, k * width + at : k * width + at + PAIR] = v

    attention_bwd(use, part(0), part(1), part(2), a_ref, go_s, put)
    acc[0][...] += nn(x_ref[0].T, g_s[...])
    use.send(0)
    use.ready(0)
    dx_ref[0] = (dh + extra_ref[0] + nt(g_s[...], w[0][...])).astype(BF16)


def cross_bwd(use, small, dv, h4_ref, h3_ref, h2_ref, q_ref, kv_ref, a_ref, o_ref, dm_ref, go_s, gq_s, gkv_s):
    width = h4_ref.shape[2]
    w, acc = use.w, use.acc
    first = decoder_first(small, h3_ref).astype(BF16)
    memory = memory_rows(small, h2_ref)
    xh, r = normalize(h4_ref[0])
    dh = norm_back(dv, xh, r, row(small, DEC_GAIN + 1))
    block_sums(use, dv, xh, dh)
    g = dh.astype(BF16)
    acc[2][...] += nn(o_ref[0].T, g)
    use.send(2)
    use.ready(2)
    go_s[...] = nt(g, w[2][...]).astype(BF16)

    def put(at, dq, dk, dvv):
        gq_s[:, at : at + PAIR] = dq
        gkv_s[:, at : at + PAIR] = dk
        gkv_s[:, width + at : width + at + PAIR] = dvv

    attention_bwd(
        use,
        lambda at: q_ref[0, :, at : at + PAIR],
        lambda at: kv_ref[0, :, at : at + PAIR],
        lambda at: kv_ref[0, :, width + at : width + at + PAIR],
        a_ref, go_s, put,
    )
    acc[0][...] += nn(first.T, gq_s[...])
    acc[1][...] += nn(memory.T, gkv_s[...])
    use.send(0, 1)
    use.ready(0, 1)
    dm_ref[0] = nt(gkv_s[...], w[1][...])
    out = dh + nt(gq_s[...], w[0][...])
    return out


def call(kernel, name, count, meta, rows, small, parts, after, out_rows, scratch):
    def by_row(shape):
        tail = tuple(shape[1:])
        return pl.BlockSpec((1,) + tail, lambda i, k=len(tail): (i,) + (0,) * k)

    width = small.shape[1]
    backs = [layout for layout, _, _, back in parts if back]
    shapes = list(out_rows) + [jax.ShapeDtypeStruct((8, width), F32)] * len(backs)
    for layout in backs:
        shapes += layout.grad_shapes()

    def body(meta, *refs):
        refs = list(refs)

        def next_refs(n):
            head = refs[:n]
            del refs[:n]
            return head

        ins = next_refs(len(rows))
        small_ref = next_refs(1)[0]
        sources = [next_refs(len(part[1])) for part in parts]
        next_refs(len(after))
        outs = next_refs(len(out_rows))
        sums = next_refs(len(backs))
        grads = [next_refs(len(layout.grad_shapes())) for layout in backs]
        uses, at = [], 0
        for (layout, _, order, back), src in zip(parts, sources):
            n = len(layout.names)
            use = Use(layout, meta[0], src, next_refs(n), next_refs(1)[0])
            use.begin(order)
            if back:
                use.add_sums(sums[at], grads[at], next_refs(n), next_refs(n), next_refs(1)[0])
                at += 1
            uses.append(use)
        for use in uses:
            use.clear()

        def sentence(*blocks):
            step = pl.program_id(0)
            for use in uses:
                use.step, use.last = step, step == count - 1
            kernel(meta, step, small_ref, uses, blocks[: len(rows)], blocks[len(rows) :], refs)

        pltpu.emit_pipeline(
            sentence, grid=(count,), in_specs=[by_row(v.shape) for v in rows], out_specs=[by_row(v.shape) for v in out_rows]
        )(*ins, *outs)
        for use in uses:
            use.end()

    scratches = []
    for layout, _, _, back in parts:
        scratches += layout.w_scratch() + (layout.acc_scratch() if back else [])
    hbm = pl.BlockSpec(memory_space=pl.ANY)
    vmem = pl.BlockSpec(memory_space=pltpu.VMEM)
    n_sources = sum(len(part[1]) for part in parts)
    result = pl.pallas_call(
        body,
        in_specs=[pl.BlockSpec(memory_space=pltpu.SMEM)] + [hbm] * len(rows) + [vmem] + [hbm] * (n_sources + len(after)),
        out_specs=[hbm] * len(out_rows) + [vmem] * len(backs) + [hbm] * (len(shapes) - len(out_rows) - len(backs)),
        out_shape=shapes,
        scratch_shapes=scratches + list(scratch),
        compiler_params=pltpu.CompilerParams(vmem_limit_bytes=VMEM_LIMIT),
        cost_estimate=pl.CostEstimate(flops=COST, bytes_accessed=COST, transcendentals=0),
        name=name,
    )(meta, *rows, small, *[v for part in parts for v in part[1]], *after)
    n = len(out_rows)
    given, sums, rest = result[:n], result[n : n + len(backs)], list(result[n + len(backs) :])
    grads = []
    for layout in backs:
        k = len(layout.grad_shapes())
        grads.append(rest[:k])
        rest = rest[k:]
    return given, sums, grads


def lookup(pair_order, lengths):
    indices = jnp.arange(lengths.shape[0], dtype=jnp.int32)
    chosen = jnp.where(pair_order[:, None] == indices[None, :], lengths[None, :], 0)
    return jnp.sum(chosen, axis=1)


class Step:
    def __init__(self, layouts, source, target, cotangent, meta):
        self.layouts, self.meta = layouts, meta
        self.source, self.target, self.cotangent = source, target, cotangent
        self.count, self.size, self.width = source.shape
        self.hidden = layouts[ENC_FFN].shapes[0][1]
        pairs = self.width // PAIR
        self.shares = jax.ShapeDtypeStruct((self.count, pairs, 2 * self.size, self.size), BF16)
        self.small, self.w = None, {}

    def f32(self, cols):
        return jax.ShapeDtypeStruct((self.count, self.size, cols), F32)

    def bf16(self, cols):
        return jax.ShapeDtypeStruct((self.count, self.size, cols), BF16)

    def run(self, kernel, name, groups, rows, out_rows, back=(), scratch=(), after=()):
        parts = [(self.layouts[g], self.w[g], order, g in back) for g, order in groups]
        return call(kernel, name, self.count, self.meta, rows, self.small, parts, list(after), out_rows, scratch)

    def rows_of(self, *columns):
        return [pltpu.VMEM((self.size, c), BF16) for c in columns]

    def enc_self_fwd(self, after=()):
        d = self.width

        def kernel(meta, step, small, uses, ins, outs, scratch):
            self_fwd(uses[0], small, *ins, *outs, meta[2 + step], False, ENC_BIAS)

        (self.h1, self.enc_qkv, self.enc_a, self.enc_o), _, _ = self.run(
            kernel, "enc_self_fwd", ((ENC_SELF, (0, 1)),), [self.source],
            [self.f32(d), self.bf16(3 * d), self.shares, self.bf16(d)], after=after,
        )

    def dec_self_fwd(self, after=()):
        d = self.width

        def kernel(meta, step, small, uses, ins, outs, scratch):
            self_fwd(uses[0], small, *ins, *outs, meta[2 + self.count + step], True, DEC_BIAS)

        (self.h3, self.dec_qkv, self.dec_a, self.dec_o), _, _ = self.run(
            kernel, "dec_self_fwd", ((DEC_SELF, (0, 1)),), [self.target],
            [self.f32(d), self.bf16(3 * d), self.shares, self.bf16(d)], after=after,
        )

    def enc_ffn_fwd(self, after=()):
        def kernel(meta, step, small, uses, ins, outs, scratch):
            ffn_fwd(uses[0], small, *ins, *outs)

        (self.h2, self.hid, self.slope), _, _ = self.run(
            kernel, "enc_ffn_fwd", ((ENC_FFN, (0, 1)),), [self.h1, self.source],
            [self.f32(self.width), self.bf16(self.hidden), self.bf16(self.hidden)], after=after,
        )

    def dec_middle(self, after=()):
        d = self.width

        def kernel(meta, step, small, uses, ins, outs, scratch):
            cross_fwd(uses[0], small, *ins[:2], *outs[:5], meta[2 + step])
            ffn_both(uses[1], small, outs[0], *ins[2:], *outs[5:], *scratch, meta[2 + self.count + step])

        rows, sums, grads = self.run(
            kernel, "dec_middle", ((CROSS, (0, 1, 2)), (DEC_FFN, (0, 1))), [self.h3, self.h2, self.target, self.cotangent],
            [self.f32(d), self.bf16(d), self.bf16(2 * d), self.shares, self.bf16(d), self.bf16(d), self.f32(d),
             self.f32(d)],
            (DEC_FFN,), self.rows_of(self.hidden, self.hidden), after,
        )
        self.h4, self.q, self.kv, self.cross_a, self.cross_o, self.decoded, self.dd2, self.dh5 = rows
        self.sums_df = sums[0]
        return grads[0]

    def dec_bwd(self, after=()):
        d = self.width

        def kernel(meta, step, small, uses, ins, outs, scratch):
            dd2, h4, h3, h2, q, kv, cross_a, cross_o, target, dh5, qkv, a, o = ins
            go, gq, gkv, g = scratch
            dd1 = cross_bwd(uses[0], small, dd2[0], h4, h3, h2, q, kv, cross_a, cross_o, outs[0], go, gq, gkv)
            self_bwd(uses[1], small, dd1, h3, target, dh5, qkv, a, o, outs[1], go, g, DEC_GAIN)

        rows, (self.sums_c, self.sums_ds), grads = self.run(
            kernel, "dec_bwd", ((CROSS, (2, 0, 1)), (DEC_SELF, (1, 0))),
            [self.dd2, self.h4, self.h3, self.h2, self.q, self.kv, self.cross_a, self.cross_o, self.target, self.dh5,
             self.dec_qkv, self.dec_a, self.dec_o],
            [self.f32(d), self.bf16(d)], (CROSS, DEC_SELF), self.rows_of(d, d, 2 * d, 3 * d), after,
        )
        self.dm, self.target_grad = rows
        return grads

    def enc_ffn_bwd(self, after=()):
        d = self.width

        def kernel(meta, step, small, uses, ins, outs, scratch):
            ffn_bwd(uses[0], small, *ins, *outs)

        (self.de1, self.dh2), (self.sums_ef,), grads = self.run(
            kernel, "enc_ffn_bwd", ((ENC_FFN, (1, 0)),), [self.dm, self.h2, self.h1, self.hid, self.slope],
            [self.f32(d), self.f32(d)], (ENC_FFN,), (), after,
        )
        return grads[0]

    def enc_self_bwd(self, after=()):
        d = self.width

        def kernel(meta, step, small, uses, ins, outs, scratch):
            self_bwd(uses[0], small, ins[0][0], *ins[1:], *outs, *scratch, ENC_GAIN)

        (self.source_grad,), (self.sums_es,), grads = self.run(
            kernel, "enc_self_bwd", ((ENC_SELF, (1, 0)),),
            [self.de1, self.h1, self.source, self.dh2, self.enc_qkv, self.enc_a, self.enc_o], [self.bf16(d)],
            (ENC_SELF,), self.rows_of(d, 3 * d), after,
        )
        return grads[0]

    def small_sums(self):
        es, ef, ds, c, df = self.sums_es, self.sums_ef, self.sums_ds, self.sums_c, self.sums_df
        return jnp.concatenate(
            [es[0:3], ef[0:1], es[3:4], ef[1:2], es[4:5], ef[2:3], ds[0:3], c[0:3], df[0:1], ds[3:4], c[3:4], df[1:2],
             ds[4:5], c[4:5], df[2:3], jnp.zeros((3, self.width), F32), ef[4:8], df[4:8]], axis=0,
        )


def simple(kernel, name, meta, inputs, outs, scratch=(), after=(), limit=SIMPLE_LIMIT):
    specs = [pl.BlockSpec(memory_space=pltpu.VMEM)] * len(inputs)
    specs += [pl.BlockSpec(memory_space=pl.ANY)] * len(after)

    def body(meta, *refs):
        return kernel(meta, *refs[: len(inputs)], *refs[len(inputs) + len(after) :])

    return pl.pallas_call(
        body,
        in_specs=[pl.BlockSpec(memory_space=pltpu.SMEM)] + specs,
        out_specs=[pl.BlockSpec(memory_space=pltpu.VMEM)] * len(outs),
        out_shape=list(outs),
        scratch_shapes=list(scratch),
        compiler_params=pltpu.CompilerParams(vmem_limit_bytes=limit),
        cost_estimate=pl.CostEstimate(flops=COST, bytes_accessed=COST, transcendentals=0),
        name=name,
    )(meta, *inputs, *after)


def pack_kernel(plan, nz, meta, *refs):
    n_in = sum(len(p) for p in plan)
    shards = refs[:n_in]
    small_refs = refs[n_in : n_in + len(SMALLS) + len(LINES)]
    outs = refs[n_in + len(small_refs) : -1]
    rows = refs[-1]
    at = 0
    for out, chunk in zip(outs, plan):
        for row in chunk:
            shard = shards[at]
            rd, cols = shard.shape
            for cb in range(cols // TILE):
                out[row + cb * rd : row + (cb + 1) * rd, :] = shard[:, cb * TILE : (cb + 1) * TILE]
            at += 1
    rank = meta[0] * nz + meta[1]
    rows[...] = jnp.zeros_like(rows)
    for ref, (_, row, _) in zip(small_refs, SMALLS + LINES):
        lines, part = ref.shape
        lane = lax.broadcasted_iota(jnp.int32, (part, TILE), 1)
        spread = (lane % part == lax.broadcasted_iota(jnp.int32, (part, TILE), 0)).astype(BF16)
        tiled = nn(ref[...], spread)
        across = lax.broadcasted_iota(jnp.int32, (lines, TILE), 1)
        if row >= ENC_FFN_BIAS:
            per = TILE // part
            tiled = jnp.broadcast_to(tiled, (4, TILE))
            across = lax.broadcasted_iota(jnp.int32, (4, TILE), 1)
            down = lax.broadcasted_iota(jnp.int32, (4, TILE), 0)
            ok = (across // part == rank % per) & (down == rank // per)
            rows[row : row + 4, :] = jnp.where(ok, tiled, 0.0)
        else:
            rows[row : row + lines, :] = jnp.where(across // part == rank, tiled, 0.0)
    outs[0][outs[0].shape[0] - SMALL_ROWS :, :] = rows[...].astype(BF16)


def along_z_kernel(nz, rows, tail, meta, *refs):
    parts = refs[:nz]
    out = refs[nz]
    z = meta[1]
    for s in range(nz):
        at = pl.multiple_of(((z + nz - s) % nz) * rows, 16)
        out[pl.ds(at, rows), :] = parts[s][:rows, :]
    if tail:
        total = parts[0][rows:, :].astype(F32)
        for s in range(1, nz):
            total = total + parts[s][rows:, :].astype(F32)
        out[nz * rows :, :] = total.astype(BF16)


def add_cores_kernel(counts, tail, halves, meta, *refs):
    n = len(counts)
    outs = refs[2 * n + 2 * bool(tail) :]
    chips, nz = refs[0].shape[:2]
    total = sum(counts)
    for k in range(chips):
        out = outs[k % 2].at[k // 2] if halves else outs[k]
        for z in range(nz):
            at = z * total
            for g, rows in enumerate(counts):
                out[at : at + rows, :] = (
                    refs[2 * g][k, z].astype(F32) + refs[2 * g + 1][k, z].astype(F32)
                ).astype(BF16)
                at += rows
        if tail:
            out[nz * total :, :] = (refs[2 * n][...].astype(F32) + refs[2 * n + 1][...].astype(F32)).astype(BF16)


def add_half_kernel(meta, kept, got, own, second):
    own[...] = (kept[0].astype(F32) + got[0].astype(F32)).astype(BF16)
    second[...] = (kept[1].astype(F32) + got[1].astype(F32)).astype(BF16)


def add_two_kernel(meta, one, two, out):
    out[...] = (one[...].astype(F32) + two[...].astype(F32)).astype(BF16)


def add_late_kernel(meta, first, one, two, out):
    nz, head = first.shape[:2]
    tail = out.shape[1] - head
    for z in range(nz):
        out[z, :head, :] = first[z]
        at = slice(z * tail, (z + 1) * tail)
        out[z, head:, :] = (one[at, :].astype(F32) + two[at, :].astype(F32)).astype(BF16)


def add_chips_kernel(nz, rows, tail, n_parts, meta, *refs):
    parts, outs = refs[:n_parts], refs[n_parts:]
    z = meta[1]
    for s in range(nz):
        at = pl.multiple_of(((z + s) % nz) * rows, 16)
        total = parts[0][pl.ds(at, rows), :].astype(F32)
        for part in parts[1:]:
            total = total + part[pl.ds(at, rows), :].astype(F32)
        outs[s][:rows, :] = total.astype(outs[s].dtype)
    if tail:
        total = parts[0][nz * rows :, :].astype(F32)
        for part in parts[1:]:
            total = total + part[nz * rows :, :].astype(F32)
        for s in range(nz):
            outs[s][rows:, :] = total.astype(outs[s].dtype)


def add_z_kernel(nz, places, rows, tail, meta, *refs):
    parts, outs = refs[:nz], refs[nz:]
    for (row, rd, cols), out in zip(places, outs):
        for cb in range(cols // TILE):
            at = row + cb * rd
            total = parts[0][at : at + rd, :].astype(F32)
            for part in parts[1:]:
                total = total + part[at : at + rd, :].astype(F32)
            out[:, cb * TILE : (cb + 1) * TILE] = total
    if tail:
        rank = meta[0] * nz + meta[1]
        total = parts[0][rows:, :]
        for part in parts[1:]:
            total = total + part[rows:, :].astype(F32)
        for out, (_, row, _) in zip(outs[len(places) :], SMALLS + LINES):
            lines, part = out.shape
            if row >= ENC_FFN_BIAS:
                per = TILE // part
                down = lax.broadcasted_iota(jnp.int32, (8, TILE), 0)
                base = total[24:32, :]
                picked = jnp.sum(
                    jnp.where(down == rank // per + (row - 24), base, 0.0), axis=0, keepdims=True
                )
                moved = pltpu.roll(jnp.broadcast_to(picked, (8, TILE)), TILE - (rank % per) * part, 1)
                out[...] = moved[0:1, :part]
            else:
                first = row // 8 * 8
                moved = pltpu.roll(total[first : first + 24 if first < 8 else 24, :], TILE - rank * part, 1)
                out[...] = moved[row - first : row - first + lines, :part]


def swap(v, size, mask):
    return lax.ppermute(v, DP, [(i, i ^ mask) for i in range(size)])


def shift(v, size, by):
    return lax.ppermute(v, FSDP, [(i, (i + by) % size) for i in range(size)])


def across(v, size, own, other):
    return lax.ppermute(v, DP, [(i, i ^ (other if i % 2 else own)) for i in range(size)])


def hold(values, *first):
    return lax.optimization_barrier((values, first))[0]


class Exchange:
    def __init__(self, layouts, meta, nd, nz):
        self.layouts, self.meta, self.nd, self.nz = layouts, meta, nd, nz

    def pack(self, shards):
        plan, sizes, inputs = [], [], []
        for groups in GATHERS:
            rows, first = [], 0
            for g in groups:
                self.layouts[g].first = first
                for n, at in zip(self.layouts[g].names, self.layouts[g].offsets):
                    rows.append(first + at)
                    inputs.append(shards[n])
                first += self.layouts[g].rows
            for g in groups:
                self.layouts[g].span = first
            plan.append(rows)
            sizes.append(first)
        inputs += [shards[n] for n, _, _ in SMALLS] + [shards[n].reshape(1, -1) for n, _, _ in LINES]
        self.sizes = sizes
        self.tails = [SMALL_ROWS] + [0] * (len(GATHERS) - 1)
        return simple(
            functools.partial(pack_kernel, plan, self.nz), "pack", self.meta, inputs,
            [jax.ShapeDtypeStruct((r + t, TILE), BF16) for r, t in zip(sizes, self.tails)],
            [pltpu.VMEM((SMALL_ROWS, TILE), F32)], limit=VMEM_LIMIT,
        )

    def gather_z(self, pack):
        return [pack] + [shift(pack, self.nz, s) for s in range(1, self.nz)]

    def join_z(self, c, parts):
        rows, tail = self.sizes[c], self.tails[c]
        return simple(
            functools.partial(along_z_kernel, self.nz, rows, tail), "join", self.meta, parts,
            [jax.ShapeDtypeStruct((self.nz * rows + tail, TILE), BF16)],
        )[0]

    def gather_chips(self, joined, *before):
        first = across(joined, self.nd, 4, 2)
        second = across(joined, self.nd, 2, 4)
        if before:
            first = hold(first, *before)
        return [joined, first, second, across(first, self.nd, 2, 4)]

    def gather_cores(self, pieces):
        return [v for piece in pieces for v in (piece, swap(piece, self.nd, 1))]

    def to_cores(self, grads):
        return [grads[0], swap(grads[1], self.nd, 1)]

    def add_cores(self, groups, parts, tail=None, halves=False):
        counts = [self.layouts[g].rows for g in groups]
        extra = 0 if tail is None else SMALL_ROWS
        if extra:
            parts = parts + [tail, swap(tail, self.nd, 1)]
        return simple(
            functools.partial(add_cores_kernel, counts, extra, halves), "add_cores", self.meta, parts,
            [jax.ShapeDtypeStruct(((2,) if halves else ()) + (self.nz * sum(counts) + extra, TILE), BF16)]
            * (2 if halves else self.nd // 2),
        )

    def add_half(self, kept, got):
        shape = jax.ShapeDtypeStruct(kept.shape[1:], BF16)
        return simple(add_half_kernel, "add_half", self.meta, [kept, got], [shape, shape])

    def to_first(self, v):
        return across(v, self.nd, 4, 2)

    def to_second(self, v):
        return across(v, self.nd, 2, 4)

    def to_chips(self, sums):
        return [sums[0], self.to_first(sums[1]), self.to_second(sums[2]), swap(sums[3], self.nd, 6)]

    def add_chips(self, groups, parts, extra=0):
        rows = sum(self.layouts[g].rows for g in groups)
        return simple(
            functools.partial(add_chips_kernel, self.nz, rows, extra, len(parts)), "add_chips", self.meta, parts,
            [jax.ShapeDtypeStruct((rows + extra, TILE), F32 if s == 0 else BF16) for s in range(self.nz)],
        )

    def add_chips_flat(self, parts):
        shape = jax.ShapeDtypeStruct(parts[0].shape, BF16)
        return simple(add_two_kernel, "add_two", self.meta, parts, [shape])[0]

    def add_late(self, first, parts):
        first = first.reshape(self.nz, -1, TILE)
        head, tail = first.shape[1], parts[0].shape[0] // self.nz
        shape = jax.ShapeDtypeStruct((self.nz, head + tail, TILE), BF16)
        return simple(add_late_kernel, "add_late", self.meta, [first] + parts, [shape])[0]

    def to_z(self, sums):
        return [sums[0]] + [shift(sums[s], self.nz, s) for s in range(1, self.nz)]

    def add_z(self, groups, parts, extra=0):
        ranks, first, places = self.nd * self.nz, 0, []
        for g in groups:
            layout = self.layouts[g]
            places += [(first + at, r // ranks, c) for at, (r, c) in zip(layout.offsets, layout.shapes)]
            first += layout.rows
        outs = [jax.ShapeDtypeStruct((rd, c), F32) for _, rd, c in places]
        if extra:
            wide = TILE // ranks
            outs += [jax.ShapeDtypeStruct((lines, wide), F32) for _, _, lines in SMALLS]
            outs += [jax.ShapeDtypeStruct((1, 4 * wide), F32)] * 2
        return simple(
            functools.partial(add_z_kernel, len(parts), places, first, extra), "add_z", self.meta, parts, outs
        )


def by_pieces(layouts, source, target, cotangent, place, meta, shards, nd, nz):
    ex = Exchange(layouts, place, nd, nz)
    packs = ex.pack(shards)
    st = Step(layouts, source, target, cotangent, hold(meta, packs))
    along0 = ex.gather_z(packs[0])
    joined0 = ex.join_z(0, along0)
    along1 = ex.gather_z(hold(packs[1], joined0))
    pieces = ex.gather_cores(hold(ex.gather_chips(joined0), along1))
    st.w[ENC_SELF] = pieces
    st.small = sum(p[p.shape[0] - SMALL_ROWS :].astype(F32) for p in pieces)
    joined1 = ex.join_z(1, along1)
    along2 = ex.gather_z(hold(packs[2], joined1))
    st.enc_self_fwd(after=[joined1])
    along2 = hold(along2, st.h1)
    chips1 = ex.gather_chips(joined1, along2)
    joined2 = ex.join_z(2, hold(along2, chips1[1]))
    st.w[ENC_FFN] = st.w[DEC_SELF] = ex.gather_cores(hold(chips1, joined2))
    st.dec_self_fwd(after=[joined2])
    chips2 = ex.gather_chips(joined2, st.h3)
    early2 = ex.gather_cores(hold(chips2[:3], st.h3))
    st.enc_ffn_fwd(after=[chips2[1], chips2[2]])
    st.w[CROSS] = st.w[DEC_FFN] = hold(early2, st.h2) + ex.gather_cores(hold(chips2[3:], st.h2))
    result = [None] * len(shards)

    def put(groups, outs):
        names = [n for g in groups for n in GROUPS[g]]
        names += [n for n, _, _ in SMALLS + LINES]
        for n, v in zip(names, outs):
            result[n] = v.reshape(shards[n].shape)

    df = st.dec_middle()[0]
    df = lax.psum_scatter(df.reshape(nd, nz, *df.shape[1:]), DP, scatter_dimension=0, tiled=True)
    both = (CROSS, DEC_SELF)
    cr, ds = st.dec_bwd()
    cr_kept, cr = ex.add_cores(both, ex.to_cores(cr) + ex.to_cores(ds), halves=True)
    cr = ex.to_first(cr)
    ef = st.enc_ffn_bwd(after=[cr_kept])
    cr, df = hold((cr, df), st.de1)
    ef = ex.to_cores(hold(ef, cr))
    cr_own, cr = ex.add_half(cr_kept, cr)
    cr = ex.to_second(cr)
    ef_kept, ef = ex.add_cores((ENC_FFN,), hold(ef, cr_own), halves=True)
    cr = ex.add_late(df, [cr_own, hold(cr, ef_kept)])
    ef = ex.to_first(ef)
    late = lax.psum_scatter(cr, FSDP, scatter_dimension=0, tiled=True)[0]
    es = st.enc_self_bwd(after=[cr, ef_kept])
    ef = hold(ef, st.source_grad)
    es = ex.to_cores(hold(es, ef))
    tail = st.small_sums().astype(BF16)
    ef_own, ef = ex.add_half(ef_kept, ef)
    ef = ex.to_second(ef)
    es = ex.to_chips(ex.add_cores((ENC_SELF,), hold(es, ef_own), tail))
    ef = ex.to_z(ex.add_chips((ENC_FFN,), hold([ef_own, ef], es[0])))
    es = ex.to_z(ex.add_chips((ENC_SELF,), hold(es, ef[0]), SMALL_ROWS))
    put((ENC_FFN,), ex.add_z((ENC_FFN,), hold(ef, es[0])))
    late = hold(late, result[A_ENC_IN])
    put((DEC_FFN,) + both, ex.add_z((DEC_FFN,) + both, [late]))
    es = hold(es, result[A_DEC_IN])
    put((ENC_SELF,), ex.add_z((ENC_SELF,), es, SMALL_ROWS))
    return (st.decoded, st.source_grad, st.target_grad) + tuple(result)


def whole(layouts, source, target, cotangent, meta, shards):
    small_names = [n for n, _, _ in SMALLS]
    full = [
        lax.all_gather(v, AXES, axis=1 if n in small_names else 0, tiled=True) for n, v in enumerate(shards)
    ]
    width = source.shape[2]
    st = Step(layouts, source, target, cotangent, meta)
    st.small = jnp.concatenate(
        [full[n] for n in small_names]
        + [jnp.zeros((3, width), BF16)]
        + [full[n].reshape(-1, width) for n, _, _ in LINES],
        axis=0,
    ).astype(F32)
    st.w = {g: [full[n] for n in names] for g, names in enumerate(GROUPS)}
    st.enc_self_fwd()
    st.enc_ffn_fwd()
    st.dec_self_fwd()
    grads = [None] * len(GROUPS)
    grads[DEC_FFN] = st.dec_middle()
    grads[CROSS], grads[DEC_SELF] = st.dec_bwd()
    grads[ENC_FFN] = st.enc_ffn_bwd()
    grads[ENC_SELF] = st.enc_self_bwd()
    sums = st.small_sums()
    result = [None] * len(shards)
    for g, names in enumerate(GROUPS):
        for n, v in zip(names, grads[g]):
            result[n] = v.astype(F32)
    for n, row, lines in SMALLS:
        result[n] = sums[row : row + lines]
    for n, row, _ in LINES:
        result[n] = sums[row : row + 4].reshape(-1)
    result = [
        lax.psum_scatter(v, AXES, scatter_dimension=1 if n in small_names else 0, tiled=True)
        for n, v in enumerate(result)
    ]
    return (st.decoded, st.source_grad, st.target_grad) + tuple(result)


def local(nd, nz, source, target, cotangent, pair_order, source_lengths, target_lengths, *shards):
    ranks = nd * nz
    matrices = [n for names in GROUPS for n in names]
    shapes = {n: (shards[n].shape[0] * ranks, shards[n].shape[1]) for n in matrices}
    pieces = nd == 8 and all(shards[n].shape[0] % 16 == 0 for n in matrices)
    modes = (PIECES, PIECES, PIECES, PIECES, RANKS) if pieces else (WHOLE,) * len(GROUPS)
    layouts = [Layout(g, shapes, modes[g], nd, nz) for g in range(len(GROUPS))]
    place = jnp.stack([lax.axis_index(DP), lax.axis_index(FSDP)]).astype(jnp.int32)
    meta = jnp.concatenate([place, lookup(pair_order, source_lengths), lookup(pair_order, target_lengths)])
    if pieces:
        return by_pieces(layouts, source, target, cotangent, place, meta, shards, nd, nz)
    return whole(layouts, source, target, cotangent, meta, shards)


def specs():
    split, rows, cols = P(AXES, None, None), P(AXES, None), P(None, AXES)
    line = P(AXES)
    weights = (
        rows, rows, rows, rows, cols, line, cols, cols,
        rows, rows, rows, rows, rows, rows, rows, cols, line, cols, cols,
    )
    return (split, split, split, line, P(), P()) + weights, (split, split, split) + weights


def solution(mesh):
    in_specs, out_specs = specs()
    return jax.shard_map(
        functools.partial(local, mesh.shape[DP], mesh.shape[FSDP]),
        mesh=mesh, in_specs=in_specs, out_specs=out_specs, check_vma=False,
    )
```
